32 devices in a mesh: slab: 8 (over z, x), col: 4 (over y, core).
Axes of the slice: x: 2, y: 2, z: 4, core: 2. Of those that a mesh axis runs over, the one named last changes fastest.
Arguments:
- order_params: float32 [16, 64, 32, 256], P(None, 'slab', 'col'), may hold values from 0 to 0.5
- layer_mask: int32 [64, 32, 256], P('slab', 'col'), may hold values 0 or 1
- coarse_temp: float32 [48, 16, 128], P('slab', 'col'), may hold values from 0.5 to 1.5, as said below
- coarse_rows: int32 [8], replicated, may hold values from 2 to 6, as said below
- grain_ids: int32 [8, 4, 16], replicated, may hold values from 0 to 303, as said below
- energy: float32 [304], replicated, may hold values from 0.5 to 6
Outputs:
- evolved: float32 [16, 64, 32, 256], P(None, 'slab', 'col')
The draws below stay inside these ranges and needn't reach their ends.
Inputs may be any that keep to these rules, and one draw needn't show every extreme that they name: coarse_rows sums to 32; the s-th block of coarse planes begins within 1 planes of s * 4; some entry equals 6. `coarse_temp`: rows of one index of slab past its entry of coarse_rows are not part of the field. `grain_ids`: the 16 ids of a block are distinct; a block shares exactly 4 ids with each block beside it along slab and along col and none with any other block.
All inputs are finite; a program needn't handle non-finite values. No bound on the sum of `layer_mask` on one device may be relied on, other than what follows from the above.
Results may differ from the reference program's by a relative error of at most 0.0001.
Values sent between devices are 32-bit elements; how exact they have to be, the bound alone decides.
No kernel may reach another device: no remote copies, remote signals or barrier semaphores. Data moves between devices by JAX's collectives and lax.ppermute only.
A program may use at most 64 MiB of HBM per device.

```python
import math
import jax
import jax.numpy as jnp
from jax import lax

Q = 16
SHARE = 4
JITTER = 1
STEPS = 4
CX = 8
CY = 8
CAPX = 6
FINE_CELLS_TRACK = 64
FINE_CELLS_ACROSS = 32
FINE_CELLS_HEIGHT = 256
NXC = 32
NYC = 16
NZC = 128
GRAINS = 304
N_SLAB = 8
N_COL = 4


def draw_coarse_temp(key, part):
    row_total = N_SLAB * CAPX
    owner = (jnp.arange(row_total) // CAPX).astype(jnp.float32)
    trend = 0.7 + 0.6 * owner / (N_SLAB - 1)
    first_key = jax.random.fold_in(key, 0)
    noise = jax.random.uniform(first_key, (row_total, NYC, NZC), jnp.float32, -0.2, 0.2)
    return (trend[:, None, None] + noise).astype(jnp.float32)


def draw_coarse_rows(key, part):
    first_key, second_key = jax.random.split(key)
    offsets = jax.random.randint(first_key, (N_SLAB + 1,), -JITTER, JITTER + 1)
    chosen = jax.random.randint(second_key, (), 1, N_SLAB - 1)
    offsets = offsets.at[chosen].set(-JITTER).at[chosen + 1].set(JITTER)
    offsets = offsets.at[0].set(0).at[N_SLAB].set(0)
    return (CX // 2 + offsets[1:] - offsets[:-1]).astype(jnp.int32)


def draw_grain_ids(key, part):
    first_key, second_key = jax.random.split(key)
    slab_index = jnp.arange(N_SLAB)[:, None, None]
    col_index = jnp.arange(N_COL)[None, :, None]
    rank_index = jnp.arange(SHARE)[None, None, :]
    across_count = (N_SLAB + 1) * N_COL * SHARE
    low_x = (slab_index * N_COL + col_index) * SHARE + rank_index
    high_x = ((slab_index + 1) * N_COL + col_index) * SHARE + rank_index
    low_y = across_count + (slab_index * (N_COL + 1) + col_index) * SHARE + rank_index
    high_y = across_count + (slab_index * (N_COL + 1) + col_index + 1) * SHARE + rank_index
    full_shape = (N_SLAB, N_COL, SHARE)
    grain_table = jnp.concatenate([jnp.broadcast_to(low_x, full_shape), jnp.broadcast_to(high_x, full_shape), jnp.broadcast_to(low_y, full_shape), jnp.broadcast_to(high_y, full_shape)], axis=-1)
    relabel = jax.random.permutation(first_key, GRAINS)
    grain_table = relabel[grain_table]
    scores = jax.random.randint(second_key, (N_SLAB, N_COL, Q), 0, 1 << 20) * Q + jnp.arange(Q)[None, None, :]
    slot_order = jnp.argsort(scores, axis=-1)
    return jnp.take_along_axis(grain_table, slot_order, axis=-1).astype(jnp.int32)


def plant(result, rng, low, largest):
    longest = result.shape.index(max(result.shape))
    spots = []
    for shift in (0, 1):
        where = [jax.random.randint(jax.random.fold_in(rng, axis), (), 0, length) for axis, length in enumerate(result.shape)]
        where[longest] = (where[longest] + shift) % result.shape[longest]
        spots.append(tuple(where))
    return result.at[spots[0]].set(low).at[spots[1]].set(largest)


def levels(rng, shape, pieces, low, high):
    loudness, own = 1.0, jax.random.fold_in(rng, 6)
    for position, blocks in pieces:
        draws = jnp.exp(jax.random.uniform(jax.random.fold_in(own, position), (blocks,), jnp.float32, low / len(pieces), high / len(pieces)))
        loudness = loudness * jnp.repeat(draws, shape[position] // blocks).reshape([-1 if axis == position else 1 for axis in range(len(shape))])
    return loudness


def setup_inputs(seed: int = 0) -> dict:
    splits = jax.random.split(jax.random.key(seed), 7)
    order_params = jnp.clip(0.5 * jax.random.uniform(splits[0], (Q, FINE_CELLS_TRACK, FINE_CELLS_ACROSS, FINE_CELLS_HEIGHT), jnp.float32) ** levels(splits[0], (Q, FINE_CELLS_TRACK, FINE_CELLS_ACROSS, FINE_CELLS_HEIGHT), ((1, 8), (2, 4)), -0.2, 0.2), 0.0, 0.5)
    layer_mask = plant((jax.random.randint(splits[1], (FINE_CELLS_TRACK, FINE_CELLS_ACROSS, FINE_CELLS_HEIGHT), 0, 4) < 3).astype(jnp.int32), jax.random.fold_in(splits[1], 1), 0, 1)
    coarse_temp = draw_coarse_temp(jax.random.fold_in(splits[6], 71), 0)
    coarse_rows = draw_coarse_rows(jax.random.fold_in(splits[6], 71), 0)
    grain_ids = draw_grain_ids(jax.random.fold_in(splits[6], 71), 0)
    energy = jnp.clip(jnp.exp(jax.random.uniform(splits[5], (GRAINS,), jnp.float32, math.log(0.5), math.log(6.0))), 0.5, 6.0)
    return {"order_params": order_params, "layer_mask": layer_mask, "coarse_temp": coarse_temp, "coarse_rows": coarse_rows, "grain_ids": grain_ids, "energy": energy}


FULL_ACCURACY = lax.Precision.HIGHEST
TIME_STEP = 0.05
COUPLING = 1.5


def linear_resample_axis(values, axis, fine_count):
    coarse_count = values.shape[axis]
    fine_index = jnp.arange(fine_count, dtype=jnp.int32)
    lower_index = (2 * fine_index - 1) // 4
    weight = ((2 * fine_index - 1) - 4 * lower_index).astype(jnp.float32) / 4.0
    lower_node = jnp.clip(lower_index, 0, coarse_count - 1).astype(jnp.int32)
    upper_node = jnp.clip(lower_index + 1, 0, coarse_count - 1).astype(jnp.int32)
    lower_values = jnp.take(values, lower_node, axis=axis)
    upper_values = jnp.take(values, upper_node, axis=axis)
    bcast_shape = [1] * values.ndim
    bcast_shape[axis] = fine_count
    weight = weight.reshape(bcast_shape)
    return (1.0 - weight) * lower_values + weight * upper_values


def slot_match(mine, theirs):
    return (mine[..., :, None] == theirs[..., None, :]).astype(jnp.float32)


def neighbour_sum(fields, grain_ids):
    blocks = fields.reshape(Q, N_SLAB, CX, N_COL, CY, FINE_CELLS_HEIGHT)
    prev_slab = slot_match(grain_ids, jnp.roll(grain_ids, 1, axis=0))
    next_slab = slot_match(grain_ids, jnp.roll(grain_ids, -1, axis=0))
    prev_col = slot_match(grain_ids, jnp.roll(grain_ids, 1, axis=1))
    next_col = slot_match(grain_ids, jnp.roll(grain_ids, -1, axis=1))
    top_faces = blocks[:, :, CX - 1]
    bottom_faces = blocks[:, :, 0]
    zero_slab = jnp.zeros_like(top_faces[:, :1])
    from_below = jnp.concatenate([zero_slab, top_faces[:, :-1]], axis=1)
    from_above = jnp.concatenate([bottom_faces[:, 1:], zero_slab], axis=1)
    below = jnp.einsum("scqr,rscyz->qscyz", prev_slab, from_below, precision=FULL_ACCURACY)
    above = jnp.einsum("scqr,rscyz->qscyz", next_slab, from_above, precision=FULL_ACCURACY)
    x_low = jnp.concatenate([below[:, :, None], blocks[:, :, :-1]], axis=2)
    x_high = jnp.concatenate([blocks[:, :, 1:], above[:, :, None]], axis=2)
    right_faces = blocks[:, :, :, :, CY - 1]
    left_faces = blocks[:, :, :, :, 0]
    zero_col = jnp.zeros_like(right_faces[:, :, :, :1])
    from_left = jnp.concatenate([zero_col, right_faces[:, :, :, :-1]], axis=3)
    from_right = jnp.concatenate([left_faces[:, :, :, 1:], zero_col], axis=3)
    lefts = jnp.einsum("scqr,rsxcz->qsxcz", prev_col, from_left, precision=FULL_ACCURACY)
    rights = jnp.einsum("scqr,rsxcz->qsxcz", next_col, from_right, precision=FULL_ACCURACY)
    y_low = jnp.concatenate([lefts[:, :, :, :, None], blocks[:, :, :, :, :-1]], axis=4)
    y_high = jnp.concatenate([blocks[:, :, :, :, 1:], rights[:, :, :, :, None]], axis=4)
    x_low = x_low.reshape(fields.shape)
    x_high = x_high.reshape(fields.shape)
    y_low = y_low.reshape(fields.shape)
    y_high = y_high.reshape(fields.shape)
    zero_plane = jnp.zeros((Q, FINE_CELLS_TRACK, FINE_CELLS_ACROSS, 1), jnp.float32)
    z_low = jnp.concatenate([zero_plane, fields[..., :-1]], axis=3)
    z_high = jnp.concatenate([fields[..., 1:], zero_plane], axis=3)
    return x_low + x_high + y_low + y_high + z_low + z_high


def rates(fields, laplace, grain_mobility, slot_energy):
    squares = jnp.sum(fields * fields, axis=0)
    force = (-fields + fields * fields * fields
             + 2.0 * COUPLING * fields * (squares - fields * fields)
             - laplace - slot_energy * fields * (1.0 - fields))
    return -grain_mobility * force


def reference(order_params, layer_mask, coarse_temp, coarse_rows, grain_ids, energy):
    block_ends = jnp.cumsum(coarse_rows).astype(jnp.int32)
    block_starts = (block_ends - coarse_rows).astype(jnp.int32)
    plane = jnp.arange(NXC, dtype=jnp.int32)
    owner = jnp.sum((block_ends[None, :] <= plane[:, None]).astype(jnp.int32), axis=1).astype(jnp.int32)
    row_index = (owner * CAPX + plane - block_starts[owner]).astype(jnp.int32)
    coarse_mesh = coarse_temp[row_index]
    thermal_profile = linear_resample_axis(coarse_mesh, 0, FINE_CELLS_TRACK)
    thermal_profile = linear_resample_axis(thermal_profile, 1, FINE_CELLS_ACROSS)
    thermal_profile = linear_resample_axis(thermal_profile, 2, FINE_CELLS_HEIGHT)
    grain_mobility = jnp.exp(2.0 * (thermal_profile - 1.0))
    deposited = layer_mask.astype(jnp.float32)
    mobility_sum = Q * jnp.sum(deposited * grain_mobility)
    energy_blocks = energy[grain_ids]
    slot_energy = jnp.broadcast_to(
        jnp.transpose(energy_blocks, (2, 0, 1))[:, :, None, :, None, None],
        (Q, N_SLAB, CX, N_COL, CY, FINE_CELLS_HEIGHT)).reshape(Q, FINE_CELLS_TRACK, FINE_CELLS_ACROSS, FINE_CELLS_HEIGHT)
    fields = order_params
    for step_index in range(STEPS):
        laplace = neighbour_sum(fields, grain_ids) - 6.0 * fields
        rate = rates(fields, laplace, grain_mobility, slot_energy)
        multiplier = jnp.sum(deposited * jnp.sum(rate, axis=0)) / mobility_sum
        fields = fields + TIME_STEP * deposited * (rate - grain_mobility * multiplier)
    return fields
```

```python
import jax
import jax.numpy as jnp
from jax import lax
from jax.sharding import PartitionSpec as P

SHARE = 4
STEPS = 4


FULL_ACCURACY = lax.Precision.HIGHEST
TIME_STEP = 0.05
COUPLING = 1.5


def padded(cells, sides, width):
    for axis, dim in sides:
        count = lax.axis_size(axis)
        ends = count - 1
        head = lax.slice_in_dim(cells, 0, width, axis=dim)
        tail = lax.slice_in_dim(cells, cells.shape[dim] - width, cells.shape[dim], axis=dim)
        cells = jnp.concatenate(
            [
                lax.ppermute(tail, axis, [(i, (i + 1) % count) for i in range(ends)]),
                cells,
                lax.ppermute(head, axis, [((i + 1) % count, i) for i in range(ends)]),
            ],
            axis=dim,
        )
    return cells


def passed_along(array, axis, by):
    peers = lax.axis_size(axis)
    pairs = [(i, i + by) for i in range(peers) if 0 <= i + by < peers]
    return lax.ppermute(array, axis, pairs)


def node_weights(fine_index, coarse_count):
    lower_index = (2 * fine_index - 1) // 4
    weight = (2 * fine_index - 1 - 4 * lower_index).astype(jnp.float32) / 4.0
    lower_node = jnp.clip(lower_index, 0, coarse_count - 1)
    upper_node = jnp.clip(lower_index + 1, 0, coarse_count - 1)
    return (lower_node, upper_node, weight)


def interpolation_matrix(lower_node, upper_node, weight, column_count):
    columns = jnp.arange(column_count, dtype=jnp.int32)
    lower_hit = (columns[None, :] == lower_node[:, None]).astype(jnp.float32)
    upper_hit = (columns[None, :] == upper_node[:, None]).astype(jnp.float32)
    return (1.0 - weight)[:, None] * lower_hit + weight[:, None] * upper_hit


def pick_entry(values, slab_iota, position):
    return jnp.sum(jnp.where(slab_iota == position, values, 0))


def block_ids(grain_ids, slab_pos, col_pos):
    slab_row = lax.dynamic_index_in_dim(grain_ids, slab_pos, 0, keepdims=False)
    return lax.dynamic_index_in_dim(slab_row, col_pos, 0, keepdims=False)


def slot_match(mine, theirs):
    return (mine[:, None] == theirs[None, :]).astype(jnp.float32)


def packing(sender, receiver):
    shared = jnp.any(sender[:, None] == receiver[None, :], axis=1)
    placed = jnp.cumsum(shared.astype(jnp.int32)) - 1
    targets = jnp.arange(SHARE, dtype=jnp.int32)
    return ((placed[None, :] == targets[:, None]) & shared[None, :]).astype(jnp.float32)


def unpacking(sender, receiver):
    return jnp.dot(
        slot_match(receiver, sender), packing(sender, receiver).T, precision=FULL_ACCURACY
    )


def apply_slots(matrix, face_cells):
    return jnp.einsum("qr,ryz->qyz", matrix, face_cells, precision=FULL_ACCURACY)


def rates(fields, laplace, grain_mobility, slot_energy):
    squares = jnp.sum(fields * fields, axis=0)
    force = (
        -fields
        + fields * fields * fields
        + 2.0 * COUPLING * fields * (squares - fields * fields)
        - laplace
        - slot_energy * fields * (1.0 - fields)
    )
    return -grain_mobility * force


def total(parts):
    devices = lax.axis_size("slab") * lax.axis_size("col")
    row = jnp.pad(jnp.stack(parts), (0, 128 - len(parts)))
    sent = jnp.broadcast_to(row, (devices, 1, 128))
    got = lax.all_to_all(sent, ("slab", "col"), 0, 0)
    return jnp.sum(got, axis=(0, 1))


def per_device(order_params, layer_mask, coarse_temp, coarse_rows, grain_ids, energy):
    slot_count, cells_x, cells_y, cells_z = order_params.shape
    slab_count = lax.axis_size("slab")
    col_count = lax.axis_size("col")
    slab_at = lax.axis_index("slab")
    col_at = lax.axis_index("col")
    capacity = coarse_temp.shape[0]
    coarse_y = coarse_temp.shape[1]
    coarse_z = coarse_temp.shape[2]
    extended = padded(coarse_temp, (("col", 1),), 1)
    block_ends = jnp.cumsum(coarse_rows)
    block_starts = block_ends - coarse_rows
    slab_iota = jnp.arange(slab_count, dtype=jnp.int32)
    start_own = pick_entry(block_starts, slab_iota, slab_at)
    end_own = pick_entry(block_ends, slab_iota, slab_at)
    start_prev = pick_entry(block_starts, slab_iota, slab_at - 1)
    fine_x = slab_at * cells_x + jnp.arange(cells_x, dtype=jnp.int32)
    lower_x, upper_x, weight_x = node_weights(fine_x, slab_count * (cells_x // 2))
    source = padded(extended, (("slab", 0),), capacity)

    def locate(plane):
        return jnp.where(
            plane < start_own,
            plane - start_prev,
            jnp.where(
                plane < end_own, capacity + plane - start_own, 2 * capacity + plane - end_own
            ),
        )

    along_x = interpolation_matrix(locate(lower_x), locate(upper_x), weight_x, source.shape[0])
    coarse_slab = jnp.einsum("ir,ryz->iyz", along_x, source, precision=FULL_ACCURACY)
    fine_y = col_at * cells_y + jnp.arange(cells_y, dtype=jnp.int32)
    lower_y, upper_y, weight_y = node_weights(fine_y, col_count * coarse_y)
    y_offset = col_at * coarse_y - 1
    along_y = interpolation_matrix(lower_y - y_offset, upper_y - y_offset, weight_y, coarse_y + 2)
    coarse_columns = jnp.einsum("jy,iyz->ijz", along_y, coarse_slab, precision=FULL_ACCURACY)
    lower_z, upper_z, weight_z = node_weights(jnp.arange(cells_z, dtype=jnp.int32), coarse_z)
    vertical_direction = interpolation_matrix(lower_z, upper_z, weight_z, coarse_z)
    thermal_profile = jnp.einsum(
        "au,hwu->hwa", vertical_direction, coarse_columns, precision=FULL_ACCURACY
    )
    grain_mobility = jnp.exp(2.0 * (thermal_profile - 1.0))
    deposited = layer_mask.astype(jnp.float32)
    local_mobility = jnp.sum(deposited * grain_mobility)
    own_ids = block_ids(grain_ids, slab_at, col_at)
    prev_slab_ids = block_ids(grain_ids, jnp.maximum(slab_at - 1, 0), col_at)
    next_slab_ids = block_ids(grain_ids, jnp.minimum(slab_at + 1, slab_count - 1), col_at)
    prev_col_ids = block_ids(grain_ids, slab_at, jnp.maximum(col_at - 1, 0))
    next_col_ids = block_ids(grain_ids, slab_at, jnp.minimum(col_at + 1, col_count - 1))
    grain_iota = jnp.arange(energy.shape[0], dtype=jnp.int32)
    slot_energy = jnp.sum(
        jnp.where(own_ids[:, None] == grain_iota[None, :], energy[None, :], 0.0), axis=1
    )[:, None, None, None]
    pack_up_slab = packing(own_ids, next_slab_ids)
    pack_down_slab = packing(own_ids, prev_slab_ids)
    pack_up_col = packing(own_ids, next_col_ids)
    pack_down_col = packing(own_ids, prev_col_ids)
    below_map = unpacking(prev_slab_ids, own_ids)
    above_map = unpacking(next_slab_ids, own_ids)
    left_map = unpacking(prev_col_ids, own_ids)
    right_map = unpacking(next_col_ids, own_ids)
    fields = order_params
    zero_plane = jnp.zeros((slot_count, cells_x, cells_y, 1), jnp.float32)
    for step_index in range(STEPS):
        from_lower = passed_along(apply_slots(pack_up_slab, fields[:, -1]), "slab", 1)
        from_upper = passed_along(apply_slots(pack_down_slab, fields[:, 0]), "slab", -1)
        from_left = passed_along(apply_slots(pack_up_col, fields[:, :, -1]), "col", 1)
        from_right = passed_along(apply_slots(pack_down_col, fields[:, :, 0]), "col", -1)
        below = apply_slots(below_map, from_lower)
        above = apply_slots(above_map, from_upper)
        left_side = apply_slots(left_map, from_left)
        right_side = apply_slots(right_map, from_right)
        x_low = jnp.concatenate([below[:, None], fields[:, :-1]], axis=1)
        x_high = jnp.concatenate([fields[:, 1:], above[:, None]], axis=1)
        y_low = jnp.concatenate([left_side[:, :, None], fields[:, :, :-1]], axis=2)
        y_high = jnp.concatenate([fields[:, :, 1:], right_side[:, :, None]], axis=2)
        z_low = jnp.concatenate([zero_plane, fields[..., :-1]], axis=3)
        z_high = jnp.concatenate([fields[..., 1:], zero_plane], axis=3)
        laplace = x_low + x_high + y_low + y_high + z_low + z_high - 6.0 * fields
        rate = rates(fields, laplace, grain_mobility, slot_energy)
        local_rate = jnp.sum(deposited * jnp.sum(rate, axis=0))
        if step_index == 0:
            sums = total([local_rate, local_mobility])
            mobility_sum = sums[1] * slot_count
        else:
            sums = total([local_rate])
        multiplier = sums[0] / mobility_sum
        fields = fields + TIME_STEP * deposited * (rate - grain_mobility * multiplier)
    return fields


def solution(mesh):
    in_specs = (
        P(None, "slab", "col", None),
        P("slab", "col", None),
        P("slab", "col", None),
        P(),
        P(),
        P(),
    )
    out_specs = P(None, "slab", "col", None)
    return jax.shard_map(
        per_device, mesh=mesh, in_specs=in_specs, out_specs=out_specs, check_vma=False
    )
```

```python
import functools

import jax
import jax.numpy as jnp
import numpy as np
from jax import lax
from jax.experimental import pallas as pl
from jax.experimental.pallas import tpu as pltpu
from jax.sharding import PartitionSpec as P

SHARE = 4
STEPS = 4
TIME_STEP = 0.05
COUPLING = 1.5
BELOW, ABOVE, LEFT, RIGHT = range(4)
FACES = 4
LANES = 128
ROWS = 8
HIGHEST = lax.Precision.HIGHEST

VMEM = pl.BlockSpec(memory_space=pltpu.VMEM)
SMEM = pl.BlockSpec(memory_space=pltpu.SMEM)


def call(body, out_shape, in_specs, out_specs, scratch=(), flops=1000, size=1000):
    return pl.pallas_call(
        body,
        out_shape=out_shape,
        in_specs=in_specs,
        out_specs=out_specs,
        scratch_shapes=list(scratch),
        compiler_params=pltpu.CompilerParams(vmem_limit_bytes=20 << 20),
        cost_estimate=pl.CostEstimate(flops=flops, bytes_accessed=size, transcendentals=0),
    )


def f32(*shape):
    return jax.ShapeDtypeStruct(shape, jnp.float32)


def present(slabs, cols):
    s, c = lax.axis_index("slab"), lax.axis_index("col")
    return (s > 0, s < slabs - 1, c > 0, c < cols - 1)


def beside(slabs, cols):
    s, c = lax.axis_index("slab"), lax.axis_index("col")
    return (
        (jnp.maximum(s - 1, 0), c),
        (jnp.minimum(s + 1, slabs - 1), c),
        (s, jnp.maximum(c - 1, 0)),
        (s, jnp.minimum(c + 1, cols - 1)),
    )


def order_body(slabs, cols, slots, ids_ref, ids_smem, energy_ref, slots_ref, energy_out):
    s, c = lax.axis_index("slab"), lax.axis_index("col")
    sub = lax.broadcasted_iota(jnp.int32, (slots, LANES), 0)
    lane = lax.broadcasted_iota(jnp.int32, (slots, LANES), 1)
    own = jnp.zeros((slots, LANES), jnp.int32)
    own_energy = jnp.zeros((slots, LANES), jnp.float32)
    for q in range(slots):
        grain = ids_smem[s, c, q]
        own = jnp.where(sub == q, grain, own)
        own_energy = jnp.where(sub == q, energy_ref[grain], own_energy)
    one, zero = jnp.float32(1.0), jnp.float32(0.0)
    have = present(slabs, cols)
    matches, ranks = [], []
    for k, (ns, nc) in enumerate(beside(slabs, cols)):
        row = ids_ref[ns, pl.ds(nc, 1), :]
        row = jnp.concatenate([row, jnp.full((1, LANES - slots), -1, jnp.int32)], axis=1)
        row = jnp.broadcast_to(jnp.where(have[k], row, -1), (slots, LANES))
        hit = jnp.where((own == row) & (row >= 0), one, zero)
        shared = jnp.max(hit, axis=0, keepdims=True)
        matches.append(jnp.sum(hit, axis=1, keepdims=True))
        ranks.append(jnp.sum(jnp.where(row < own, shared, zero), axis=1, keepdims=True))
    free = one - (matches[0] + matches[1] + matches[2] + matches[3])
    subf = sub.astype(jnp.float32)
    lanef = lane.astype(jnp.float32)
    free_row = jnp.sum(jnp.where(sub == lane, free, zero), axis=0, keepdims=True)
    free_rank = jnp.sum(jnp.where(lane < sub, free_row, zero), axis=1, keepdims=True)
    place = jnp.zeros((slots, LANES), jnp.float32)
    skipped = jnp.int32(0)
    for k in range(FACES):
        at = matches[k] * (ranks[k] + k * SHARE - lanef)
        place = jnp.where((matches[k] > 0.5) & (jnp.abs(at) < 0.5), one, place)
        local = free_rank - (skipped * SHARE).astype(jnp.float32)
        inside = (local > -0.5) & (local < SHARE - 0.5) & (free > 0.5)
        inside = inside & jnp.logical_not(have[k])
        place = jnp.where(inside & (jnp.abs(local + k * SHARE - lanef) < 0.5), one, place)
        skipped = skipped + jnp.where(have[k], 0, 1)
    slot_row = jnp.sum(place * subf, axis=0, keepdims=True)
    energy_row = jnp.sum(place * own_energy, axis=0, keepdims=True)
    lane1 = lax.broadcasted_iota(jnp.int32, (1, LANES), 1)
    for q in range(slots):
        slots_ref[q] = jnp.sum(jnp.where(lane1 == q, slot_row, zero)).astype(jnp.int32)
        value = jnp.sum(jnp.where(lane1 == q, energy_row, zero), axis=1, keepdims=True)
        energy_out[q * ROWS : (q + 1) * ROWS, :] = jnp.broadcast_to(value, (ROWS, LANES))


def take(ref, at, rows, stride=1):
    half = ref.shape[0] // 2
    if stride == 1:
        if not isinstance(at, int):
            at = pl.multiple_of(at, ROWS)
        return ref[pl.ds(at, rows), :], ref[pl.ds(at + half, rows), :]
    return ref[pl.ds(at, rows, stride=stride), :], ref[pl.ds(at + half, rows, stride=stride), :]


def put(ref, at, i, value):
    if not isinstance(at, int):
        at = pl.multiple_of(at, ROWS)
    ref[pl.ds(at + i * (ref.shape[0] // 2), value.shape[0]), :] = value


def fill(out, index, pair):
    out[index, :, :LANES], out[index, :, LANES:] = pair


def pair_faces(axis, low, high):
    even = lax.rem(lax.axis_index(axis), 2) == 0
    return even, (jnp.where(even, high, low), jnp.where(even, low, high))


def pack_faces(fields, cx, cy, slots, out_refs, axis, columns):
    low, high = (LEFT, RIGHT) if columns else (BELOW, ABOVE)
    _, faces = pair_faces(axis, low, high)
    for out, face in zip(out_refs, faces):
        is_high = face == high
        for depth in range(2):
            if columns:
                first = jnp.where(is_high, cy - 1 - depth, depth)
                plane = lambda q: take(fields, q * (cx * cy) + first, cx, cy)
            else:
                first = jnp.where(is_high, cx - 1 - depth, depth) * cy
                plane = lambda q: take(fields, q * (cx * cy) + first, cy)
            for j in range(SHARE):
                fill(out, depth * SHARE + j, plane(face * SHARE + j))
            if depth == 0:
                s0 = s1 = None
                for q in range(slots):
                    v0, v1 = plane(q)
                    s0 = v0 * v0 if s0 is None else s0 + v0 * v0
                    s1 = v1 * v1 if s1 is None else s1 + v1 * v1
                fill(out, 2 * SHARE, (s0, s1))


def open_body(cx, cy, slots, fields_raw, mask_ref, coarse_ref, slots_ref, fields, msg_a, msg_b, mask_halves):
    cells = cx * cy
    for q in range(slots):
        at = pl.multiple_of(slots_ref[q] * cells, cells)
        for i in range(2):
            put(fields, q * cells, i, fields_raw[pl.ds(at, cells), i * LANES : (i + 1) * LANES])
    for i in range(2):
        put(mask_halves, 0, i, mask_ref[:, i * LANES : (i + 1) * LANES].astype(jnp.float32))
    pack_faces(fields, cx, cy, slots, (msg_a, msg_b), "col", True)
    _, faces = pair_faces("col", LEFT, RIGHT)
    capacity, coarse_y, _ = coarse_ref.shape
    for out, face in zip((msg_a, msg_b), faces):
        first = jnp.where(face == RIGHT, cy - 1, 0)
        fill(out, 2 * SHARE + 1, take(mask_halves, first, cx, cy))
        out[2 * SHARE + 2] = jnp.zeros((ROWS, out.shape[2]), jnp.float32)
        row = jnp.where(face == RIGHT, coarse_y - 1, 0)
        for p in range(capacity):
            out[2 * SHARE + 2, p : p + 1, :LANES] = coarse_ref[p, pl.ds(row, 1), :]


def slab_body(
    cx, cy, slots, slabs, cols, fields, mask_ref, coarse_ref, rows_ref, got_a, got_b, msg_a, msg_b, planes
):
    capacity, coarse_y, _ = coarse_ref.shape
    have = present(slabs, cols)
    even, _ = pair_faces("col", LEFT, RIGHT)
    thermal = 2 * SHARE + 2
    for p in range(capacity):
        from_a = got_a[thermal, p : p + 1, :LANES]
        from_b = got_b[thermal, p : p + 1, :LANES]
        lower = jnp.where(even, from_b, from_a)
        upper = jnp.where(even, from_a, from_b)
        base = p * ROWS
        planes[base : base + ROWS, :] = jnp.zeros((ROWS, LANES), jnp.float32)
        planes[base : base + 1, :] = jnp.where(have[LEFT], lower, coarse_ref[p, 0:1, :])
        planes[base + 1 : base + 1 + coarse_y, :] = coarse_ref[p]
        planes[base + 1 + coarse_y : base + 2 + coarse_y, :] = jnp.where(
            have[RIGHT], upper, coarse_ref[p, coarse_y - 1 : coarse_y, :]
        )
    pack_faces(fields, cx, cy, slots, (msg_a, msg_b), "slab", False)
    _, faces = pair_faces("slab", BELOW, ABOVE)
    live = rows_ref[lax.axis_index("slab")]
    for out, face in zip((msg_a, msg_b), faces):
        first = jnp.where(face == ABOVE, cx - 1, 0) * cy
        out[2 * SHARE + 1] = mask_ref[pl.ds(pl.multiple_of(first, ROWS), cy), :].astype(jnp.float32)
        row = jnp.where(face == ABOVE, live - 2, 0) * ROWS
        out[thermal, :, :LANES] = planes[pl.ds(pl.multiple_of(row, ROWS), ROWS), :]
        out[thermal, :, LANES:] = planes[pl.ds(pl.multiple_of(row + ROWS, ROWS), ROWS), :]


def axis_weights(cells):
    fine = np.arange(-1, cells + 1)
    lower = (2 * fine - 1) // 4
    weight = (2 * fine - 1 - 4 * lower) / 4.0
    out = np.zeros((cells + 2, cells // 2 + 2), np.float32)
    out[np.arange(cells + 2), lower + 1] += 1.0 - weight
    out[np.arange(cells + 2), lower + 2] += weight
    return out


def plane_weights(cx, cy):
    along, across = axis_weights(cx), axis_weights(cy)
    inner = [(x + 1, y + 1) for x in range(cx) for y in range(cy)]
    inner += [(0, y + 1) for y in range(cy)] + [(cx + 1, y + 1) for y in range(cy)]
    inner += [(x + 1, 0) for x in range(cx)] + [(x + 1, cy + 1) for x in range(cx)]
    out = np.zeros((len(inner), cx // 2 + 2, ROWS), np.float32)
    for row, (x, y) in enumerate(inner):
        out[row, :, : cy // 2 + 2] = along[x][:, None] * across[y][None, :]
    return out.reshape(len(inner), -1)


def height_weights(cells, coarse):
    fine = np.arange(cells)
    lower = (2 * fine - 1) // 4
    weight = (2 * fine - 1 - 4 * lower) / 4.0
    out = np.zeros((coarse, cells), np.float32)
    np.add.at(out, (np.clip(lower, 0, coarse - 1), fine), 1.0 - weight)
    np.add.at(out, (np.clip(lower + 1, 0, coarse - 1), fine), weight)
    return out


def mobility_body(
    cx, cy, slabs, cols, planes, rows_ref, mask_ref, weights, height, col_a, col_b, slab_a, slab_b, rate_ref, near
):
    s = lax.axis_index("slab")
    start = jnp.int32(0)
    for t in range(slabs):
        start = start + jnp.where(t < s, rows_ref[t], 0)
    end = start + rows_ref[s]
    even_s, _ = pair_faces("slab", BELOW, ABOVE)
    even_c, _ = pair_faces("col", LEFT, RIGHT)
    thermal, mask = 2 * SHARE + 2, 2 * SHARE + 1
    below = jnp.where(even_s, slab_b[thermal], slab_a[thermal])
    above = jnp.where(even_s, slab_a[thermal], slab_b[thermal])
    capacity = planes.shape[0] // ROWS
    for i in range(cx // 2 + 2):
        p = jnp.clip(s * (cx // 2) - 1 + i, 0, slabs * (cx // 2) - 1)
        own = planes[pl.ds(pl.multiple_of(jnp.clip(p - start, 0, capacity - 1) * ROWS, ROWS), ROWS), :]
        lower = jnp.where(p == start - 2, below[:, :LANES], below[:, LANES:])
        upper = jnp.where(p == end, above[:, :LANES], above[:, LANES:])
        near[i * ROWS : (i + 1) * ROWS, :] = jnp.where(p < start, lower, jnp.where(p < end, own, upper))
    flat = jnp.dot(weights[...], near[...], precision=HIGHEST, preferred_element_type=jnp.float32)
    profile = jnp.dot(flat, height[...], precision=HIGHEST, preferred_element_type=jnp.float32)
    mobility = jnp.exp(2.0 * (profile - 1.0)) * TIME_STEP
    cells = cx * cy
    rate_ref[0:cells, :] = mask_ref[...].astype(jnp.float32) * mobility[:cells]
    have = present(slabs, cols)
    masks = (
        jnp.where(even_s, slab_b[mask], slab_a[mask]),
        jnp.where(even_s, slab_a[mask], slab_b[mask]),
        jnp.where(even_c, col_b[mask], col_a[mask]),
        jnp.where(even_c, col_a[mask], col_b[mask]),
    )
    for k in range(FACES):
        at = cells + k * ROWS
        rate_ref[at : at + ROWS, :] = jnp.where(have[k], masks[k] * mobility[at : at + ROWS], 0.0)


def split(value):
    return value[:, :LANES], value[:, LANES:]


def along_height(v0, v1, first, last):
    r0, r1 = pltpu.roll(v0, 1, 1), pltpu.roll(v1, 1, 1)
    q0, q1 = pltpu.roll(v0, LANES - 1, 1), pltpu.roll(v1, LANES - 1, 1)
    return (
        jnp.where(first, 0.0, r0) + jnp.where(last, q1, q0),
        jnp.where(first, r0, r1) + jnp.where(last, 0.0, q1),
    )


def along_rows(v, top, bottom, lower, upper):
    down = jnp.where(top, 0.0 if lower is None else lower, pltpu.roll(v, 1, 0))
    up = jnp.where(bottom, 0.0 if upper is None else upper, pltpu.roll(v, ROWS - 1, 0))
    return down + up


def edges():
    lane = lax.broadcasted_iota(jnp.int32, (ROWS, LANES), 1)
    row = lax.broadcasted_iota(jnp.int32, (ROWS, LANES), 0)
    return lane == 0, lane == LANES - 1, row == 0, row == ROWS - 1


def spread_row(ref, base, x):
    row = ref[pl.ds(base + x, 1), :]
    return split(jnp.broadcast_to(row, (ROWS, 2 * LANES)))


def neighbours(x, last_x, load, centre, halo, kind, marks):
    first, last, top, bottom = marks
    v0, v1 = centre
    n0, n1 = along_height(v0, v1, first, last)
    low = high = (None, None)
    if kind == LEFT:
        low = halo(x)
    if kind == RIGHT:
        high = halo(x)
    n0 = n0 + along_rows(v0, top, bottom, low[0], high[0])
    n1 = n1 + along_rows(v1, top, bottom, low[1], high[1])
    sides = []
    if not (isinstance(x, int) and x == 0):
        sides.append(load(x - 1))
    elif kind == BELOW:
        sides.append(halo(None))
    if not (isinstance(x, int) and x == last_x):
        sides.append(load(x + 1))
    elif kind == ABOVE:
        sides.append(halo(None))
    for a, b in sides:
        n0, n1 = n0 + a, n1 + b
    return n0, n1


def over_planes(cx, visit, carry):
    carry = visit(0, carry)
    carry = lax.fori_loop(1, cx - 1, visit, carry)
    return visit(cx - 1, carry)


def slot_access(fields, halos, q, cells, cy):
    def load(x):
        return take(fields, q * cells + x * cy, cy)

    def halo(x):
        if x is None:
            return split(halos[q * ROWS : (q + 1) * ROWS, :])
        return spread_row(halos, q * ROWS, x)

    return load, halo


def plane_of(ref, base, x, cy):
    at = base + x * cy
    if not isinstance(x, int):
        at = pl.multiple_of(at, ROWS)
    return split(ref[pl.ds(at, cy), :])


def force_of(v, n, squares3, energy):
    return v * (squares3 + ((5.0 - energy) + v * (energy - 2.0 * v))) - n


def triple_squares(fields, x, slots, cells, cy):
    total = None
    for q in range(slots):
        v0, v1 = take(fields, q * cells + x * cy, cy)
        total = (v0 * v0, v1 * v1) if total is None else (total[0] + v0 * v0, total[1] + v1 * v1)
    return 2.0 * COUPLING * total[0], 2.0 * COUPLING * total[1]


def sums_body(
    cx, cy, slots, slabs, cols, devices, fields, rate_ref, energy, col_a, col_b, slab_a, slab_b,
    grown, grown_halo, sums_ref, halos, field_sum,
):
    cells = cx * cy
    marks = edges()
    first, last, top, bottom = marks
    have = present(slabs, cols)
    even_s, _ = pair_faces("slab", BELOW, ABOVE)
    even_c, _ = pair_faces("col", LEFT, RIGHT)
    arrived = ((slab_b, slab_a, even_s), (slab_a, slab_b, even_s), (col_b, col_a, even_c), (col_a, col_b, even_c))

    for k, (if_even, if_odd, even) in enumerate(arrived):
        pick = lambda i: jnp.where(even, if_even[i], if_odd[i])
        s0, s1 = split(2.0 * COUPLING * pick(2 * SHARE))
        h0, h1 = split(rate_ref[cells + k * ROWS : cells + (k + 1) * ROWS, :])
        for j in range(SHARE):
            q = k * SHARE + j
            plane = jnp.where(have[k], pick(j), 0.0)
            halos[q * ROWS : (q + 1) * ROWS, :] = plane
            v0, v1 = split(plane)
            o0, o1 = split(pick(SHARE + j))
            if k == BELOW:
                i0, i1 = take(fields, q * cells, cy)
            elif k == ABOVE:
                i0, i1 = take(fields, (q + 1) * cells - cy, cy)
            elif k == LEFT:
                i0, i1 = take(fields, q * cells, cx, cy)
            else:
                i0, i1 = take(fields, q * cells + cy - 1, cx, cy)
            n0, n1 = along_height(v0, v1, first, last)
            n0 = n0 + along_rows(v0, top, bottom, None, None) + o0 + i0
            n1 = n1 + along_rows(v1, top, bottom, None, None) + o1 + i1
            e = energy[q * ROWS : (q + 1) * ROWS, :]
            grown_halo[q * ROWS : (q + 1) * ROWS, :LANES] = v0 - h0 * force_of(v0, n0, s0, e)
            grown_halo[q * ROWS : (q + 1) * ROWS, LANES:] = v1 - h1 * force_of(v1, n1, s1, e)

    energy_sum = None
    for q in range(slots):
        e = energy[q * ROWS : (q + 1) * ROWS, :]
        energy_sum = e if energy_sum is None else energy_sum + e
    zero = jnp.zeros((ROWS, LANES), jnp.float32)

    def visit(x, carry):
        total, c0, c1, c2, c3, weight = carry
        squares = triple_squares(fields, x, slots, cells, cy)
        rate = plane_of(rate_ref, 0, x, cy)
        forces, powers = [zero, zero], [zero, zero]
        a1, a2, b1 = [zero, zero], [zero, zero], [zero, zero]
        for q in range(slots):
            load, halo = slot_access(fields, halos, q, cells, cy)
            centre = load(x)
            near = neighbours(x, cx - 1, load, centre, halo, q // SHARE, marks)
            e = energy[q * ROWS : (q + 1) * ROWS, :]
            for i in range(2):
                force = force_of(centre[i], near[i], squares[i], e)
                g = centre[i] - rate[i] * force
                put(grown, q * cells + x * cy, i, g)
                forces[i] = forces[i] + force
                powers[i] = powers[i] + g * ((5.0 - e) + g * (e - 2.0 * g))
                a1[i] = a1[i] + g
                a2[i] = a2[i] + g * g
                b1[i] = b1[i] + e * g
        at = x * cy if isinstance(x, int) else pl.multiple_of(x * cy, ROWS)
        for i in range(2):
            h = rate[i]
            field_sum[pl.ds(at, cy), i * LANES : (i + 1) * LANES] = a1[i]
            total = total + h * forces[i]
            c0 = c0 + h * (powers[i] + 2.0 * COUPLING * a1[i] * a2[i])
            linear = (
                energy_sum
                - 5.0 * slots
                - 2.0 * b1[i]
                + (6.0 - 2.0 * COUPLING * slots) * a2[i]
                - 4.0 * COUPLING * (a1[i] * a1[i])
            )
            c1 = c1 + h * h * linear
            c2 = c2 + h * h * h * (energy_sum + (6.0 * COUPLING * slots - 6.0) * a1[i])
            c3 = c3 + (h * h) * (h * h)
            weight = weight + h
        return total, c0, c1, c2, c3, weight

    total, c0, c1, c2, c3, weight = over_planes(cx, visit, (zero,) * 6)

    def face_sum(k, x):
        base = k * SHARE * ROWS
        if x is None:
            parts = [split(grown_halo[base + j * ROWS : base + (j + 1) * ROWS, :]) for j in range(SHARE)]
            rate = split(rate_ref[cells + k * ROWS : cells + (k + 1) * ROWS, :])
        else:
            parts = [spread_row(grown_halo, base + j * ROWS, x) for j in range(SHARE)]
            rate = spread_row(rate_ref, cells + k * ROWS, x)
        g = [parts[0][i] + parts[1][i] + parts[2][i] + parts[3][i] for i in range(2)]
        return g, rate

    def visit_sum(x, carry):
        c0, c1 = carry
        left, right = face_sum(LEFT, x), face_sum(RIGHT, x)
        rate = plane_of(rate_ref, 0, x, cy)
        sums = []
        for source, base, factor in ((field_sum, 0, 0), (rate_ref, 0, 1)):
            load = lambda y: plane_of(source, base, y, cy)
            v = load(x)
            near = list(along_height(v[0], v[1], first, last))
            for i in range(2):
                near[i] = near[i] + along_rows(v[i], top, bottom, None, None)
                if not (isinstance(x, int) and x == 0):
                    near[i] = near[i] + load(x - 1)[i]
                if not (isinstance(x, int) and x == cx - 1):
                    near[i] = near[i] + load(x + 1)[i]
                if factor:
                    near[i] = near[i] * float(slots)
                scale = float(SHARE) if factor else 1.0
                near[i] = near[i] + jnp.where(top, left[factor][i] * scale, 0.0)
                near[i] = near[i] + jnp.where(bottom, right[factor][i] * scale, 0.0)
                if isinstance(x, int):
                    near[i] = near[i] + face_sum(BELOW if x == 0 else ABOVE, None)[factor][i] * scale
            sums.append(near)
        for i in range(2):
            c0 = c0 - rate[i] * sums[0][i]
            c1 = c1 + rate[i] * sums[1][i]
        return c0, c1

    c0, c1 = over_planes(cx, visit_sum, (c0, c1))
    back = -1.0 / TIME_STEP
    scales = (back, back, back, back, back * (2.0 * slots - 2.0 * COUPLING * slots * slots), 1.0 / TIME_STEP)
    lane = lax.broadcasted_iota(jnp.int32, (1, LANES), 1)
    row = jnp.zeros((1, LANES), jnp.float32)
    for i, (part, scale) in enumerate(zip((total, c0, c1, c2, c3, weight), scales)):
        value = jnp.sum(jnp.sum(part, axis=0, keepdims=True), axis=1, keepdims=True) * scale
        row = jnp.where(lane == i, value, row)
    sums_ref[...] = jnp.broadcast_to(row[None], (devices, 1, LANES))


def multipliers(got, slots):
    total = jnp.sum(got[...], axis=0)
    lane = lax.broadcasted_iota(jnp.int32, (1, LANES), 1)
    part = [jnp.sum(jnp.where(lane == i, total, 0.0), axis=1, keepdims=True) for i in range(6)]
    whole = slots * part[5]
    here = part[0] / whole
    later = (part[1] + here * (part[2] + here * (part[3] + here * part[4]))) / whole
    spread = lambda value: jnp.broadcast_to(value, (ROWS, LANES))
    return spread(here), spread(later)


def advance(cx, cy, slots, got, grown, grown_halo, rate_ref, energy, halos, now, squares_ref, store):
    cells = cx * cy
    marks = edges()
    here, later = multipliers(got, slots)
    for k in range(FACES):
        h0, h1 = split(rate_ref[cells + k * ROWS : cells + (k + 1) * ROWS, :])
        for q in range(k * SHARE, (k + 1) * SHARE):
            v0, v1 = split(grown_halo[q * ROWS : (q + 1) * ROWS, :])
            halos[q * ROWS : (q + 1) * ROWS, :LANES] = v0 - here * h0
            halos[q * ROWS : (q + 1) * ROWS, LANES:] = v1 - here * h1

    def settle(x, carry):
        base = pl.multiple_of(x * cy, ROWS)
        h = split(rate_ref[pl.ds(base, cy), :])
        off = [here * h[i] for i in range(2)]
        squares = [None, None]
        for q in range(slots):
            at = q * cells + x * cy
            v = take(grown, at, cy)
            for i in range(2):
                f = v[i] - off[i]
                put(now, at, i, f)
                squares[i] = f * f if squares[i] is None else squares[i] + f * f
        for i in range(2):
            squares_ref[pl.ds(base, cy), i * LANES : (i + 1) * LANES] = 2.0 * COUPLING * squares[i]
        return carry

    lax.fori_loop(0, cx, settle, 0)

    def visit(x, carry):
        squares = plane_of(squares_ref, 0, x, cy)
        rate = plane_of(rate_ref, 0, x, cy)
        for q in range(slots):
            load, halo = slot_access(now, halos, q, cells, cy)
            centre = load(x)
            near = neighbours(x, cx - 1, load, centre, halo, q // SHARE, marks)
            e = energy[q * ROWS : (q + 1) * ROWS, :]
            for i in range(2):
                force = force_of(centre[i], near[i], squares[i], e)
                store(q, x, i, centre[i] - rate[i] * (force + later))
        return carry

    over_planes(cx, visit, 0)


def middle_body(
    cx, cy, slots, got, grown, grown_halo, rate_ref, energy, fields, col_a, col_b, slab_a, slab_b,
    halos, now, squares_ref,
):
    cells = cx * cy

    def store(q, x, i, value):
        put(fields, q * cells + x * cy, i, value)

    advance(cx, cy, slots, got, grown, grown_halo, rate_ref, energy, halos, now, squares_ref, store)
    pack_faces(fields, cx, cy, slots, (slab_a, slab_b), "slab", False)
    pack_faces(fields, cx, cy, slots, (col_a, col_b), "col", True)


def last_body(cx, cy, slots, got, grown, grown_halo, rate_ref, energy, slots_ref, out, halos, now, squares_ref):
    cells = cx * cy

    def store(q, x, i, value):
        at = pl.multiple_of(slots_ref[q] * cells + x * cy, ROWS)
        out[pl.ds(at, cy), i * LANES : (i + 1) * LANES] = value

    advance(cx, cy, slots, got, grown, grown_halo, rate_ref, energy, halos, now, squares_ref, store)


def exchange(first, second, axis):
    count = lax.axis_size(axis)
    one = [(i, i ^ 1) for i in range(count)]
    two = [(i, (i - 1) % count if i % 2 == 0 else (i + 1) % count) for i in range(count)]
    return lax.ppermute(first, axis, one), lax.ppermute(second, axis, two)


def per_device(order_params, layer_mask, coarse_temp, coarse_rows, grain_ids, energy):
    slots, cx, cy, cz = order_params.shape
    slabs, cols = lax.axis_size("slab"), lax.axis_size("col")
    devices = slabs * cols
    cells = cx * cy
    capacity, _, coarse_z = coarse_temp.shape
    raw = order_params.reshape(slots * cells, cz)
    mask = layer_mask.reshape(cells, cz)
    wide = FACES * ROWS
    message = f32(2 * SHARE + 3, ROWS, cz)
    short = f32(2 * SHARE + 1, ROWS, cz)
    state = f32(2 * slots * cells, cz // 2)
    halo = f32(slots * ROWS, cz)

    slot_order, slot_energy = call(
        functools.partial(order_body, slabs, cols, slots),
        (jax.ShapeDtypeStruct((slots,), jnp.int32), f32(slots * ROWS, LANES)),
        [VMEM, SMEM, SMEM],
        (SMEM, VMEM),
    )(grain_ids, grain_ids, energy)
    fields, col_a, col_b = call(
        functools.partial(open_body, cx, cy, slots),
        (state, message, message),
        [VMEM, VMEM, VMEM, SMEM],
        (VMEM,) * 3,
        [pltpu.VMEM((2 * cells, cz // 2), jnp.float32)],
    )(raw, mask, coarse_temp, slot_order)
    col_a, col_b = exchange(col_a, col_b, "col")
    slab_a, slab_b, planes = call(
        functools.partial(slab_body, cx, cy, slots, slabs, cols),
        (message, message, f32(capacity * ROWS, LANES)),
        [VMEM, VMEM, VMEM, SMEM, VMEM, VMEM],
        (VMEM,) * 3,
    )(fields, mask, coarse_temp, coarse_rows, col_a, col_b)
    slab_a, slab_b = exchange(slab_a, slab_b, "slab")
    weights = jnp.asarray(plane_weights(cx, cy))
    height = jnp.asarray(height_weights(cz, coarse_z))
    rate = call(
        functools.partial(mobility_body, cx, cy, slabs, cols),
        f32(cells + wide, cz),
        [VMEM, SMEM] + [VMEM] * 7,
        VMEM,
        [pltpu.VMEM(((cx // 2 + 2) * ROWS, LANES), jnp.float32)],
    )(planes, coarse_rows, mask, weights, height, col_a, col_b, slab_a, slab_b)

    buffers = [pltpu.VMEM(halo.shape, jnp.float32), pltpu.VMEM(state.shape, jnp.float32)]
    buffers += [pltpu.VMEM((cells, cz), jnp.float32)]
    for pair in range(STEPS // 2):
        grown, grown_halo, sums = call(
            functools.partial(sums_body, cx, cy, slots, slabs, cols, devices),
            (state, halo, f32(devices, 1, LANES)),
            [VMEM] * 7,
            (VMEM,) * 3,
            [pltpu.VMEM(halo.shape, jnp.float32), pltpu.VMEM((cells, cz), jnp.float32)],
        )(fields, rate, slot_energy, col_a, col_b, slab_a, slab_b)
        got = lax.all_to_all(sums, ("slab", "col"), 0, 0)
        if pair < STEPS // 2 - 1:
            fields, col_a, col_b, slab_a, slab_b = call(
                functools.partial(middle_body, cx, cy, slots),
                (state, short, short, short, short),
                [VMEM] * 5,
                (VMEM,) * 5,
                buffers,
            )(got, grown, grown_halo, rate, slot_energy)
            slab_a, slab_b = exchange(slab_a, slab_b, "slab")
            col_a, col_b = exchange(col_a, col_b, "col")
        else:
            fields = call(
                functools.partial(last_body, cx, cy, slots),
                f32(slots * cells, cz),
                [VMEM] * 5 + [SMEM],
                VMEM,
                buffers,
            )(got, grown, grown_halo, rate, slot_energy, slot_order)
    return fields.reshape(order_params.shape)


def solution(mesh):
    in_specs = (
        P(None, "slab", "col", None),
        P("slab", "col", None),
        P("slab", "col", None),
        P(),
        P(),
        P(),
    )
    out_specs = P(None, "slab", "col", None)
    return jax.shard_map(
        per_device, mesh=mesh, in_specs=in_specs, out_specs=out_specs, check_vma=False
    )
```

```python
import functools

import jax
import jax.numpy as jnp
import numpy as np
from jax import lax
from jax.experimental import pallas as pl
from jax.experimental.pallas import tpu as pltpu
from jax.sharding import PartitionSpec as P

SHARE = 4
STEPS = 4
TIME_STEP = 0.05
COUPLING = 1.5
BELOW, ABOVE, LEFT, RIGHT = range(4)
FACES = 4
LANES = 128
ROWS = 8
HIGHEST = lax.Precision.HIGHEST

VMEM = pl.BlockSpec(memory_space=pltpu.VMEM)
SMEM = pl.BlockSpec(memory_space=pltpu.SMEM)
HBM = pl.BlockSpec(memory_space=pltpu.HBM)


def call(body, out_shape, in_specs, out_specs, scratch=(), flops=1 << 20, size=1 << 20):
    return pl.pallas_call(
        body,
        out_shape=out_shape,
        in_specs=in_specs,
        out_specs=out_specs,
        scratch_shapes=list(scratch),
        compiler_params=pltpu.CompilerParams(vmem_limit_bytes=20 << 20),
        cost_estimate=pl.CostEstimate(flops=flops, bytes_accessed=size, transcendentals=0),
    )


def f32(*shape):
    return jax.ShapeDtypeStruct(shape, jnp.float32)


def present(slabs, cols):
    s, c = lax.axis_index("slab"), lax.axis_index("col")
    return (s > 0, s < slabs - 1, c > 0, c < cols - 1)


def beside(slabs, cols):
    s, c = lax.axis_index("slab"), lax.axis_index("col")
    return (
        (jnp.maximum(s - 1, 0), c),
        (jnp.minimum(s + 1, slabs - 1), c),
        (s, jnp.maximum(c - 1, 0)),
        (s, jnp.minimum(c + 1, cols - 1)),
    )


def slot_places(slabs, cols, slots, ids_ref, ids_smem):
    s, c = lax.axis_index("slab"), lax.axis_index("col")
    sub = lax.broadcasted_iota(jnp.int32, (slots, LANES), 0)
    lane = lax.broadcasted_iota(jnp.int32, (slots, LANES), 1)
    own = jnp.zeros((slots, LANES), jnp.int32)
    for q in range(slots):
        own = jnp.where(sub == q, ids_smem[s, c, q], own)
    one, zero = jnp.float32(1.0), jnp.float32(0.0)
    have = present(slabs, cols)
    matches, ranks = [], []
    for k, (ns, nc) in enumerate(beside(slabs, cols)):
        row = ids_ref[ns, pl.ds(nc, 1), :]
        row = jnp.concatenate([row, jnp.full((1, LANES - slots), -1, jnp.int32)], axis=1)
        row = jnp.broadcast_to(jnp.where(have[k], row, -1), (slots, LANES))
        hit = jnp.where((own == row) & (row >= 0), one, zero)
        shared = jnp.max(hit, axis=0, keepdims=True)
        matches.append(jnp.sum(hit, axis=1, keepdims=True))
        ranks.append(jnp.sum(jnp.where(row < own, shared, zero), axis=1, keepdims=True))
    free = one - (matches[0] + matches[1] + matches[2] + matches[3])
    lanef = lane.astype(jnp.float32)
    free_row = jnp.sum(jnp.where(sub == lane, free, zero), axis=0, keepdims=True)
    free_rank = jnp.sum(jnp.where(lane < sub, free_row, zero), axis=1, keepdims=True)
    place = jnp.zeros((slots, LANES), jnp.float32)
    skipped = jnp.int32(0)
    for k in range(FACES):
        at = matches[k] * (ranks[k] + k * SHARE - lanef)
        place = jnp.where((matches[k] > 0.5) & (jnp.abs(at) < 0.5), one, place)
        local = free_rank - (skipped * SHARE).astype(jnp.float32)
        inside = (local > -0.5) & (local < SHARE - 0.5) & (free > 0.5)
        inside = inside & jnp.logical_not(have[k])
        place = jnp.where(inside & (jnp.abs(local + k * SHARE - lanef) < 0.5), one, place)
        skipped = skipped + jnp.where(have[k], 0, 1)
    return place


def take(ref, at, rows, stride=1):
    half = ref.shape[0] // 2
    if stride == 1:
        if not isinstance(at, int):
            at = pl.multiple_of(at, ROWS)
        return ref[pl.ds(at, rows), :], ref[pl.ds(at + half, rows), :]
    return ref[pl.ds(at, rows, stride=stride), :], ref[pl.ds(at + half, rows, stride=stride), :]


def put(ref, at, i, value):
    if not isinstance(at, int):
        at = pl.multiple_of(at, ROWS)
    ref[pl.ds(at + i * (ref.shape[0] // 2), value.shape[0]), :] = value


def fill(out, index, pair):
    out[index, :, :LANES], out[index, :, LANES:] = pair


def pair_faces(axis, low, high):
    even = lax.rem(lax.axis_index(axis), 2) == 0
    return even, (jnp.where(even, high, low), jnp.where(even, low, high))


def pack_faces(fields, cx, cy, slots, out_refs, axis, columns, slot_of=lambda place: place):
    low, high = (LEFT, RIGHT) if columns else (BELOW, ABOVE)
    _, faces = pair_faces(axis, low, high)
    for out, face in zip(out_refs, faces):
        is_high = face == high
        for depth in range(2):
            if columns:
                first = jnp.where(is_high, cy - 1 - depth, depth)
                plane = lambda q: take(fields, q * (cx * cy) + first, cx, cy)
            else:
                first = jnp.where(is_high, cx - 1 - depth, depth) * cy
                plane = lambda q: take(fields, q * (cx * cy) + first, cy)
            for j in range(SHARE):
                fill(out, depth * SHARE + j, plane(slot_of(face * SHARE + j)))
            if depth == 0:
                s0 = s1 = None
                for q in range(slots):
                    v0, v1 = plane(q)
                    s0 = v0 * v0 if s0 is None else s0 + v0 * v0
                    s1 = v1 * v1 if s1 is None else s1 + v1 * v1
                fill(out, 2 * SHARE, (s0, s1))


def open_body(
    cx, cy, slots, slabs, cols, ids_hbm, fields_hbm, mask_hbm, coarse_hbm,
    raw, mask, slots_ref, msg_a, msg_b, ids_smem, ids_ref, coarse_ref, mask_ref, sems,
):
    cells = cx * cy
    loads = [
        pltpu.make_async_copy(ids_hbm, ids_smem, sems.at[0]),
        pltpu.make_async_copy(ids_hbm, ids_ref, sems.at[1]),
        pltpu.make_async_copy(coarse_hbm, coarse_ref, sems.at[2]),
    ]
    for i in range(2):
        half = pl.ds(i * LANES, LANES)
        loads.append(
            pltpu.make_async_copy(mask_hbm.at[:, half], mask_ref.at[pl.ds(i * cells, cells), :], sems.at[3 + i])
        )
        rows = slots * cells
        loads.append(
            pltpu.make_async_copy(fields_hbm.at[:, half], raw.at[pl.ds(i * rows, rows), :], sems.at[5 + i])
        )
    for load in loads:
        load.start()
    loads[0].wait()
    loads[1].wait()
    place = slot_places(slabs, cols, slots, ids_ref, ids_smem)
    sub = lax.broadcasted_iota(jnp.int32, (slots, LANES), 0).astype(jnp.float32)
    slot_row = jnp.sum(place * sub, axis=0, keepdims=True)
    lane = lax.broadcasted_iota(jnp.int32, (1, LANES), 1)
    for q in range(slots):
        slots_ref[q] = jnp.sum(jnp.where(lane == q, slot_row, 0.0)).astype(jnp.int32)
    for load in loads[2:]:
        load.wait()
    mask[...] = mask_ref[...].astype(jnp.float32)
    pack_faces(raw, cx, cy, slots, (msg_a, msg_b), "col", True, lambda place: slots_ref[place])
    _, faces = pair_faces("col", LEFT, RIGHT)
    capacity, coarse_y, _ = coarse_ref.shape
    for out, face in zip((msg_a, msg_b), faces):
        first = jnp.where(face == RIGHT, cy - 1, 0)
        fill(out, 2 * SHARE + 1, take(mask, first, cx, cy))
        out[2 * SHARE + 2] = jnp.zeros((ROWS, out.shape[2]), jnp.float32)
        row = jnp.where(face == RIGHT, coarse_y - 1, 0)
        for p in range(capacity):
            out[2 * SHARE + 2, p : p + 1, :LANES] = coarse_ref[p, pl.ds(row, 1), :]


def arrange_body(cells, slots, raw, slots_ref, ids_ref, energy_ref, fields, energy_out):
    s, c = lax.axis_index("slab"), lax.axis_index("col")
    for q in range(slots):
        slot = slots_ref[q]
        for i, part in enumerate(take(raw, slot * cells, cells)):
            put(fields, q * cells, i, part)
        value = jnp.full((ROWS, LANES), energy_ref[ids_ref[s, c, slot]], jnp.float32)
        energy_out[q * ROWS : (q + 1) * ROWS, :] = value


def slab_body(
    cx, cy, slots, slabs, cols, fields, mask_ref, coarse_ref, rows_ref, got_a, got_b, msg_a, msg_b, planes
):
    capacity, coarse_y, _ = coarse_ref.shape
    have = present(slabs, cols)
    even, _ = pair_faces("col", LEFT, RIGHT)
    thermal = 2 * SHARE + 2
    for p in range(capacity):
        from_a = got_a[thermal, p : p + 1, :LANES]
        from_b = got_b[thermal, p : p + 1, :LANES]
        lower = jnp.where(even, from_b, from_a)
        upper = jnp.where(even, from_a, from_b)
        base = p * ROWS
        planes[base : base + ROWS, :] = jnp.zeros((ROWS, LANES), jnp.float32)
        planes[base : base + 1, :] = jnp.where(have[LEFT], lower, coarse_ref[p, 0:1, :])
        planes[base + 1 : base + 1 + coarse_y, :] = coarse_ref[p]
        planes[base + 1 + coarse_y : base + 2 + coarse_y, :] = jnp.where(
            have[RIGHT], upper, coarse_ref[p, coarse_y - 1 : coarse_y, :]
        )
    pack_faces(fields, cx, cy, slots, (msg_a, msg_b), "slab", False)
    _, faces = pair_faces("slab", BELOW, ABOVE)
    live = rows_ref[lax.axis_index("slab")]
    for out, face in zip((msg_a, msg_b), faces):
        first = jnp.where(face == ABOVE, cx - 1, 0) * cy
        fill(out, 2 * SHARE + 1, take(mask_ref, first, cy))
        row = jnp.where(face == ABOVE, live - 2, 0) * ROWS
        out[thermal, :, :LANES] = planes[pl.ds(pl.multiple_of(row, ROWS), ROWS), :]
        out[thermal, :, LANES:] = planes[pl.ds(pl.multiple_of(row + ROWS, ROWS), ROWS), :]


def axis_weights(cells):
    fine = np.arange(-1, cells + 1)
    lower = (2 * fine - 1) // 4
    weight = (2 * fine - 1 - 4 * lower) / 4.0
    out = np.zeros((cells + 2, cells // 2 + 2), np.float32)
    out[np.arange(cells + 2), lower + 1] += 1.0 - weight
    out[np.arange(cells + 2), lower + 2] += weight
    return out


def plane_weights(cx, cy):
    along, across = axis_weights(cx), axis_weights(cy)
    inner = [(x + 1, y + 1) for x in range(cx) for y in range(cy)]
    inner += [(0, y + 1) for y in range(cy)] + [(cx + 1, y + 1) for y in range(cy)]
    inner += [(x + 1, 0) for x in range(cx)] + [(x + 1, cy + 1) for x in range(cx)]
    out = np.zeros((len(inner), cx // 2 + 2, ROWS), np.float32)
    for row, (x, y) in enumerate(inner):
        out[row, :, : cy // 2 + 2] = along[x][:, None] * across[y][None, :]
    return out.reshape(len(inner), -1)


def height_weights(cells, coarse):
    fine = np.arange(cells)
    lower = (2 * fine - 1) // 4
    weight = (2 * fine - 1 - 4 * lower) / 4.0
    out = np.zeros((coarse, cells), np.float32)
    np.add.at(out, (np.clip(lower, 0, coarse - 1), fine), 1.0 - weight)
    np.add.at(out, (np.clip(lower + 1, 0, coarse - 1), fine), weight)
    return out


def mobility_body(
    cx, cy, slabs, cols, planes, rows_ref, mask_ref, weights, height, col_a, col_b, slab_a, slab_b, rate_ref, near
):
    s = lax.axis_index("slab")
    start = jnp.int32(0)
    for t in range(slabs):
        start = start + jnp.where(t < s, rows_ref[t], 0)
    end = start + rows_ref[s]
    even_s, _ = pair_faces("slab", BELOW, ABOVE)
    even_c, _ = pair_faces("col", LEFT, RIGHT)
    thermal, mask = 2 * SHARE + 2, 2 * SHARE + 1
    below = jnp.where(even_s, slab_b[thermal], slab_a[thermal])
    above = jnp.where(even_s, slab_a[thermal], slab_b[thermal])
    capacity = planes.shape[0] // ROWS
    for i in range(cx // 2 + 2):
        p = jnp.clip(s * (cx // 2) - 1 + i, 0, slabs * (cx // 2) - 1)
        own = planes[pl.ds(pl.multiple_of(jnp.clip(p - start, 0, capacity - 1) * ROWS, ROWS), ROWS), :]
        lower = jnp.where(p == start - 2, below[:, :LANES], below[:, LANES:])
        upper = jnp.where(p == end, above[:, :LANES], above[:, LANES:])
        near[i * ROWS : (i + 1) * ROWS, :] = jnp.where(p < start, lower, jnp.where(p < end, own, upper))
    flat = jnp.dot(weights[...], near[...], precision=HIGHEST, preferred_element_type=jnp.float32)
    profile = jnp.dot(flat, height[...], precision=HIGHEST, preferred_element_type=jnp.float32)
    mobility = jnp.exp(2.0 * (profile - 1.0)) * TIME_STEP
    cells = cx * cy
    for i, part in enumerate(take(mask_ref, 0, cells)):
        half = slice(i * LANES, (i + 1) * LANES)
        rate_ref[0:cells, half] = part * mobility[:cells, half]
    have = present(slabs, cols)
    masks = (
        jnp.where(even_s, slab_b[mask], slab_a[mask]),
        jnp.where(even_s, slab_a[mask], slab_b[mask]),
        jnp.where(even_c, col_b[mask], col_a[mask]),
        jnp.where(even_c, col_a[mask], col_b[mask]),
    )
    for k in range(FACES):
        at = cells + k * ROWS
        rate_ref[at : at + ROWS, :] = jnp.where(have[k], masks[k] * mobility[at : at + ROWS], 0.0)


def split(value):
    return value[:, :LANES], value[:, LANES:]


def along_height(v0, v1, first, last):
    r0, r1 = pltpu.roll(v0, 1, 1), pltpu.roll(v1, 1, 1)
    q0, q1 = pltpu.roll(v0, LANES - 1, 1), pltpu.roll(v1, LANES - 1, 1)
    return (
        jnp.where(first, 0.0, r0) + jnp.where(last, q1, q0),
        jnp.where(first, r0, r1) + jnp.where(last, 0.0, q1),
    )


def along_rows(v, top, bottom, lower, upper):
    down = jnp.where(top, 0.0 if lower is None else lower, pltpu.roll(v, 1, 0))
    up = jnp.where(bottom, 0.0 if upper is None else upper, pltpu.roll(v, ROWS - 1, 0))
    return down + up


def edges():
    lane = lax.broadcasted_iota(jnp.int32, (ROWS, LANES), 1)
    row = lax.broadcasted_iota(jnp.int32, (ROWS, LANES), 0)
    return lane == 0, lane == LANES - 1, row == 0, row == ROWS - 1


def spread_row(ref, base, x):
    row = ref[pl.ds(base + x, 1), :]
    return split(jnp.broadcast_to(row, (ROWS, 2 * LANES)))


def neighbours(x, last_x, load, centre, halo, kind, marks):
    first, last, top, bottom = marks
    v0, v1 = centre
    n0, n1 = along_height(v0, v1, first, last)
    low = high = (None, None)
    if kind == LEFT:
        low = halo(x)
    if kind == RIGHT:
        high = halo(x)
    n0 = n0 + along_rows(v0, top, bottom, low[0], high[0])
    n1 = n1 + along_rows(v1, top, bottom, low[1], high[1])
    sides = []
    if not (isinstance(x, int) and x == 0):
        sides.append(load(x - 1))
    elif kind == BELOW:
        sides.append(halo(None))
    if not (isinstance(x, int) and x == last_x):
        sides.append(load(x + 1))
    elif kind == ABOVE:
        sides.append(halo(None))
    for a, b in sides:
        n0, n1 = n0 + a, n1 + b
    return n0, n1


def over_planes(cx, visit, carry):
    carry = visit(0, carry)
    carry = lax.fori_loop(1, cx - 1, visit, carry)
    return visit(cx - 1, carry)


def slot_access(fields, halos, q, cells, cy):
    def load(x):
        return take(fields, q * cells + x * cy, cy)

    def halo(x):
        if x is None:
            return split(halos[q * ROWS : (q + 1) * ROWS, :])
        return spread_row(halos, q * ROWS, x)

    return load, halo


def plane_of(ref, base, x, cy):
    at = base + x * cy
    if not isinstance(x, int):
        at = pl.multiple_of(at, ROWS)
    return split(ref[pl.ds(at, cy), :])


def force_of(v, n, squares3, energy):
    return v * (squares3 + ((5.0 - energy) + v * (energy - 2.0 * v))) - n


def triple_squares(fields, x, slots, cells, cy):
    total = None
    for q in range(slots):
        v0, v1 = take(fields, q * cells + x * cy, cy)
        total = (v0 * v0, v1 * v1) if total is None else (total[0] + v0 * v0, total[1] + v1 * v1)
    return 2.0 * COUPLING * total[0], 2.0 * COUPLING * total[1]


def sums_body(
    cx, cy, slots, slabs, cols, devices, fields, rate_ref, energy, col_a, col_b, slab_a, slab_b,
    grown, grown_halo, sums_ref, halos, field_sum,
):
    cells = cx * cy
    marks = edges()
    first, last, top, bottom = marks
    have = present(slabs, cols)
    even_s, _ = pair_faces("slab", BELOW, ABOVE)
    even_c, _ = pair_faces("col", LEFT, RIGHT)
    arrived = ((slab_b, slab_a, even_s), (slab_a, slab_b, even_s), (col_b, col_a, even_c), (col_a, col_b, even_c))

    for k, (if_even, if_odd, even) in enumerate(arrived):
        pick = lambda i: jnp.where(even, if_even[i], if_odd[i])
        s0, s1 = split(2.0 * COUPLING * pick(2 * SHARE))
        h0, h1 = split(rate_ref[cells + k * ROWS : cells + (k + 1) * ROWS, :])
        for j in range(SHARE):
            q = k * SHARE + j
            plane = jnp.where(have[k], pick(j), 0.0)
            halos[q * ROWS : (q + 1) * ROWS, :] = plane
            v0, v1 = split(plane)
            o0, o1 = split(pick(SHARE + j))
            if k == BELOW:
                i0, i1 = take(fields, q * cells, cy)
            elif k == ABOVE:
                i0, i1 = take(fields, (q + 1) * cells - cy, cy)
            elif k == LEFT:
                i0, i1 = take(fields, q * cells, cx, cy)
            else:
                i0, i1 = take(fields, q * cells + cy - 1, cx, cy)
            n0, n1 = along_height(v0, v1, first, last)
            n0 = n0 + along_rows(v0, top, bottom, None, None) + o0 + i0
            n1 = n1 + along_rows(v1, top, bottom, None, None) + o1 + i1
            e = energy[q * ROWS : (q + 1) * ROWS, :]
            grown_halo[q * ROWS : (q + 1) * ROWS, :LANES] = v0 - h0 * force_of(v0, n0, s0, e)
            grown_halo[q * ROWS : (q + 1) * ROWS, LANES:] = v1 - h1 * force_of(v1, n1, s1, e)

    energy_sum = None
    for q in range(slots):
        e = energy[q * ROWS : (q + 1) * ROWS, :]
        energy_sum = e if energy_sum is None else energy_sum + e
    zero = jnp.zeros((ROWS, LANES), jnp.float32)

    def visit(x, carry):
        total, c0, c1, c2, c3, weight = carry
        squares = triple_squares(fields, x, slots, cells, cy)
        rate = plane_of(rate_ref, 0, x, cy)
        forces, powers = [zero, zero], [zero, zero]
        a1, a2, b1 = [zero, zero], [zero, zero], [zero, zero]
        for q in range(slots):
            load, halo = slot_access(fields, halos, q, cells, cy)
            centre = load(x)
            near = neighbours(x, cx - 1, load, centre, halo, q // SHARE, marks)
            e = energy[q * ROWS : (q + 1) * ROWS, :]
            for i in range(2):
                force = force_of(centre[i], near[i], squares[i], e)
                g = centre[i] - rate[i] * force
                put(grown, q * cells + x * cy, i, g)
                forces[i] = forces[i] + force
                powers[i] = powers[i] + g * ((5.0 - e) + g * (e - 2.0 * g))
                a1[i] = a1[i] + g
                a2[i] = a2[i] + g * g
                b1[i] = b1[i] + e * g
        at = x * cy if isinstance(x, int) else pl.multiple_of(x * cy, ROWS)
        for i in range(2):
            h = rate[i]
            field_sum[pl.ds(at, cy), i * LANES : (i + 1) * LANES] = a1[i]
            total = total + h * forces[i]
            c0 = c0 + h * (powers[i] + 2.0 * COUPLING * a1[i] * a2[i])
            linear = (
                energy_sum
                - 5.0 * slots
                - 2.0 * b1[i]
                + (6.0 - 2.0 * COUPLING * slots) * a2[i]
                - 4.0 * COUPLING * (a1[i] * a1[i])
            )
            c1 = c1 + h * h * linear
            c2 = c2 + h * h * h * (energy_sum + (6.0 * COUPLING * slots - 6.0) * a1[i])
            c3 = c3 + (h * h) * (h * h)
            weight = weight + h
        return total, c0, c1, c2, c3, weight

    total, c0, c1, c2, c3, weight = over_planes(cx, visit, (zero,) * 6)

    def face_sum(k, x):
        base = k * SHARE * ROWS
        if x is None:
            parts = [split(grown_halo[base + j * ROWS : base + (j + 1) * ROWS, :]) for j in range(SHARE)]
            rate = split(rate_ref[cells + k * ROWS : cells + (k + 1) * ROWS, :])
        else:
            parts = [spread_row(grown_halo, base + j * ROWS, x) for j in range(SHARE)]
            rate = spread_row(rate_ref, cells + k * ROWS, x)
        g = [parts[0][i] + parts[1][i] + parts[2][i] + parts[3][i] for i in range(2)]
        return g, rate

    def visit_sum(x, carry):
        c0, c1 = carry
        left, right = face_sum(LEFT, x), face_sum(RIGHT, x)
        rate = plane_of(rate_ref, 0, x, cy)
        sums = []
        for source, base, factor in ((field_sum, 0, 0), (rate_ref, 0, 1)):
            load = lambda y: plane_of(source, base, y, cy)
            v = load(x)
            near = list(along_height(v[0], v[1], first, last))
            for i in range(2):
                near[i] = near[i] + along_rows(v[i], top, bottom, None, None)
                if not (isinstance(x, int) and x == 0):
                    near[i] = near[i] + load(x - 1)[i]
                if not (isinstance(x, int) and x == cx - 1):
                    near[i] = near[i] + load(x + 1)[i]
                if factor:
                    near[i] = near[i] * float(slots)
                scale = float(SHARE) if factor else 1.0
                near[i] = near[i] + jnp.where(top, left[factor][i] * scale, 0.0)
                near[i] = near[i] + jnp.where(bottom, right[factor][i] * scale, 0.0)
                if isinstance(x, int):
                    near[i] = near[i] + face_sum(BELOW if x == 0 else ABOVE, None)[factor][i] * scale
            sums.append(near)
        for i in range(2):
            c0 = c0 - rate[i] * sums[0][i]
            c1 = c1 + rate[i] * sums[1][i]
        return c0, c1

    c0, c1 = over_planes(cx, visit_sum, (c0, c1))
    back = -1.0 / TIME_STEP
    scales = (back, back, back, back, back * (2.0 * slots - 2.0 * COUPLING * slots * slots), 1.0 / TIME_STEP)
    lane = lax.broadcasted_iota(jnp.int32, (1, LANES), 1)
    row = jnp.zeros((1, LANES), jnp.float32)
    for i, (part, scale) in enumerate(zip((total, c0, c1, c2, c3, weight), scales)):
        value = jnp.sum(jnp.sum(part, axis=0, keepdims=True), axis=1, keepdims=True) * scale
        row = jnp.where(lane == i, value, row)
    sums_ref[...] = jnp.broadcast_to(row[None], (devices, 1, LANES))


def multipliers(got, slots):
    total = jnp.sum(got[...], axis=0)
    lane = lax.broadcasted_iota(jnp.int32, (1, LANES), 1)
    part = [jnp.sum(jnp.where(lane == i, total, 0.0), axis=1, keepdims=True) for i in range(6)]
    whole = slots * part[5]
    here = part[0] / whole
    later = (part[1] + here * (part[2] + here * (part[3] + here * part[4]))) / whole
    spread = lambda value: jnp.broadcast_to(value, (ROWS, LANES))
    return spread(here), spread(later)


def advance(cx, cy, slots, got, grown, grown_halo, rate_ref, energy, halos, now, squares_ref, store, done=None):
    cells = cx * cy
    marks = edges()
    here, later = multipliers(got, slots)
    for k in range(FACES):
        h0, h1 = split(rate_ref[cells + k * ROWS : cells + (k + 1) * ROWS, :])
        for q in range(k * SHARE, (k + 1) * SHARE):
            v0, v1 = split(grown_halo[q * ROWS : (q + 1) * ROWS, :])
            halos[q * ROWS : (q + 1) * ROWS, :LANES] = v0 - here * h0
            halos[q * ROWS : (q + 1) * ROWS, LANES:] = v1 - here * h1

    def settle(x, carry):
        base = pl.multiple_of(x * cy, ROWS)
        h = split(rate_ref[pl.ds(base, cy), :])
        off = [here * h[i] for i in range(2)]
        squares = [None, None]
        for q in range(slots):
            at = q * cells + x * cy
            v = take(grown, at, cy)
            for i in range(2):
                f = v[i] - off[i]
                put(now, at, i, f)
                squares[i] = f * f if squares[i] is None else squares[i] + f * f
        for i in range(2):
            squares_ref[pl.ds(base, cy), i * LANES : (i + 1) * LANES] = 2.0 * COUPLING * squares[i]
        return carry

    lax.fori_loop(0, cx, settle, 0)

    def visit(x, carry):
        squares = plane_of(squares_ref, 0, x, cy)
        rate = plane_of(rate_ref, 0, x, cy)
        for q in range(slots):
            load, halo = slot_access(now, halos, q, cells, cy)
            centre = load(x)
            near = neighbours(x, cx - 1, load, centre, halo, q // SHARE, marks)
            e = energy[q * ROWS : (q + 1) * ROWS, :]
            for i in range(2):
                force = force_of(centre[i], near[i], squares[i], e)
                store(q, x, i, centre[i] - rate[i] * (force + later))
        if done is not None:
            done(x)
        return carry

    over_planes(cx, visit, 0)


def middle_body(
    cx, cy, slots, got, grown, grown_halo, rate_ref, energy, fields, col_a, col_b, slab_a, slab_b,
    halos, now, squares_ref,
):
    cells = cx * cy

    def store(q, x, i, value):
        put(fields, q * cells + x * cy, i, value)

    advance(cx, cy, slots, got, grown, grown_halo, rate_ref, energy, halos, now, squares_ref, store)
    pack_faces(fields, cx, cy, slots, (slab_a, slab_b), "slab", False)
    pack_faces(fields, cx, cy, slots, (col_a, col_b), "col", True)


def last_body(
    cx, cy, slots, got, grown, grown_halo, rate_ref, energy, slots_ref, out, halos, now, squares_ref, result, sems
):
    def plane(x):
        at = x * cy if isinstance(x, int) else pl.multiple_of(x * cy, ROWS)
        rows = pl.ds(at, cy)
        return pltpu.make_async_copy(result.at[:, rows, :], out.at[:, rows, :], sems.at[x])

    def store(q, x, i, value):
        at = x * cy if isinstance(x, int) else pl.multiple_of(x * cy, ROWS)
        result[slots_ref[q], pl.ds(at, cy), i * LANES : (i + 1) * LANES] = value

    def done(x):
        plane(x).start()

    advance(cx, cy, slots, got, grown, grown_halo, rate_ref, energy, halos, now, squares_ref, store, done)
    for x in range(cx):
        plane(x).wait()


def exchange_cols(first, second):
    count = lax.axis_size("col")
    one = [(i, i ^ 1) for i in range(count)]
    two = [(i, (i - 1) % count if i % 2 == 0 else (i + 1) % count) for i in range(count)]
    return lax.ppermute(first, "col", one), lax.ppermute(second, "col", two)


def exchange_slabs(first, second):
    count, cols = lax.axis_size("slab"), lax.axis_size("col")
    one = [(i, i ^ 1) for i in range(count)]
    two = []
    for s in range(count):
        other = s - 1 if s % 2 == 0 else s + 1
        for c in range(cols):
            target = other * cols + c if 0 <= other < count else s * cols + (c ^ 1)
            two.append((s * cols + c, target))
    return lax.ppermute(second, ("slab", "col"), two), lax.ppermute(first, "slab", one)


def per_device(order_params, layer_mask, coarse_temp, coarse_rows, grain_ids, energy):
    slots, cx, cy, cz = order_params.shape
    slabs, cols = lax.axis_size("slab"), lax.axis_size("col")
    devices = slabs * cols
    cells = cx * cy
    capacity, _, coarse_z = coarse_temp.shape
    raw = order_params.reshape(slots * cells, cz)
    mask = layer_mask.reshape(cells, cz)
    wide = FACES * ROWS
    message = f32(2 * SHARE + 3, ROWS, cz)
    short = f32(2 * SHARE + 1, ROWS, cz)
    state = f32(2 * slots * cells, cz // 2)
    halo = f32(slots * ROWS, cz)

    hbm = lambda x: pltpu.with_memory_space_constraint(x, pltpu.HBM)
    raw, mask, slot_order, col_a, col_b = call(
        functools.partial(open_body, cx, cy, slots, slabs, cols),
        (state, f32(2 * cells, LANES), jax.ShapeDtypeStruct((slots,), jnp.int32), message, message),
        [HBM] * 4,
        (VMEM, VMEM, SMEM, VMEM, VMEM),
        [
            pltpu.SMEM(grain_ids.shape, jnp.int32),
            pltpu.VMEM(grain_ids.shape, jnp.int32),
            pltpu.VMEM(coarse_temp.shape, jnp.float32),
            pltpu.VMEM((2 * cells, LANES), jnp.int32),
            pltpu.SemaphoreType.DMA((7,)),
        ],
    )(hbm(grain_ids), hbm(raw), hbm(mask), hbm(coarse_temp))
    col_a, col_b = exchange_cols(col_a, col_b)
    fields, slot_energy = call(
        functools.partial(arrange_body, cells, slots),
        (state, f32(slots * ROWS, LANES)),
        [VMEM, SMEM, SMEM, SMEM],
        (VMEM, VMEM),
    )(raw, slot_order, grain_ids, energy)
    slab_a, slab_b, planes = call(
        functools.partial(slab_body, cx, cy, slots, slabs, cols),
        (message, message, f32(capacity * ROWS, LANES)),
        [VMEM, VMEM, VMEM, SMEM, VMEM, VMEM],
        (VMEM,) * 3,
    )(fields, mask, coarse_temp, coarse_rows, col_a, col_b)
    slab_b, slab_a = exchange_slabs(slab_a, slab_b)
    weights = jnp.asarray(plane_weights(cx, cy))
    height = jnp.asarray(height_weights(cz, coarse_z))
    rate = call(
        functools.partial(mobility_body, cx, cy, slabs, cols),
        f32(cells + wide, cz),
        [VMEM, SMEM] + [VMEM] * 7,
        VMEM,
        [pltpu.VMEM(((cx // 2 + 2) * ROWS, LANES), jnp.float32)],
    )(planes, coarse_rows, mask, weights, height, col_a, col_b, slab_a, slab_b)

    buffers = [pltpu.VMEM(halo.shape, jnp.float32), pltpu.VMEM(state.shape, jnp.float32)]
    buffers += [pltpu.VMEM((cells, cz), jnp.float32)]
    for pair in range(STEPS // 2):
        grown, grown_halo, sums = call(
            functools.partial(sums_body, cx, cy, slots, slabs, cols, devices),
            (state, halo, f32(devices, 1, LANES)),
            [VMEM] * 7,
            (VMEM,) * 3,
            [pltpu.VMEM(halo.shape, jnp.float32), pltpu.VMEM((cells, cz), jnp.float32)],
        )(fields, rate, slot_energy, col_a, col_b, slab_a, slab_b)
        got = lax.all_to_all(sums, ("slab", "col"), 0, 0)
        if pair < STEPS // 2 - 1:
            fields, col_a, col_b, slab_a, slab_b = call(
                functools.partial(middle_body, cx, cy, slots),
                (state, short, short, short, short),
                [VMEM] * 5,
                (VMEM,) * 5,
                buffers,
            )(got, grown, grown_halo, rate, slot_energy)
            slab_b, slab_a = exchange_slabs(slab_a, slab_b)
            col_a, col_b = exchange_cols(col_a, col_b)
        else:
            fields = call(
                functools.partial(last_body, cx, cy, slots),
                f32(slots, cells, cz),
                [VMEM] * 5 + [SMEM],
                HBM,
                buffers + [pltpu.VMEM((slots, cells, cz), jnp.float32), pltpu.SemaphoreType.DMA((cx,))],
            )(got, grown, grown_halo, rate, slot_energy, slot_order)
    return fields.reshape(order_params.shape)


def solution(mesh):
    in_specs = (
        P(None, "slab", "col", None),
        P("slab", "col", None),
        P("slab", "col", None),
        P(),
        P(),
        P(),
    )
    out_specs = P(None, "slab", "col", None)
    return jax.shard_map(
        per_device, mesh=mesh, in_specs=in_specs, out_specs=out_specs, check_vma=False
    )
```

```python
import functools

import jax
import jax.numpy as jnp
import numpy as np
from jax import lax
from jax.experimental import pallas as pl
from jax.experimental.pallas import tpu as pltpu
from jax.sharding import PartitionSpec as P

SHARE = 4
STEPS = 4
TIME_STEP = 0.05
COUPLING = 1.5
BELOW, ABOVE, LEFT, RIGHT = range(4)
FACES = 4
LANES = 128
ROWS = 8
HIGHEST = lax.Precision.HIGHEST

VMEM = pl.BlockSpec(memory_space=pltpu.VMEM)
SMEM = pl.BlockSpec(memory_space=pltpu.SMEM)
HBM = pl.BlockSpec(memory_space=pltpu.HBM)


def call(body, out_shape, in_specs, out_specs, scratch=(), flops=1 << 20, size=1 << 20):
    return pl.pallas_call(
        body,
        out_shape=out_shape,
        in_specs=in_specs,
        out_specs=out_specs,
        scratch_shapes=list(scratch),
        compiler_params=pltpu.CompilerParams(vmem_limit_bytes=20 << 20),
        cost_estimate=pl.CostEstimate(flops=flops, bytes_accessed=size, transcendentals=0),
    )


def f32(*shape):
    return jax.ShapeDtypeStruct(shape, jnp.float32)


def present(slabs, cols):
    s, c = lax.axis_index("slab"), lax.axis_index("col")
    return (s > 0, s < slabs - 1, c > 0, c < cols - 1)


def beside(slabs, cols):
    s, c = lax.axis_index("slab"), lax.axis_index("col")
    return (
        (jnp.maximum(s - 1, 0), c),
        (jnp.minimum(s + 1, slabs - 1), c),
        (s, jnp.maximum(c - 1, 0)),
        (s, jnp.minimum(c + 1, cols - 1)),
    )


def slot_places(slabs, cols, slots, ids_ref, ids_smem):
    s, c = lax.axis_index("slab"), lax.axis_index("col")
    sub = lax.broadcasted_iota(jnp.int32, (slots, LANES), 0)
    lane = lax.broadcasted_iota(jnp.int32, (slots, LANES), 1)
    own = jnp.zeros((slots, LANES), jnp.int32)
    for q in range(slots):
        own = jnp.where(sub == q, ids_smem[s, c, q], own)
    one, zero = jnp.float32(1.0), jnp.float32(0.0)
    have = present(slabs, cols)
    matches, ranks = [], []
    for k, (ns, nc) in enumerate(beside(slabs, cols)):
        row = ids_ref[ns, pl.ds(nc, 1), :]
        row = jnp.concatenate([row, jnp.full((1, LANES - slots), -1, jnp.int32)], axis=1)
        row = jnp.broadcast_to(jnp.where(have[k], row, -1), (slots, LANES))
        hit = jnp.where((own == row) & (row >= 0), one, zero)
        shared = jnp.max(hit, axis=0, keepdims=True)
        matches.append(jnp.sum(hit, axis=1, keepdims=True))
        ranks.append(jnp.sum(jnp.where(row < own, shared, zero), axis=1, keepdims=True))
    free = one - (matches[0] + matches[1] + matches[2] + matches[3])
    lanef = lane.astype(jnp.float32)
    free_row = jnp.sum(jnp.where(sub == lane, free, zero), axis=0, keepdims=True)
    free_rank = jnp.sum(jnp.where(lane < sub, free_row, zero), axis=1, keepdims=True)
    place = jnp.zeros((slots, LANES), jnp.float32)
    skipped = jnp.int32(0)
    for k in range(FACES):
        at = matches[k] * (ranks[k] + k * SHARE - lanef)
        place = jnp.where((matches[k] > 0.5) & (jnp.abs(at) < 0.5), one, place)
        local = free_rank - (skipped * SHARE).astype(jnp.float32)
        inside = (local > -0.5) & (local < SHARE - 0.5) & (free > 0.5)
        inside = inside & jnp.logical_not(have[k])
        place = jnp.where(inside & (jnp.abs(local + k * SHARE - lanef) < 0.5), one, place)
        skipped = skipped + jnp.where(have[k], 0, 1)
    return place


def take(ref, at, rows, stride=1):
    half = ref.shape[0] // 2
    if stride == 1:
        if not isinstance(at, int):
            at = pl.multiple_of(at, ROWS)
        return ref[pl.ds(at, rows), :], ref[pl.ds(at + half, rows), :]
    return ref[pl.ds(at, rows, stride=stride), :], ref[pl.ds(at + half, rows, stride=stride), :]


def put(ref, at, i, value):
    if not isinstance(at, int):
        at = pl.multiple_of(at, ROWS)
    ref[pl.ds(at + i * (ref.shape[0] // 2), value.shape[0]), :] = value


def spread(ref, row):
    half = ref.shape[0] // 2
    return tuple(jnp.broadcast_to(ref[pl.ds(row + i * half, 1), :], (ROWS, LANES)) for i in range(2))


class Kept:
    def __init__(self, ref, base, cx, cy, slots):
        self.ref, self.cy, self.cells = ref, cy, cx * cy
        self.base = base
        self.near_base = base + self.cells + FACES * ROWS
        self.energy_base = self.near_base + FACES * self.cells
        self.slots_base = self.energy_base + slots * ROWS

    @staticmethod
    def rows(cells, slots):
        return cells + FACES * ROWS + FACES * cells + slots * ROWS + ROWS

    def rate(self, x):
        return take(self.ref, self.base + x * self.cy, self.cy)

    def rate_beside(self, k):
        return take(self.ref, self.base + self.cells + k * ROWS, ROWS)

    def near(self, k, x):
        return take(self.ref, self.near_base + k * self.cells + x * self.cy, self.cy)

    def energy(self, q):
        return self.ref[self.energy_base + q * ROWS : self.energy_base + (q + 1) * ROWS, :]


def keep_on(out, out_base, kept, count):
    for i in range(2):
        put(out, out_base, i, take(kept.ref, kept.base, count)[i])


def fill(out, index, pair):
    out[index, :, :LANES], out[index, :, LANES:] = pair


def pair_faces(axis, low, high):
    even = lax.rem(lax.axis_index(axis), 2) == 0
    return even, (jnp.where(even, high, low), jnp.where(even, low, high))


def pack_faces(fields, cx, cy, slots, out_refs, axis, columns, slot_of=lambda place: place[0] * SHARE + place[1]):
    low, high = (LEFT, RIGHT) if columns else (BELOW, ABOVE)
    _, faces = pair_faces(axis, low, high)
    for out, face in zip(out_refs, faces):
        is_high = face == high
        for depth in range(2):
            if columns:
                first = jnp.where(is_high, cy - 1 - depth, depth)
                plane = lambda q: take(fields, q * (cx * cy) + first, cx, cy)
            else:
                first = jnp.where(is_high, cx - 1 - depth, depth) * cy
                plane = lambda q: take(fields, q * (cx * cy) + first, cy)
            for j in range(SHARE):
                fill(out, depth * SHARE + j, plane(slot_of((face, j))))
            if depth == 0:
                s0 = s1 = None
                for q in range(slots):
                    v0, v1 = plane(q)
                    s0 = v0 * v0 if s0 is None else s0 + v0 * v0
                    s1 = v1 * v1 if s1 is None else s1 + v1 * v1
                fill(out, 2 * SHARE, (s0, s1))


def open_body(
    cx, cy, slots, slabs, cols, ids_hbm, rows_hbm, fields_hbm, mask_hbm, coarse_hbm,
    raw, mask, slots_ref, bounds, planes, msg_a, msg_b, ids_smem, rows_smem, ids_ref, coarse_ref, mask_ref, sems,
):
    cells = cx * cy
    loads = [
        pltpu.make_async_copy(ids_hbm, ids_smem, sems.at[0]),
        pltpu.make_async_copy(ids_hbm, ids_ref, sems.at[1]),
        pltpu.make_async_copy(rows_hbm, rows_smem, sems.at[2]),
        pltpu.make_async_copy(coarse_hbm, coarse_ref, sems.at[3]),
    ]
    for i in range(2):
        half = pl.ds(i * LANES, LANES)
        loads.append(
            pltpu.make_async_copy(mask_hbm.at[:, half], mask_ref.at[pl.ds(i * cells, cells), :], sems.at[4 + i])
        )
        rows = slots * cells
        loads.append(
            pltpu.make_async_copy(fields_hbm.at[:, half], raw.at[pl.ds(i * rows, rows), :], sems.at[6 + i])
        )
    for load in loads:
        load.start()
    for load in loads[:4]:
        load.wait()
    place = slot_places(slabs, cols, slots, ids_ref, ids_smem)
    sub = lax.broadcasted_iota(jnp.int32, (slots, LANES), 0).astype(jnp.float32)
    slot_row = jnp.sum(place * sub, axis=0, keepdims=True)
    slots_ref[...] = jnp.broadcast_to(slot_row, (ROWS, LANES))
    lane = lax.broadcasted_iota(jnp.int32, (1, LANES), 1)
    taken = lambda q: jnp.sum(jnp.where(lane == q, slot_row, 0.0)).astype(jnp.int32)
    left = [taken(LEFT * SHARE + j) for j in range(SHARE)]
    right = [taken(RIGHT * SHARE + j) for j in range(SHARE)]

    s = lax.axis_index("slab")
    start = jnp.int32(0)
    for t in range(slabs):
        start = start + jnp.where(t < s, rows_smem[t], 0)
    live = rows_smem[s]
    bounds[0:ROWS, :] = jnp.full((ROWS, LANES), start, jnp.int32)
    bounds[ROWS : 2 * ROWS, :] = jnp.full((ROWS, LANES), start + live, jnp.int32)
    capacity, coarse_y, _ = coarse_ref.shape
    chosen = [
        jnp.clip(plane - start, 0, capacity - 1) for plane in near_planes(cx, slabs)
    ] + [jnp.int32(0), jnp.int32(1), live - 2, live - 1]
    _, faces = pair_faces("col", LEFT, RIGHT)
    for out in (msg_a, msg_b):
        out[2 * SHARE + 2] = jnp.zeros((ROWS, out.shape[2]), jnp.float32)
    planes[...] = jnp.zeros(planes.shape, jnp.float32)
    for i, p in enumerate(chosen):
        planes[i * ROWS + 1 : i * ROWS + 1 + coarse_y, :] = coarse_ref[p]
        for out, face in zip((msg_a, msg_b), faces):
            row = jnp.where(face == RIGHT, coarse_y - 1, 0)
            spot = slice(i // ROWS * LANES, (i // ROWS + 1) * LANES)
            out[2 * SHARE + 2, i % ROWS : i % ROWS + 1, spot] = coarse_ref[p, pl.ds(row, 1), :]

    for load in loads[4:]:
        load.wait()
    mask[...] = mask_ref[...].astype(jnp.float32)

    def slot_of(place):
        face, j = place
        return jnp.where(face == RIGHT, right[j], left[j])

    pack_faces(raw, cx, cy, slots, (msg_a, msg_b), "col", True, slot_of)
    for out, face in zip((msg_a, msg_b), faces):
        first = jnp.where(face == RIGHT, cy - 1, 0)
        fill(out, 2 * SHARE + 1, take(mask, first, cx, cy))


def near_planes(cx, slabs):
    s = lax.axis_index("slab")
    half = cx // 2
    return [jnp.clip(s * half - 1 + i, 0, slabs * half - 1) for i in range(half + 2)]


def arrange_body(
    cx, cy, slots, raw, mask, slots_ref, ids_ref, energy_ref, fields, energy_out, pre_a, pre_b
):
    cells = cx * cy
    s, c = lax.axis_index("slab"), lax.axis_index("col")
    for q in range(slots):
        slot = slots_ref[0, q].astype(jnp.int32)
        for i, part in enumerate(take(raw, slot * cells, cells)):
            put(fields, q * cells, i, part)
        value = jnp.full((ROWS, LANES), energy_ref[ids_ref[s, c, slot]], jnp.float32)
        energy_out[q * ROWS : (q + 1) * ROWS, :] = value
    pack_faces(fields, cx, cy, slots, (pre_a, pre_b), "slab", False)
    _, faces = pair_faces("slab", BELOW, ABOVE)
    for out, face in zip((pre_a, pre_b), faces):
        first = jnp.where(face == ABOVE, cx - 1, 0) * cy
        fill(out, 2 * SHARE + 1, take(mask, first, cy))


def slab_body(cx, slabs, cols, coarse_y, own, pre_a, pre_b, got_a, got_b, msg_a, msg_b, planes):
    have = present(slabs, cols)
    even, _ = pair_faces("col", LEFT, RIGHT)
    thermal = 2 * SHARE + 2
    from_a, from_b = got_a[thermal], got_b[thermal]
    lower = jnp.where(even, from_b, from_a)
    upper = jnp.where(even, from_a, from_b)
    sub = lax.broadcasted_iota(jnp.int32, (ROWS, LANES), 0)
    last = coarse_y + 1
    widened = []
    for i in range(cx // 2 + 6):
        plane = own[i * ROWS : (i + 1) * ROWS, :]
        spot = slice(i // ROWS * LANES, (i // ROWS + 1) * LANES)
        below = jnp.where(have[LEFT], lower[i % ROWS : i % ROWS + 1, spot], plane[1:2, :])
        above = jnp.where(have[RIGHT], upper[i % ROWS : i % ROWS + 1, spot], plane[coarse_y : coarse_y + 1, :])
        plane = jnp.where(sub == 0, below, jnp.where(sub == last, above, plane))
        widened.append(plane)
        if i < cx // 2 + 2:
            planes[i * ROWS : (i + 1) * ROWS, :] = plane
    first = cx // 2 + 2
    _, faces = pair_faces("slab", BELOW, ABOVE)
    for out, pre, face in zip((msg_a, msg_b), (pre_a, pre_b), faces):
        out[:thermal] = pre[...]
        for i in range(2):
            plane = jnp.where(face == ABOVE, widened[first + 2 + i], widened[first + i])
            out[thermal, :, i * LANES : (i + 1) * LANES] = plane


def axis_weights(cells):
    fine = np.arange(-1, cells + 1)
    lower = (2 * fine - 1) // 4
    weight = (2 * fine - 1 - 4 * lower) / 4.0
    out = np.zeros((cells + 2, cells // 2 + 2), np.float32)
    out[np.arange(cells + 2), lower + 1] += 1.0 - weight
    out[np.arange(cells + 2), lower + 2] += weight
    return out


def plane_weights(cx, cy):
    along, across = axis_weights(cx), axis_weights(cy)
    inner = [(x + 1, y + 1) for x in range(cx) for y in range(cy)]
    inner += [(0, y + 1) for y in range(cy)] + [(cx + 1, y + 1) for y in range(cy)]
    inner += [(x + 1, 0) for x in range(cx)] + [(x + 1, cy + 1) for x in range(cx)]
    out = np.zeros((len(inner), cx // 2 + 2, ROWS), np.float32)
    for row, (x, y) in enumerate(inner):
        out[row, :, : cy // 2 + 2] = along[x][:, None] * across[y][None, :]
    return out.reshape(len(inner), -1)


def height_weights(cells, coarse):
    fine = np.arange(cells)
    lower = (2 * fine - 1) // 4
    weight = (2 * fine - 1 - 4 * lower) / 4.0
    out = np.zeros((coarse, cells), np.float32)
    np.add.at(out, (np.clip(lower, 0, coarse - 1), fine), 1.0 - weight)
    np.add.at(out, (np.clip(lower + 1, 0, coarse - 1), fine), weight)
    return out


def mobility_body(
    cx, cy, slots, slabs, cols, planes, bounds, mask_ref, weights, height, energy, slots_ref,
    col_a, col_b, slab_a, slab_b, keep, near,
):
    start, end = bounds[0:ROWS, :], bounds[ROWS : 2 * ROWS, :]
    even_s, _ = pair_faces("slab", BELOW, ABOVE)
    even_c, _ = pair_faces("col", LEFT, RIGHT)
    thermal, mask = 2 * SHARE + 2, 2 * SHARE + 1
    below = jnp.where(even_s, slab_b[thermal], slab_a[thermal])
    above = jnp.where(even_s, slab_a[thermal], slab_b[thermal])
    for i, p in enumerate(near_planes(cx, slabs)):
        p = jnp.full((ROWS, LANES), p, jnp.int32)
        own = planes[i * ROWS : (i + 1) * ROWS, :]
        lower = jnp.where(p == start - 2, below[:, :LANES], below[:, LANES:])
        upper = jnp.where(p == end, above[:, :LANES], above[:, LANES:])
        near[i * ROWS : (i + 1) * ROWS, :] = jnp.where(p < start, lower, jnp.where(p < end, own, upper))
    flat = jnp.dot(weights[...], near[...], precision=HIGHEST, preferred_element_type=jnp.float32)
    profile = jnp.dot(flat, height[...], precision=HIGHEST, preferred_element_type=jnp.float32)
    mobility = jnp.exp(2.0 * (profile - 1.0)) * TIME_STEP
    cells = cx * cy
    kept = Kept(keep, 0, cx, cy, slots)
    for i, part in enumerate(take(mask_ref, 0, cells)):
        put(keep, 0, i, part * mobility[:cells, i * LANES : (i + 1) * LANES])
    have = present(slabs, cols)
    masks = (
        jnp.where(even_s, slab_b[mask], slab_a[mask]),
        jnp.where(even_s, slab_a[mask], slab_b[mask]),
        jnp.where(even_c, col_b[mask], col_a[mask]),
        jnp.where(even_c, col_a[mask], col_b[mask]),
    )
    for k in range(FACES):
        at = cells + k * ROWS
        for i, part in enumerate(split(jnp.where(have[k], masks[k] * mobility[at : at + ROWS], 0.0))):
            put(keep, at, i, part)
    for i in range(2):
        put(keep, kept.energy_base, i, energy[...])
        put(keep, kept.slots_base, i, slots_ref[...])
    marks = edges()
    top, bottom = marks[2:]
    for x in range(cx):
        sums = neighbours(x, cx - 1, kept.rate, kept.rate(x), None, None, marks)
        extra = [None] * FACES
        if x == 0:
            extra[BELOW] = kept.rate_beside(BELOW)
        if x == cx - 1:
            extra[ABOVE] = kept.rate_beside(ABOVE)
        extra[LEFT] = [jnp.where(top, v, 0.0) for v in spread(keep, cells + LEFT * ROWS + x)]
        extra[RIGHT] = [jnp.where(bottom, v, 0.0) for v in spread(keep, cells + RIGHT * ROWS + x)]
        for k in range(FACES):
            for i in range(2):
                value = sums[i] if extra[k] is None else sums[i] + extra[k][i]
                put(keep, kept.near_base + k * cells + x * cy, i, value)


def split(value):
    return value[:, :LANES], value[:, LANES:]


def along_height(v0, v1, first, last):
    r0, r1 = pltpu.roll(v0, 1, 1), pltpu.roll(v1, 1, 1)
    q0, q1 = pltpu.roll(v0, LANES - 1, 1), pltpu.roll(v1, LANES - 1, 1)
    return (
        jnp.where(first, 0.0, r0) + jnp.where(last, q1, q0),
        jnp.where(first, r0, r1) + jnp.where(last, 0.0, q1),
    )


def along_rows(v, top, bottom, lower, upper):
    down = jnp.where(top, 0.0 if lower is None else lower, pltpu.roll(v, 1, 0))
    up = jnp.where(bottom, 0.0 if upper is None else upper, pltpu.roll(v, ROWS - 1, 0))
    return down + up


def edges():
    lane = lax.broadcasted_iota(jnp.int32, (ROWS, LANES), 1)
    row = lax.broadcasted_iota(jnp.int32, (ROWS, LANES), 0)
    return lane == 0, lane == LANES - 1, row == 0, row == ROWS - 1


def neighbours(x, last_x, load, centre, halo, kind, marks):
    first, last, top, bottom = marks
    v0, v1 = centre
    n0, n1 = along_height(v0, v1, first, last)
    low = high = (None, None)
    if kind == LEFT:
        low = halo(x)
    if kind == RIGHT:
        high = halo(x)
    n0 = n0 + along_rows(v0, top, bottom, low[0], high[0])
    n1 = n1 + along_rows(v1, top, bottom, low[1], high[1])
    sides = []
    if not (isinstance(x, int) and x == 0):
        sides.append(load(x - 1))
    elif kind == BELOW:
        sides.append(halo(None))
    if not (isinstance(x, int) and x == last_x):
        sides.append(load(x + 1))
    elif kind == ABOVE:
        sides.append(halo(None))
    for a, b in sides:
        n0, n1 = n0 + a, n1 + b
    return n0, n1


def over_planes(cx, visit, carry):
    carry = visit(0, carry)
    carry = lax.fori_loop(1, cx - 1, visit, carry)
    return visit(cx - 1, carry)


def slot_access(fields, halos, base, q, cells, cy):
    def load(x):
        return take(fields, q * cells + x * cy, cy)

    def halo(x):
        if x is None:
            return take(halos, base + q * ROWS, ROWS)
        return spread(halos, base + q * ROWS + x)

    return load, halo


def force_of(v, n, squares3, energy):
    return v * (squares3 + ((5.0 - energy) + v * (energy - 2.0 * v))) - n


def triple_squares(fields, x, slots, cells, cy):
    total = None
    for q in range(slots):
        v0, v1 = take(fields, q * cells + x * cy, cy)
        total = (v0 * v0, v1 * v1) if total is None else (total[0] + v0 * v0, total[1] + v1 * v1)
    return 2.0 * COUPLING * total[0], 2.0 * COUPLING * total[1]


def inner_body(cx, cy, slots, base, *refs):
    fields, force_out = refs[0], refs[-1]
    cells = cx * cy
    marks = edges()
    if base is None:
        energy = lambda q: refs[1][q * ROWS : (q + 1) * ROWS, :]
    else:
        energy = Kept(fields, base, cx, cy, slots).energy

    def visit(x, carry):
        squares = triple_squares(fields, x, slots, cells, cy)
        for q in range(slots):
            load, _ = slot_access(fields, None, None, q, cells, cy)
            centre = load(x)
            near = neighbours(x, cx - 1, load, centre, None, None, marks)
            e = energy(q)
            for i in range(2):
                put(force_out, q * cells + x * cy, i, force_of(centre[i], near[i], squares[i], e))
        return carry

    over_planes(cx, visit, 0)


def arrivals(col_a, col_b, slab_a, slab_b):
    even_s, _ = pair_faces("slab", BELOW, ABOVE)
    even_c, _ = pair_faces("col", LEFT, RIGHT)
    pairs = ((slab_b, slab_a, even_s), (slab_a, slab_b, even_s), (col_b, col_a, even_c), (col_a, col_b, even_c))
    return [functools.partial(lambda u, v, even, i: jnp.where(even, u[i], v[i]), *pair) for pair in pairs]


class Grown:
    def __init__(self, cx, cy, slots):
        self.cells = cx * cy
        self.sum = slots * self.cells
        self.squares = self.sum + self.cells
        self.halos = self.squares + self.cells
        self.kept = self.halos + slots * ROWS
        self.count = Kept.rows(self.cells, slots)
        self.rows = self.kept + self.count


def sums_body(
    cx, cy, slots, slabs, cols, devices, base, fields, keep, force_in, col_a, col_b, slab_a, slab_b,
    grown, sums_ref, halos,
):
    cells = cx * cy
    marks = edges()
    first, last, top, bottom = marks
    have = present(slabs, cols)
    kept = Kept(keep, base, cx, cy, slots)
    layout = Grown(cx, cy, slots)
    keep_on(grown, layout.kept, kept, layout.count)
    for k, pick in enumerate(arrivals(col_a, col_b, slab_a, slab_b)):
        s0, s1 = split(2.0 * COUPLING * pick(2 * SHARE))
        h0, h1 = kept.rate_beside(k)
        for j in range(SHARE):
            q = k * SHARE + j
            v0, v1 = split(jnp.where(have[k], pick(j), 0.0))
            put(halos, q * ROWS, 0, v0)
            put(halos, q * ROWS, 1, v1)
            o0, o1 = split(pick(SHARE + j))
            if k == BELOW:
                i0, i1 = take(fields, q * cells, cy)
            elif k == ABOVE:
                i0, i1 = take(fields, (q + 1) * cells - cy, cy)
            elif k == LEFT:
                i0, i1 = take(fields, q * cells, cx, cy)
            else:
                i0, i1 = take(fields, q * cells + cy - 1, cx, cy)
            n0, n1 = along_height(v0, v1, first, last)
            n0 = n0 + along_rows(v0, top, bottom, None, None) + o0 + i0
            n1 = n1 + along_rows(v1, top, bottom, None, None) + o1 + i1
            e = kept.energy(q)
            put(grown, layout.halos + q * ROWS, 0, v0 - h0 * force_of(v0, n0, s0, e))
            put(grown, layout.halos + q * ROWS, 1, v1 - h1 * force_of(v1, n1, s1, e))

    energy_sum = None
    for q in range(slots):
        energy_sum = kept.energy(q) if energy_sum is None else energy_sum + kept.energy(q)
    zero = jnp.zeros((ROWS, LANES), jnp.float32)

    def visit(x, carry):
        total, c0, c1, c2, c3, weight = carry
        rate = kept.rate(x)
        forces, powers = [zero, zero], [zero, zero]
        a2, b1 = [zero, zero], [zero, zero]
        a1 = [[zero, zero] for _ in range(FACES)]
        for q in range(slots):
            k = q // SHARE
            centre = take(fields, q * cells + x * cy, cy)
            inner = take(force_in, q * cells + x * cy, cy)
            e = kept.energy(q)
            cross = (None, None)
            if k in (LEFT, RIGHT):
                row = spread(halos, q * ROWS + x)
                cross = [jnp.where(top if k == LEFT else bottom, row[i], 0.0) for i in range(2)]
            elif isinstance(x, int) and (k, x) in ((BELOW, 0), (ABOVE, cx - 1)):
                cross = take(halos, q * ROWS, ROWS)
            for i in range(2):
                force = inner[i] if cross[i] is None else inner[i] - cross[i]
                g = centre[i] - rate[i] * force
                put(grown, q * cells + x * cy, i, g)
                weighted, square = e * g, g * g
                forces[i] = forces[i] + force
                powers[i] = powers[i] + g * (weighted - (square + square))
                a1[k][i] = a1[k][i] + g
                a2[i] = a2[i] + square
                b1[i] = b1[i] + weighted
        beside = [kept.near(k, x) for k in range(FACES)]
        for i in range(2):
            h = rate[i]
            whole = (a1[0][i] + a1[1][i]) + (a1[2][i] + a1[3][i])
            near = [beside[k][i] for k in range(FACES)]
            put(grown, layout.sum + x * cy, i, whole)
            put(grown, layout.squares + x * cy, i, a2[i])
            total = total + h * forces[i]
            c0 = c0 + h * (powers[i] + 5.0 * whole - b1[i] + 2.0 * COUPLING * whole * a2[i])
            for k in range(FACES):
                c0 = c0 - a1[k][i] * near[k]
            linear = (
                energy_sum
                - 5.0 * slots
                - 2.0 * b1[i]
                + (6.0 - 2.0 * COUPLING * slots) * a2[i]
                - 4.0 * COUPLING * (whole * whole)
            )
            c1 = c1 + h * (h * linear + float(SHARE) * ((near[0] + near[1]) + (near[2] + near[3])))
            c2 = c2 + h * h * h * (energy_sum + (6.0 * COUPLING * slots - 6.0) * whole)
            c3 = c3 + (h * h) * (h * h)
            weight = weight + h
        return total, c0, c1, c2, c3, weight

    parts = over_planes(cx, visit, (zero,) * 6)
    back = -1.0 / TIME_STEP
    scales = (back, back, back, back, back * (2.0 * slots - 2.0 * COUPLING * slots * slots), 1.0 / TIME_STEP)
    lane = lax.broadcasted_iota(jnp.int32, (1, LANES), 1)
    row = jnp.zeros((1, LANES), jnp.float32)
    for i, (part, scale) in enumerate(zip(parts, scales)):
        value = jnp.sum(jnp.sum(part, axis=0, keepdims=True), axis=1, keepdims=True) * scale
        row = jnp.where(lane == i, value, row)
    sums_ref[...] = jnp.broadcast_to(row[None], (devices, 1, LANES))


def near_body(cx, cy, slots, grown, near_out):
    cells = cx * cy
    marks = edges()
    halos = Grown(cx, cy, slots).halos

    def visit(x, carry):
        for q in range(slots):
            load, halo = slot_access(grown, grown, halos, q, cells, cy)
            near = neighbours(x, cx - 1, load, load(x), halo, q // SHARE, marks)
            for i in range(2):
                put(near_out, q * cells + x * cy, i, near[i])
        return carry

    over_planes(cx, visit, 0)


def multipliers(got, slots):
    total = jnp.sum(got[...], axis=0)
    lane = lax.broadcasted_iota(jnp.int32, (1, LANES), 1)
    part = [jnp.sum(jnp.where(lane == i, total, 0.0), axis=1, keepdims=True) for i in range(6)]
    whole = slots * part[5]
    here = part[0] / whole
    later = (part[1] + here * (part[2] + here * (part[3] + here * part[4]))) / whole
    return jnp.broadcast_to(here, (ROWS, LANES)), jnp.broadcast_to(later, (ROWS, LANES))


def settle(cx, cy, slots, got, grown, near_in, store, done=None):
    cells = cx * cy
    here, later = multipliers(got, slots)
    layout = Grown(cx, cy, slots)
    kept = Kept(grown, layout.kept, cx, cy, slots)
    for k in range(FACES):

        def visit(x, carry):
            rate = kept.rate(x)
            near = kept.near(k, x)
            a1 = take(grown, layout.sum + x * cy, cy)
            a2 = take(grown, layout.squares + x * cy, cy)
            off = [here * rate[i] for i in range(2)]
            base = [
                5.0 + 2.0 * COUPLING * (a2[i] - off[i] * (2.0 * a1[i] - float(slots) * off[i])) for i in range(2)
            ]
            extra = [here * near[i] + later for i in range(2)]
            for q in range(k * SHARE, (k + 1) * SHARE):
                e = kept.energy(q)
                g = take(grown, q * cells + x * cy, cy)
                n = take(near_in, q * cells + x * cy, cy)
                for i in range(2):
                    f = g[i] - off[i]
                    force = f * ((base[i] - e) + f * (e - (f + f))) - (n[i] - extra[i])
                    store(q, x, i, f - rate[i] * force)
            return carry

        lax.fori_loop(0, cx, visit, 0)
        if done is not None:
            done(k)


def middle_body(cx, cy, slots, got, grown, near_in, fields, col_a, col_b, slab_a, slab_b):
    def store(q, x, i, value):
        put(fields, q * cx * cy + x * cy, i, value)

    settle(cx, cy, slots, got, grown, near_in, store)
    pack_faces(fields, cx, cy, slots, (slab_a, slab_b), "slab", False)
    pack_faces(fields, cx, cy, slots, (col_a, col_b), "col", True)
    layout = Grown(cx, cy, slots)
    keep_on(fields, slots * cx * cy, Kept(grown, layout.kept, cx, cy, slots), layout.count)


def last_body(cx, cy, slots, got, grown, near_in, out, result, order, sems, order_sem):
    kept = Kept(grown, Grown(cx, cy, slots).kept, cx, cy, slots)
    fetch = pltpu.make_async_copy(grown.at[pl.ds(kept.slots_base, ROWS), :], order, order_sem)
    fetch.start()

    def store(q, x, i, value):
        at = x * cy if isinstance(x, int) else pl.multiple_of(x * cy, ROWS)
        result[q, pl.ds(at, cy), i * LANES : (i + 1) * LANES] = value

    def send(q):
        return pltpu.make_async_copy(result.at[q], out.at[order[0, q].astype(jnp.int32)], sems.at[q])

    def done(k):
        if k == 0:
            fetch.wait()
        for q in range(k * SHARE, (k + 1) * SHARE):
            send(q).start()

    settle(cx, cy, slots, got, grown, near_in, store, done)
    for q in range(slots):
        send(q).wait()


def exchange_cols(first, second):
    count = lax.axis_size("col")
    one = [(i, i ^ 1) for i in range(count)]
    two = [(i, (i - 1) % count if i % 2 == 0 else (i + 1) % count) for i in range(count)]
    return lax.ppermute(first, "col", one), lax.ppermute(second, "col", two)


def exchange_slabs(first, second):
    count, cols = lax.axis_size("slab"), lax.axis_size("col")
    one = [(i, i ^ 1) for i in range(count)]
    two = []
    for s in range(count):
        other = s - 1 if s % 2 == 0 else s + 1
        for c in range(cols):
            target = other * cols + c if 0 <= other < count else s * cols + (c ^ 1)
            two.append((s * cols + c, target))
    return lax.ppermute(second, ("slab", "col"), two), lax.ppermute(first, "slab", one)


def per_device(order_params, layer_mask, coarse_temp, coarse_rows, grain_ids, energy):
    slots, cx, cy, cz = order_params.shape
    slabs, cols = lax.axis_size("slab"), lax.axis_size("col")
    devices = slabs * cols
    cells = cx * cy
    capacity, _, coarse_z = coarse_temp.shape
    raw = order_params.reshape(slots * cells, cz)
    mask = layer_mask.reshape(cells, cz)
    message = f32(2 * SHARE + 3, ROWS, cz)
    short = f32(2 * SHARE + 1, ROWS, cz)
    state = f32(2 * slots * cells, cz // 2)

    hbm = lambda x: pltpu.with_memory_space_constraint(x, pltpu.HBM)
    near = cx // 2 + 2
    raw, mask, slot_order, bounds, planes, col_a, col_b = call(
        functools.partial(open_body, cx, cy, slots, slabs, cols),
        (
            state,
            f32(2 * cells, LANES),
            f32(ROWS, LANES),
            jax.ShapeDtypeStruct((2 * ROWS, LANES), jnp.int32),
            f32((near + 4) * ROWS, LANES),
            message,
            message,
        ),
        [HBM] * 5,
        (VMEM,) * 7,
        [
            pltpu.SMEM(grain_ids.shape, jnp.int32),
            pltpu.SMEM(coarse_rows.shape, jnp.int32),
            pltpu.VMEM(grain_ids.shape, jnp.int32),
            pltpu.VMEM(coarse_temp.shape, jnp.float32),
            pltpu.VMEM((2 * cells, LANES), jnp.int32),
            pltpu.SemaphoreType.DMA((8,)),
        ],
    )(hbm(grain_ids), hbm(coarse_rows), hbm(raw), hbm(mask), hbm(coarse_temp))
    col_a, col_b = exchange_cols(col_a, col_b)
    packed = f32(2 * SHARE + 2, ROWS, cz)
    fields, slot_energy, pre_a, pre_b = call(
        functools.partial(arrange_body, cx, cy, slots),
        (state, f32(slots * ROWS, LANES), packed, packed),
        [VMEM, VMEM, SMEM, SMEM, SMEM],
        (VMEM,) * 4,
    )(raw, mask, slot_order, grain_ids, energy)
    slab_a, slab_b, planes = call(
        functools.partial(slab_body, cx, slabs, cols, coarse_temp.shape[1]),
        (message, message, f32(near * ROWS, LANES)),
        [VMEM] * 5,
        (VMEM,) * 3,
    )(planes, pre_a, pre_b, col_a, col_b)
    slab_b, slab_a = exchange_slabs(slab_a, slab_b)
    weights = jnp.asarray(plane_weights(cx, cy))
    height = jnp.asarray(height_weights(cz, coarse_z))
    count = Kept.rows(cells, slots)
    keep = call(
        functools.partial(mobility_body, cx, cy, slots, slabs, cols),
        f32(2 * count, LANES),
        [VMEM] * 11,
        VMEM,
        [pltpu.VMEM((near * ROWS, LANES), jnp.float32)],
    )(planes, bounds, mask, weights, height, slot_energy, slot_order, col_a, col_b, slab_a, slab_b)

    for pair in range(STEPS // 2):
        base = None if pair == 0 else slots * cells
        inputs = (fields, slot_energy) if pair == 0 else (fields,)
        force = call(
            functools.partial(inner_body, cx, cy, slots, base),
            state,
            [VMEM] * len(inputs),
            VMEM,
            flops=1 << 23,
            size=1 << 22,
        )(*inputs)
        grown, sums = call(
            functools.partial(sums_body, cx, cy, slots, slabs, cols, devices, base or 0),
            (f32(2 * Grown(cx, cy, slots).rows, LANES), f32(devices, 1, LANES)),
            [VMEM] * 7,
            (VMEM,) * 2,
            [pltpu.VMEM((2 * slots * ROWS, LANES), jnp.float32)],
        )(fields, keep if pair == 0 else fields, force, col_a, col_b, slab_a, slab_b)
        got = lax.all_to_all(sums, ("slab", "col"), 0, 0)
        grown_near = call(
            functools.partial(near_body, cx, cy, slots),
            state,
            [VMEM],
            VMEM,
            flops=1 << 23,
            size=1 << 22,
        )(grown)
        if pair < STEPS // 2 - 1:
            fields, col_a, col_b, slab_a, slab_b = call(
                functools.partial(middle_body, cx, cy, slots),
                (f32(2 * (slots * cells + count), LANES), short, short, short, short),
                [VMEM] * 3,
                (VMEM,) * 5,
            )(got, grown, grown_near)
            slab_b, slab_a = exchange_slabs(slab_a, slab_b)
            col_a, col_b = exchange_cols(col_a, col_b)
        else:
            fields = call(
                functools.partial(last_body, cx, cy, slots),
                f32(slots, cells, cz),
                [VMEM] * 3,
                HBM,
                [
                    pltpu.VMEM((slots, cells, cz), jnp.float32),
                    pltpu.SMEM((ROWS, LANES), jnp.float32),
                    pltpu.SemaphoreType.DMA((slots,)),
                    pltpu.SemaphoreType.DMA(()),
                ],
            )(got, grown, grown_near)
    return fields.reshape(order_params.shape)


def solution(mesh):
    in_specs = (
        P(None, "slab", "col", None),
        P("slab", "col", None),
        P("slab", "col", None),
        P(),
        P(),
        P(),
    )
    out_specs = P(None, "slab", "col", None)
    return jax.shard_map(
        per_device, mesh=mesh, in_specs=in_specs, out_specs=out_specs, check_vma=False
    )
```

```python
import functools

import jax
import jax.numpy as jnp
import numpy as np
from jax import lax
from jax.experimental import pallas as pl
from jax.experimental.pallas import tpu as pltpu
from jax.sharding import PartitionSpec as P

SHARE = 4
STEPS = 4
TIME_STEP = 0.05
COUPLING = 1.5
BELOW, ABOVE, LEFT, RIGHT = range(4)
FACES = 4
LANES = 128
ROWS = 8
HIGHEST = lax.Precision.HIGHEST

VMEM = pl.BlockSpec(memory_space=pltpu.VMEM)
SMEM = pl.BlockSpec(memory_space=pltpu.SMEM)
HBM = pl.BlockSpec(memory_space=pltpu.HBM)


def call(body, out_shape, in_specs, out_specs, scratch=(), flops=1 << 20, size=1 << 20):
    return pl.pallas_call(
        body,
        out_shape=out_shape,
        in_specs=in_specs,
        out_specs=out_specs,
        scratch_shapes=list(scratch),
        compiler_params=pltpu.CompilerParams(vmem_limit_bytes=20 << 20),
        cost_estimate=pl.CostEstimate(flops=flops, bytes_accessed=size, transcendentals=0),
    )


def f32(*shape):
    return jax.ShapeDtypeStruct(shape, jnp.float32)


def present(slabs, cols):
    s, c = lax.axis_index("slab"), lax.axis_index("col")
    return (s > 0, s < slabs - 1, c > 0, c < cols - 1)


def beside(slabs, cols):
    s, c = lax.axis_index("slab"), lax.axis_index("col")
    return (
        (jnp.maximum(s - 1, 0), c),
        (jnp.minimum(s + 1, slabs - 1), c),
        (s, jnp.maximum(c - 1, 0)),
        (s, jnp.minimum(c + 1, cols - 1)),
    )


def slot_places(slabs, cols, slots, ids_ref, ids_smem):
    s, c = lax.axis_index("slab"), lax.axis_index("col")
    sub = lax.broadcasted_iota(jnp.int32, (slots, LANES), 0)
    lane = lax.broadcasted_iota(jnp.int32, (slots, LANES), 1)
    own = jnp.zeros((slots, LANES), jnp.int32)
    for q in range(slots):
        own = jnp.where(sub == q, ids_smem[s, c, q], own)
    one, zero = jnp.float32(1.0), jnp.float32(0.0)
    have = present(slabs, cols)
    matches, ranks = [], []
    for k, (ns, nc) in enumerate(beside(slabs, cols)):
        row = ids_ref[ns, pl.ds(nc, 1), :]
        row = jnp.concatenate([row, jnp.full((1, LANES - slots), -1, jnp.int32)], axis=1)
        row = jnp.broadcast_to(jnp.where(have[k], row, -1), (slots, LANES))
        hit = jnp.where((own == row) & (row >= 0), one, zero)
        shared = jnp.max(hit, axis=0, keepdims=True)
        matches.append(jnp.sum(hit, axis=1, keepdims=True))
        ranks.append(jnp.sum(jnp.where(row < own, shared, zero), axis=1, keepdims=True))
    free = one - (matches[0] + matches[1] + matches[2] + matches[3])
    lanef = lane.astype(jnp.float32)
    free_row = jnp.sum(jnp.where(sub == lane, free, zero), axis=0, keepdims=True)
    free_rank = jnp.sum(jnp.where(lane < sub, free_row, zero), axis=1, keepdims=True)
    place = jnp.zeros((slots, LANES), jnp.float32)
    skipped = jnp.int32(0)
    for k in range(FACES):
        at = matches[k] * (ranks[k] + k * SHARE - lanef)
        place = jnp.where((matches[k] > 0.5) & (jnp.abs(at) < 0.5), one, place)
        local = free_rank - (skipped * SHARE).astype(jnp.float32)
        inside = (local > -0.5) & (local < SHARE - 0.5) & (free > 0.5)
        inside = inside & jnp.logical_not(have[k])
        place = jnp.where(inside & (jnp.abs(local + k * SHARE - lanef) < 0.5), one, place)
        skipped = skipped + jnp.where(have[k], 0, 1)
    return place


def take(ref, at, rows, stride=1):
    half = ref.shape[0] // 2
    if stride == 1:
        if not isinstance(at, int):
            at = pl.multiple_of(at, ROWS)
        return ref[pl.ds(at, rows), :], ref[pl.ds(at + half, rows), :]
    return ref[pl.ds(at, rows, stride=stride), :], ref[pl.ds(at + half, rows, stride=stride), :]


def put(ref, at, i, value):
    if not isinstance(at, int):
        at = pl.multiple_of(at, ROWS)
    ref[pl.ds(at + i * (ref.shape[0] // 2), value.shape[0]), :] = value


def spread(ref, row):
    half = ref.shape[0] // 2
    return tuple(jnp.broadcast_to(ref[pl.ds(row + i * half, 1), :], (ROWS, LANES)) for i in range(2))


class Kept:
    def __init__(self, ref, base, cx, cy, slots):
        self.ref, self.cy, self.cells = ref, cy, cx * cy
        self.base = base
        self.near_base = base + self.cells + FACES * ROWS
        self.energy_base = self.near_base + FACES * self.cells
        self.slots_base = self.energy_base + slots * ROWS

    @staticmethod
    def rows(cells, slots):
        return cells + FACES * ROWS + FACES * cells + slots * ROWS + ROWS

    def rate(self, x):
        return take(self.ref, self.base + x * self.cy, self.cy)

    def rate_beside(self, k):
        return take(self.ref, self.base + self.cells + k * ROWS, ROWS)

    def near(self, k, x):
        return take(self.ref, self.near_base + k * self.cells + x * self.cy, self.cy)

    def energy(self, q):
        return self.ref[self.energy_base + q * ROWS : self.energy_base + (q + 1) * ROWS, :]


def keep_on(out, out_base, kept, count):
    for i in range(2):
        put(out, out_base, i, take(kept.ref, kept.base, count)[i])


def fill(out, index, pair):
    out[index, :, :LANES], out[index, :, LANES:] = pair


def pair_faces(axis, low, high):
    even = lax.rem(lax.axis_index(axis), 2) == 0
    return even, (jnp.where(even, high, low), jnp.where(even, low, high))


def pack_faces(fields, cx, cy, slots, out_refs, axis, columns, slot_of=lambda place: place[0] * SHARE + place[1]):
    low, high = (LEFT, RIGHT) if columns else (BELOW, ABOVE)
    _, faces = pair_faces(axis, low, high)
    for out, face in zip(out_refs, faces):
        is_high = face == high
        for depth in range(2):
            if columns:
                first = jnp.where(is_high, cy - 1 - depth, depth)
                plane = lambda q: take(fields, q * (cx * cy) + first, cx, cy)
            else:
                first = jnp.where(is_high, cx - 1 - depth, depth) * cy
                plane = lambda q: take(fields, q * (cx * cy) + first, cy)
            for j in range(SHARE):
                fill(out, depth * SHARE + j, plane(slot_of((face, j))))
            if depth == 0:
                s0 = s1 = None
                for q in range(slots):
                    v0, v1 = plane(q)
                    s0 = v0 * v0 if s0 is None else s0 + v0 * v0
                    s1 = v1 * v1 if s1 is None else s1 + v1 * v1
                fill(out, 2 * SHARE, (s0, s1))


def open_body(
    cx, cy, slots, slabs, cols, ids_hbm, rows_hbm, fields_hbm, mask_hbm, coarse_hbm,
    raw, mask, slots_ref, bounds, planes, msg_a, msg_b, ids_smem, rows_smem, ids_ref, coarse_ref, mask_ref, sems,
):
    cells = cx * cy
    loads = [
        pltpu.make_async_copy(ids_hbm, ids_smem, sems.at[0]),
        pltpu.make_async_copy(ids_hbm, ids_ref, sems.at[1]),
        pltpu.make_async_copy(rows_hbm, rows_smem, sems.at[2]),
        pltpu.make_async_copy(coarse_hbm, coarse_ref, sems.at[3]),
    ]
    for i in range(2):
        half = pl.ds(i * LANES, LANES)
        loads.append(
            pltpu.make_async_copy(mask_hbm.at[:, half], mask_ref.at[pl.ds(i * cells, cells), :], sems.at[4 + i])
        )
        rows = slots * cells
        loads.append(
            pltpu.make_async_copy(fields_hbm.at[:, half], raw.at[pl.ds(i * rows, rows), :], sems.at[6 + i])
        )
    for load in loads:
        load.start()
    for load in loads[:4]:
        load.wait()
    place = slot_places(slabs, cols, slots, ids_ref, ids_smem)
    sub = lax.broadcasted_iota(jnp.int32, (slots, LANES), 0).astype(jnp.float32)
    slot_row = jnp.sum(place * sub, axis=0, keepdims=True)
    slots_ref[...] = jnp.broadcast_to(slot_row, (ROWS, LANES))
    lane = lax.broadcasted_iota(jnp.int32, (1, LANES), 1)
    taken = lambda q: jnp.sum(jnp.where(lane == q, slot_row, 0.0)).astype(jnp.int32)
    left = [taken(LEFT * SHARE + j) for j in range(SHARE)]
    right = [taken(RIGHT * SHARE + j) for j in range(SHARE)]

    s = lax.axis_index("slab")
    start = jnp.int32(0)
    for t in range(slabs):
        start = start + jnp.where(t < s, rows_smem[t], 0)
    live = rows_smem[s]
    bounds[0:ROWS, :] = jnp.full((ROWS, LANES), start, jnp.int32)
    bounds[ROWS : 2 * ROWS, :] = jnp.full((ROWS, LANES), start + live, jnp.int32)
    capacity, coarse_y, _ = coarse_ref.shape
    chosen = [
        jnp.clip(plane - start, 0, capacity - 1) for plane in near_planes(cx, slabs)
    ] + [jnp.int32(0), jnp.int32(1), live - 2, live - 1]
    _, faces = pair_faces("col", LEFT, RIGHT)
    for out in (msg_a, msg_b):
        out[2 * SHARE + 2] = jnp.zeros((ROWS, out.shape[2]), jnp.float32)
    planes[...] = jnp.zeros(planes.shape, jnp.float32)
    for i, p in enumerate(chosen):
        planes[i * ROWS + 1 : i * ROWS + 1 + coarse_y, :] = coarse_ref[p]
        for out, face in zip((msg_a, msg_b), faces):
            row = jnp.where(face == RIGHT, coarse_y - 1, 0)
            spot = slice(i // ROWS * LANES, (i // ROWS + 1) * LANES)
            out[2 * SHARE + 2, i % ROWS : i % ROWS + 1, spot] = coarse_ref[p, pl.ds(row, 1), :]

    for load in loads[4:]:
        load.wait()
    mask[...] = mask_ref[...].astype(jnp.float32)

    def slot_of(place):
        face, j = place
        return jnp.where(face == RIGHT, right[j], left[j])

    pack_faces(raw, cx, cy, slots, (msg_a, msg_b), "col", True, slot_of)
    for out, face in zip((msg_a, msg_b), faces):
        first = jnp.where(face == RIGHT, cy - 1, 0)
        fill(out, 2 * SHARE + 1, take(mask, first, cx, cy))


def near_planes(cx, slabs):
    s = lax.axis_index("slab")
    half = cx // 2
    return [jnp.clip(s * half - 1 + i, 0, slabs * half - 1) for i in range(half + 2)]


def arrange_body(
    cx, cy, slots, raw, mask, slots_ref, ids_ref, energy_ref, fields, energy_out, pre_a, pre_b
):
    cells = cx * cy
    s, c = lax.axis_index("slab"), lax.axis_index("col")
    for q in range(slots):
        slot = slots_ref[0, q].astype(jnp.int32)
        for i, part in enumerate(take(raw, slot * cells, cells)):
            put(fields, q * cells, i, part)
        value = jnp.full((ROWS, LANES), energy_ref[ids_ref[s, c, slot]], jnp.float32)
        energy_out[q * ROWS : (q + 1) * ROWS, :] = value
    pack_faces(fields, cx, cy, slots, (pre_a, pre_b), "slab", False)
    _, faces = pair_faces("slab", BELOW, ABOVE)
    for out, face in zip((pre_a, pre_b), faces):
        first = jnp.where(face == ABOVE, cx - 1, 0) * cy
        fill(out, 2 * SHARE + 1, take(mask, first, cy))


def slab_body(cx, slabs, cols, coarse_y, own, pre_a, pre_b, got_a, got_b, msg_a, msg_b, planes):
    have = present(slabs, cols)
    even, _ = pair_faces("col", LEFT, RIGHT)
    thermal = 2 * SHARE + 2
    from_a, from_b = got_a[thermal], got_b[thermal]
    lower = jnp.where(even, from_b, from_a)
    upper = jnp.where(even, from_a, from_b)
    sub = lax.broadcasted_iota(jnp.int32, (ROWS, LANES), 0)
    last = coarse_y + 1
    widened = []
    for i in range(cx // 2 + 6):
        plane = own[i * ROWS : (i + 1) * ROWS, :]
        spot = slice(i // ROWS * LANES, (i // ROWS + 1) * LANES)
        below = jnp.where(have[LEFT], lower[i % ROWS : i % ROWS + 1, spot], plane[1:2, :])
        above = jnp.where(have[RIGHT], upper[i % ROWS : i % ROWS + 1, spot], plane[coarse_y : coarse_y + 1, :])
        plane = jnp.where(sub == 0, below, jnp.where(sub == last, above, plane))
        widened.append(plane)
        if i < cx // 2 + 2:
            planes[i * ROWS : (i + 1) * ROWS, :] = plane
    first = cx // 2 + 2
    _, faces = pair_faces("slab", BELOW, ABOVE)
    for out, pre, face in zip((msg_a, msg_b), (pre_a, pre_b), faces):
        out[:thermal] = pre[...]
        for i in range(2):
            plane = jnp.where(face == ABOVE, widened[first + 2 + i], widened[first + i])
            out[thermal, :, i * LANES : (i + 1) * LANES] = plane


def axis_weights(cells):
    fine = np.arange(-1, cells + 1)
    lower = (2 * fine - 1) // 4
    weight = (2 * fine - 1 - 4 * lower) / 4.0
    out = np.zeros((cells + 2, cells // 2 + 2), np.float32)
    out[np.arange(cells + 2), lower + 1] += 1.0 - weight
    out[np.arange(cells + 2), lower + 2] += weight
    return out


def plane_weights(cx, cy):
    along, across = axis_weights(cx), axis_weights(cy)
    inner = [(x + 1, y + 1) for x in range(cx) for y in range(cy)]
    inner += [(0, y + 1) for y in range(cy)] + [(cx + 1, y + 1) for y in range(cy)]
    inner += [(x + 1, 0) for x in range(cx)] + [(x + 1, cy + 1) for x in range(cx)]
    out = np.zeros((len(inner), cx // 2 + 2, ROWS), np.float32)
    for row, (x, y) in enumerate(inner):
        out[row, :, : cy // 2 + 2] = along[x][:, None] * across[y][None, :]
    return out.reshape(len(inner), -1)


def height_weights(cells, coarse):
    fine = np.arange(cells)
    lower = (2 * fine - 1) // 4
    weight = (2 * fine - 1 - 4 * lower) / 4.0
    out = np.zeros((coarse, cells), np.float32)
    np.add.at(out, (np.clip(lower, 0, coarse - 1), fine), 1.0 - weight)
    np.add.at(out, (np.clip(lower + 1, 0, coarse - 1), fine), weight)
    return out


def mobility_body(
    cx, cy, slots, slabs, cols, planes, bounds, mask_ref, weights, height, energy, slots_ref,
    col_a, col_b, slab_a, slab_b, keep, near,
):
    start, end = bounds[0:ROWS, :], bounds[ROWS : 2 * ROWS, :]
    even_s, _ = pair_faces("slab", BELOW, ABOVE)
    even_c, _ = pair_faces("col", LEFT, RIGHT)
    thermal, mask = 2 * SHARE + 2, 2 * SHARE + 1
    below = jnp.where(even_s, slab_b[thermal], slab_a[thermal])
    above = jnp.where(even_s, slab_a[thermal], slab_b[thermal])
    for i, p in enumerate(near_planes(cx, slabs)):
        p = jnp.full((ROWS, LANES), p, jnp.int32)
        own = planes[i * ROWS : (i + 1) * ROWS, :]
        lower = jnp.where(p == start - 2, below[:, :LANES], below[:, LANES:])
        upper = jnp.where(p == end, above[:, :LANES], above[:, LANES:])
        near[i * ROWS : (i + 1) * ROWS, :] = jnp.where(p < start, lower, jnp.where(p < end, own, upper))
    flat = jnp.dot(weights[...], near[...], precision=HIGHEST, preferred_element_type=jnp.float32)
    profile = jnp.dot(flat, height[...], precision=HIGHEST, preferred_element_type=jnp.float32)
    mobility = jnp.exp(2.0 * (profile - 1.0)) * TIME_STEP
    cells = cx * cy
    kept = Kept(keep, 0, cx, cy, slots)
    for i, part in enumerate(take(mask_ref, 0, cells)):
        put(keep, 0, i, part * mobility[:cells, i * LANES : (i + 1) * LANES])
    have = present(slabs, cols)
    masks = (
        jnp.where(even_s, slab_b[mask], slab_a[mask]),
        jnp.where(even_s, slab_a[mask], slab_b[mask]),
        jnp.where(even_c, col_b[mask], col_a[mask]),
        jnp.where(even_c, col_a[mask], col_b[mask]),
    )
    for k in range(FACES):
        at = cells + k * ROWS
        for i, part in enumerate(split(jnp.where(have[k], masks[k] * mobility[at : at + ROWS], 0.0))):
            put(keep, at, i, part)
    for i in range(2):
        put(keep, kept.energy_base, i, energy[...])
        put(keep, kept.slots_base, i, slots_ref[...])
    marks = edges()
    top, bottom = marks[2:]
    for x in range(cx):
        sums = neighbours(x, cx - 1, kept.rate, kept.rate(x), None, None, marks)
        extra = [None] * FACES
        if x == 0:
            extra[BELOW] = kept.rate_beside(BELOW)
        if x == cx - 1:
            extra[ABOVE] = kept.rate_beside(ABOVE)
        extra[LEFT] = [jnp.where(top, v, 0.0) for v in spread(keep, cells + LEFT * ROWS + x)]
        extra[RIGHT] = [jnp.where(bottom, v, 0.0) for v in spread(keep, cells + RIGHT * ROWS + x)]
        for k in range(FACES):
            for i in range(2):
                value = sums[i] if extra[k] is None else sums[i] + extra[k][i]
                put(keep, kept.near_base + k * cells + x * cy, i, value)


def split(value):
    return value[:, :LANES], value[:, LANES:]


def along_height(v0, v1, first, last):
    r0, r1 = pltpu.roll(v0, 1, 1), pltpu.roll(v1, 1, 1)
    q0, q1 = pltpu.roll(v0, LANES - 1, 1), pltpu.roll(v1, LANES - 1, 1)
    return (
        jnp.where(first, 0.0, r0) + jnp.where(last, q1, q0),
        jnp.where(first, r0, r1) + jnp.where(last, 0.0, q1),
    )


def along_rows(v, top, bottom, lower, upper):
    down = jnp.where(top, 0.0 if lower is None else lower, pltpu.roll(v, 1, 0))
    up = jnp.where(bottom, 0.0 if upper is None else upper, pltpu.roll(v, ROWS - 1, 0))
    return down + up


def edges():
    lane = lax.broadcasted_iota(jnp.int32, (ROWS, LANES), 1)
    row = lax.broadcasted_iota(jnp.int32, (ROWS, LANES), 0)
    return lane == 0, lane == LANES - 1, row == 0, row == ROWS - 1


def neighbours(x, last_x, load, centre, halo, kind, marks):
    first, last, top, bottom = marks
    v0, v1 = centre
    n0, n1 = along_height(v0, v1, first, last)
    low = high = (None, None)
    if kind == LEFT:
        low = halo(x)
    if kind == RIGHT:
        high = halo(x)
    n0 = n0 + along_rows(v0, top, bottom, low[0], high[0])
    n1 = n1 + along_rows(v1, top, bottom, low[1], high[1])
    sides = []
    if not (isinstance(x, int) and x == 0):
        sides.append(load(x - 1))
    elif kind == BELOW:
        sides.append(halo(None))
    if not (isinstance(x, int) and x == last_x):
        sides.append(load(x + 1))
    elif kind == ABOVE:
        sides.append(halo(None))
    for a, b in sides:
        n0, n1 = n0 + a, n1 + b
    return n0, n1


def over_planes(cx, visit, carry):
    carry = visit(0, carry)
    carry = lax.fori_loop(1, cx - 1, visit, carry)
    return visit(cx - 1, carry)


def slot_access(fields, halos, base, q, cells, cy):
    def load(x):
        return take(fields, q * cells + x * cy, cy)

    def halo(x):
        if x is None:
            return take(halos, base + q * ROWS, ROWS)
        return spread(halos, base + q * ROWS + x)

    return load, halo


def force_of(v, n, squares3, energy):
    return v * (squares3 + ((5.0 - energy) + v * (energy - 2.0 * v))) - n


def triple_squares(fields, x, slots, cells, cy):
    total = None
    for q in range(slots):
        v0, v1 = take(fields, q * cells + x * cy, cy)
        total = (v0 * v0, v1 * v1) if total is None else (total[0] + v0 * v0, total[1] + v1 * v1)
    return 2.0 * COUPLING * total[0], 2.0 * COUPLING * total[1]


def inner_body(cx, cy, slots, base, *refs):
    fields, force_out = refs[0], refs[-1]
    cells = cx * cy
    marks = edges()
    if base is None:
        energy = lambda q: refs[1][q * ROWS : (q + 1) * ROWS, :]
    else:
        energy = Kept(fields, base, cx, cy, slots).energy

    def visit(x, carry):
        squares = triple_squares(fields, x, slots, cells, cy)
        for q in range(slots):
            load, _ = slot_access(fields, None, None, q, cells, cy)
            centre = load(x)
            near = neighbours(x, cx - 1, load, centre, None, None, marks)
            e = energy(q)
            for i in range(2):
                put(force_out, q * cells + x * cy, i, force_of(centre[i], near[i], squares[i], e))
        return carry

    over_planes(cx, visit, 0)


def arrivals(col_a, col_b, slab_a, slab_b):
    even_s, _ = pair_faces("slab", BELOW, ABOVE)
    even_c, _ = pair_faces("col", LEFT, RIGHT)
    pairs = ((slab_b, slab_a, even_s), (slab_a, slab_b, even_s), (col_b, col_a, even_c), (col_a, col_b, even_c))
    return [functools.partial(lambda u, v, even, i: jnp.where(even, u[i], v[i]), *pair) for pair in pairs]


class Grown:
    def __init__(self, cx, cy, slots):
        self.cells = cx * cy
        self.sum = slots * self.cells
        self.squares = self.sum + self.cells
        self.halos = self.squares + self.cells
        self.kept = self.halos + slots * ROWS
        self.count = Kept.rows(self.cells, slots)
        self.rows = self.kept + self.count


def sums_body(
    cx, cy, slots, slabs, cols, devices, base, fields, keep, force_in, col_a, col_b, slab_a, slab_b,
    grown, sums_ref, halos,
):
    cells = cx * cy
    marks = edges()
    first, last, top, bottom = marks
    have = present(slabs, cols)
    kept = Kept(keep, base, cx, cy, slots)
    layout = Grown(cx, cy, slots)
    keep_on(grown, layout.kept, kept, layout.count)
    for k, pick in enumerate(arrivals(col_a, col_b, slab_a, slab_b)):
        s0, s1 = split(2.0 * COUPLING * pick(2 * SHARE))
        h0, h1 = kept.rate_beside(k)
        for j in range(SHARE):
            q = k * SHARE + j
            v0, v1 = split(jnp.where(have[k], pick(j), 0.0))
            put(halos, q * ROWS, 0, v0)
            put(halos, q * ROWS, 1, v1)
            o0, o1 = split(pick(SHARE + j))
            if k == BELOW:
                i0, i1 = take(fields, q * cells, cy)
            elif k == ABOVE:
                i0, i1 = take(fields, (q + 1) * cells - cy, cy)
            elif k == LEFT:
                i0, i1 = take(fields, q * cells, cx, cy)
            else:
                i0, i1 = take(fields, q * cells + cy - 1, cx, cy)
            n0, n1 = along_height(v0, v1, first, last)
            n0 = n0 + along_rows(v0, top, bottom, None, None) + o0 + i0
            n1 = n1 + along_rows(v1, top, bottom, None, None) + o1 + i1
            e = kept.energy(q)
            put(grown, layout.halos + q * ROWS, 0, v0 - h0 * force_of(v0, n0, s0, e))
            put(grown, layout.halos + q * ROWS, 1, v1 - h1 * force_of(v1, n1, s1, e))

    energy_sum = None
    for q in range(slots):
        energy_sum = kept.energy(q) if energy_sum is None else energy_sum + kept.energy(q)
    zero = jnp.zeros((ROWS, LANES), jnp.float32)

    def visit(x, carry):
        total, c0, c1, c2, c3, weight = carry
        rate = kept.rate(x)
        forces, powers = [zero, zero], [zero, zero]
        a2, b1 = [zero, zero], [zero, zero]
        a1 = [[zero, zero] for _ in range(FACES)]
        for q in range(slots):
            k = q // SHARE
            centre = take(fields, q * cells + x * cy, cy)
            inner = take(force_in, q * cells + x * cy, cy)
            e = kept.energy(q)
            cross = (None, None)
            if k in (LEFT, RIGHT):
                row = spread(halos, q * ROWS + x)
                cross = [jnp.where(top if k == LEFT else bottom, row[i], 0.0) for i in range(2)]
            elif isinstance(x, int) and (k, x) in ((BELOW, 0), (ABOVE, cx - 1)):
                cross = take(halos, q * ROWS, ROWS)
            for i in range(2):
                force = inner[i] if cross[i] is None else inner[i] - cross[i]
                g = centre[i] - rate[i] * force
                put(grown, q * cells + x * cy, i, g)
                weighted, square = e * g, g * g
                forces[i] = forces[i] + force
                powers[i] = powers[i] + g * (weighted - (square + square))
                a1[k][i] = a1[k][i] + g
                a2[i] = a2[i] + square
                b1[i] = b1[i] + weighted
        beside = [kept.near(k, x) for k in range(FACES)]
        for i in range(2):
            h = rate[i]
            whole = (a1[0][i] + a1[1][i]) + (a1[2][i] + a1[3][i])
            near = [beside[k][i] for k in range(FACES)]
            put(grown, layout.sum + x * cy, i, whole)
            put(grown, layout.squares + x * cy, i, a2[i])
            total = total + h * forces[i]
            c0 = c0 + h * (powers[i] + 5.0 * whole - b1[i] + 2.0 * COUPLING * whole * a2[i])
            for k in range(FACES):
                c0 = c0 - a1[k][i] * near[k]
            linear = (
                energy_sum
                - 5.0 * slots
                - 2.0 * b1[i]
                + (6.0 - 2.0 * COUPLING * slots) * a2[i]
                - 4.0 * COUPLING * (whole * whole)
            )
            c1 = c1 + h * (h * linear + float(SHARE) * ((near[0] + near[1]) + (near[2] + near[3])))
            c2 = c2 + h * h * h * (energy_sum + (6.0 * COUPLING * slots - 6.0) * whole)
            c3 = c3 + (h * h) * (h * h)
            weight = weight + h
        return total, c0, c1, c2, c3, weight

    parts = over_planes(cx, visit, (zero,) * 6)
    back = -1.0 / TIME_STEP
    scales = (back, back, back, back, back * (2.0 * slots - 2.0 * COUPLING * slots * slots), 1.0 / TIME_STEP)
    lane = lax.broadcasted_iota(jnp.int32, (1, LANES), 1)
    row = jnp.zeros((1, LANES), jnp.float32)
    for i, (part, scale) in enumerate(zip(parts, scales)):
        value = jnp.sum(jnp.sum(part, axis=0, keepdims=True), axis=1, keepdims=True) * scale
        row = jnp.where(lane == i, value, row)
    sums_ref[...] = jnp.broadcast_to(row[None], (devices, 1, LANES))


def near_body(cx, cy, slots, grown, near_out):
    cells = cx * cy
    marks = edges()
    halos = Grown(cx, cy, slots).halos

    def visit(x, carry):
        for q in range(slots):
            load, halo = slot_access(grown, grown, halos, q, cells, cy)
            near = neighbours(x, cx - 1, load, load(x), halo, q // SHARE, marks)
            for i in range(2):
                put(near_out, q * cells + x * cy, i, near[i])
        return carry

    over_planes(cx, visit, 0)


def multipliers(got, slots):
    total = jnp.sum(got[...], axis=0)
    lane = lax.broadcasted_iota(jnp.int32, (1, LANES), 1)
    part = [jnp.sum(jnp.where(lane == i, total, 0.0), axis=1, keepdims=True) for i in range(6)]
    whole = slots * part[5]
    here = part[0] / whole
    later = (part[1] + here * (part[2] + here * (part[3] + here * part[4]))) / whole
    return jnp.broadcast_to(here, (ROWS, LANES)), jnp.broadcast_to(later, (ROWS, LANES))


def settle(cx, cy, slots, got, grown, near_in, store, done=None):
    cells = cx * cy
    here, later = multipliers(got, slots)
    layout = Grown(cx, cy, slots)
    kept = Kept(grown, layout.kept, cx, cy, slots)
    for k in range(FACES):

        def visit(x, carry):
            rate = kept.rate(x)
            near = kept.near(k, x)
            a1 = take(grown, layout.sum + x * cy, cy)
            a2 = take(grown, layout.squares + x * cy, cy)
            off = [here * rate[i] for i in range(2)]
            base = [
                5.0 + 2.0 * COUPLING * (a2[i] - off[i] * (2.0 * a1[i] - float(slots) * off[i])) for i in range(2)
            ]
            extra = [here * near[i] + later for i in range(2)]
            for q in range(k * SHARE, (k + 1) * SHARE):
                e = kept.energy(q)
                g = take(grown, q * cells + x * cy, cy)
                n = take(near_in, q * cells + x * cy, cy)
                for i in range(2):
                    f = g[i] - off[i]
                    force = f * ((base[i] - e) + f * (e - (f + f))) - (n[i] - extra[i])
                    store(q, x, i, f - rate[i] * force)
            return carry

        lax.fori_loop(0, cx, visit, 0)
        if done is not None:
            done(k)


def middle_body(cx, cy, slots, got, grown, near_in, fields, slab_a, slab_b):
    def store(q, x, i, value):
        put(fields, q * cx * cy + x * cy, i, value)

    settle(cx, cy, slots, got, grown, near_in, store)
    pack_faces(fields, cx, cy, slots, (slab_a, slab_b), "slab", False)
    layout = Grown(cx, cy, slots)
    keep_on(fields, slots * cx * cy, Kept(grown, layout.kept, cx, cy, slots), layout.count)


def cols_body(cx, cy, slots, fields, col_a, col_b):
    pack_faces(fields, cx, cy, slots, (col_a, col_b), "col", True)


def last_body(cx, cy, slots, got, grown, near_in, out, result, order, sems, order_sem):
    kept = Kept(grown, Grown(cx, cy, slots).kept, cx, cy, slots)
    fetch = pltpu.make_async_copy(grown.at[pl.ds(kept.slots_base, ROWS), :], order, order_sem)
    fetch.start()

    def store(q, x, i, value):
        at = x * cy if isinstance(x, int) else pl.multiple_of(x * cy, ROWS)
        result[q, pl.ds(at, cy), i * LANES : (i + 1) * LANES] = value

    def send(q):
        return pltpu.make_async_copy(result.at[q], out.at[order[0, q].astype(jnp.int32)], sems.at[q])

    def done(k):
        if k == 0:
            fetch.wait()
        for q in range(k * SHARE, (k + 1) * SHARE):
            send(q).start()

    settle(cx, cy, slots, got, grown, near_in, store, done)
    for q in range(slots):
        send(q).wait()


def exchange_cols(first, second):
    count = lax.axis_size("col")
    one = [(i, i ^ 1) for i in range(count)]
    two = [(i, (i - 1) % count if i % 2 == 0 else (i + 1) % count) for i in range(count)]
    return lax.ppermute(first, "col", one), lax.ppermute(second, "col", two)


def exchange_slabs(first, second):
    count, cols = lax.axis_size("slab"), lax.axis_size("col")
    one = [(i, i ^ 1) for i in range(count)]
    two = []
    for s in range(count):
        other = s - 1 if s % 2 == 0 else s + 1
        for c in range(cols):
            target = other * cols + c if 0 <= other < count else s * cols + (c ^ 1)
            two.append((s * cols + c, target))
    return lax.ppermute(second, ("slab", "col"), two), lax.ppermute(first, "slab", one)


def per_device(order_params, layer_mask, coarse_temp, coarse_rows, grain_ids, energy):
    slots, cx, cy, cz = order_params.shape
    slabs, cols = lax.axis_size("slab"), lax.axis_size("col")
    devices = slabs * cols
    cells = cx * cy
    capacity, _, coarse_z = coarse_temp.shape
    raw = order_params.reshape(slots * cells, cz)
    mask = layer_mask.reshape(cells, cz)
    message = f32(2 * SHARE + 3, ROWS, cz)
    short = f32(2 * SHARE + 1, ROWS, cz)
    state = f32(2 * slots * cells, cz // 2)

    hbm = lambda x: pltpu.with_memory_space_constraint(x, pltpu.HBM)
    near = cx // 2 + 2
    raw, mask, slot_order, bounds, planes, col_a, col_b = call(
        functools.partial(open_body, cx, cy, slots, slabs, cols),
        (
            state,
            f32(2 * cells, LANES),
            f32(ROWS, LANES),
            jax.ShapeDtypeStruct((2 * ROWS, LANES), jnp.int32),
            f32((near + 4) * ROWS, LANES),
            message,
            message,
        ),
        [HBM] * 5,
        (VMEM,) * 7,
        [
            pltpu.SMEM(grain_ids.shape, jnp.int32),
            pltpu.SMEM(coarse_rows.shape, jnp.int32),
            pltpu.VMEM(grain_ids.shape, jnp.int32),
            pltpu.VMEM(coarse_temp.shape, jnp.float32),
            pltpu.VMEM((2 * cells, LANES), jnp.int32),
            pltpu.SemaphoreType.DMA((8,)),
        ],
    )(hbm(grain_ids), hbm(coarse_rows), hbm(raw), hbm(mask), hbm(coarse_temp))
    col_a, col_b = exchange_cols(col_a, col_b)
    packed = f32(2 * SHARE + 2, ROWS, cz)
    fields, slot_energy, pre_a, pre_b = call(
        functools.partial(arrange_body, cx, cy, slots),
        (state, f32(slots * ROWS, LANES), packed, packed),
        [VMEM, VMEM, SMEM, SMEM, SMEM],
        (VMEM,) * 4,
    )(raw, mask, slot_order, grain_ids, energy)
    slab_a, slab_b, planes = call(
        functools.partial(slab_body, cx, slabs, cols, coarse_temp.shape[1]),
        (message, message, f32(near * ROWS, LANES)),
        [VMEM] * 5,
        (VMEM,) * 3,
    )(planes, pre_a, pre_b, col_a, col_b)
    slab_b, slab_a = exchange_slabs(slab_a, slab_b)
    weights = jnp.asarray(plane_weights(cx, cy))
    height = jnp.asarray(height_weights(cz, coarse_z))
    count = Kept.rows(cells, slots)
    keep = call(
        functools.partial(mobility_body, cx, cy, slots, slabs, cols),
        f32(2 * count, LANES),
        [VMEM] * 11,
        VMEM,
        [pltpu.VMEM((near * ROWS, LANES), jnp.float32)],
    )(planes, bounds, mask, weights, height, slot_energy, slot_order, col_a, col_b, slab_a, slab_b)

    for pair in range(STEPS // 2):
        base = None if pair == 0 else slots * cells
        inputs = (fields, slot_energy) if pair == 0 else (fields,)
        force = call(
            functools.partial(inner_body, cx, cy, slots, base),
            state,
            [VMEM] * len(inputs),
            VMEM,
            flops=1 << 23,
            size=1 << 22,
        )(*inputs)
        grown, sums = call(
            functools.partial(sums_body, cx, cy, slots, slabs, cols, devices, base or 0),
            (f32(2 * Grown(cx, cy, slots).rows, LANES), f32(devices, 1, LANES)),
            [VMEM] * 7,
            (VMEM,) * 2,
            [pltpu.VMEM((2 * slots * ROWS, LANES), jnp.float32)],
        )(fields, keep if pair == 0 else fields, force, col_a, col_b, slab_a, slab_b)
        got = lax.all_to_all(sums, ("slab", "col"), 0, 0)
        grown_near = call(
            functools.partial(near_body, cx, cy, slots),
            state,
            [VMEM],
            VMEM,
            flops=1 << 23,
            size=1 << 22,
        )(grown)
        if pair < STEPS // 2 - 1:
            fields, slab_a, slab_b = call(
                functools.partial(middle_body, cx, cy, slots),
                (f32(2 * (slots * cells + count), LANES), short, short),
                [VMEM] * 3,
                (VMEM,) * 3,
            )(got, grown, grown_near)
            col_a, col_b = call(
                functools.partial(cols_body, cx, cy, slots), (short, short), [VMEM], (VMEM,) * 2
            )(fields)
            slab_b, slab_a = exchange_slabs(slab_a, slab_b)
            col_a, col_b = exchange_cols(col_a, col_b)
        else:
            fields = call(
                functools.partial(last_body, cx, cy, slots),
                f32(slots, cells, cz),
                [VMEM] * 3,
                HBM,
                [
                    pltpu.VMEM((slots, cells, cz), jnp.float32),
                    pltpu.SMEM((ROWS, LANES), jnp.float32),
                    pltpu.SemaphoreType.DMA((slots,)),
                    pltpu.SemaphoreType.DMA(()),
                ],
            )(got, grown, grown_near)
    return fields.reshape(order_params.shape)


def solution(mesh):
    in_specs = (
        P(None, "slab", "col", None),
        P("slab", "col", None),
        P("slab", "col", None),
        P(),
        P(),
        P(),
    )
    out_specs = P(None, "slab", "col", None)
    return jax.shard_map(
        per_device, mesh=mesh, in_specs=in_specs, out_specs=out_specs, check_vma=False
    )
```

```python
import functools

import jax
import jax.numpy as jnp
import numpy as np
from jax import lax
from jax.experimental import pallas as pl
from jax.experimental.pallas import tpu as pltpu
from jax.sharding import PartitionSpec as P

SHARE = 4
STEPS = 4
TIME_STEP = 0.05
COUPLING = 1.5
BELOW, ABOVE, LEFT, RIGHT = range(4)
FACES = 4
LANES = 128
ROWS = 8
HIGHEST = lax.Precision.HIGHEST

VMEM = pl.BlockSpec(memory_space=pltpu.VMEM)
SMEM = pl.BlockSpec(memory_space=pltpu.SMEM)
HBM = pl.BlockSpec(memory_space=pltpu.HBM)


def call(body, out_shape, in_specs, out_specs, scratch=(), flops=1 << 20, size=1 << 20):
    return pl.pallas_call(
        body,
        out_shape=out_shape,
        in_specs=in_specs,
        out_specs=out_specs,
        scratch_shapes=list(scratch),
        compiler_params=pltpu.CompilerParams(vmem_limit_bytes=20 << 20),
        cost_estimate=pl.CostEstimate(flops=flops, bytes_accessed=size, transcendentals=0),
    )


def f32(*shape):
    return jax.ShapeDtypeStruct(shape, jnp.float32)


def present(slabs, cols):
    s, c = lax.axis_index("slab"), lax.axis_index("col")
    return (s > 0, s < slabs - 1, c > 0, c < cols - 1)


def beside(slabs, cols):
    s, c = lax.axis_index("slab"), lax.axis_index("col")
    return (
        (jnp.maximum(s - 1, 0), c),
        (jnp.minimum(s + 1, slabs - 1), c),
        (s, jnp.maximum(c - 1, 0)),
        (s, jnp.minimum(c + 1, cols - 1)),
    )


def slot_places(slabs, cols, slots, ids_ref, ids_smem):
    s, c = lax.axis_index("slab"), lax.axis_index("col")
    sub = lax.broadcasted_iota(jnp.int32, (slots, LANES), 0)
    lane = lax.broadcasted_iota(jnp.int32, (slots, LANES), 1)
    own = jnp.zeros((slots, LANES), jnp.int32)
    for q in range(slots):
        own = jnp.where(sub == q, ids_smem[s, c, q], own)
    one, zero = jnp.float32(1.0), jnp.float32(0.0)
    have = present(slabs, cols)
    matches, ranks = [], []
    for k, (ns, nc) in enumerate(beside(slabs, cols)):
        row = ids_ref[ns, pl.ds(nc, 1), :]
        row = jnp.concatenate([row, jnp.full((1, LANES - slots), -1, jnp.int32)], axis=1)
        row = jnp.broadcast_to(jnp.where(have[k], row, -1), (slots, LANES))
        hit = jnp.where((own == row) & (row >= 0), one, zero)
        shared = jnp.max(hit, axis=0, keepdims=True)
        matches.append(jnp.sum(hit, axis=1, keepdims=True))
        ranks.append(jnp.sum(jnp.where(row < own, shared, zero), axis=1, keepdims=True))
    free = one - (matches[0] + matches[1] + matches[2] + matches[3])
    lanef = lane.astype(jnp.float32)
    free_row = jnp.sum(jnp.where(sub == lane, free, zero), axis=0, keepdims=True)
    free_rank = jnp.sum(jnp.where(lane < sub, free_row, zero), axis=1, keepdims=True)
    place = jnp.zeros((slots, LANES), jnp.float32)
    skipped = jnp.int32(0)
    for k in range(FACES):
        at = matches[k] * (ranks[k] + k * SHARE - lanef)
        place = jnp.where((matches[k] > 0.5) & (jnp.abs(at) < 0.5), one, place)
        local = free_rank - (skipped * SHARE).astype(jnp.float32)
        inside = (local > -0.5) & (local < SHARE - 0.5) & (free > 0.5)
        inside = inside & jnp.logical_not(have[k])
        place = jnp.where(inside & (jnp.abs(local + k * SHARE - lanef) < 0.5), one, place)
        skipped = skipped + jnp.where(have[k], 0, 1)
    return place


def take(ref, at, rows, stride=1):
    half = ref.shape[0] // 2
    if stride == 1:
        if not isinstance(at, int):
            at = pl.multiple_of(at, ROWS)
        return ref[pl.ds(at, rows), :], ref[pl.ds(at + half, rows), :]
    return ref[pl.ds(at, rows, stride=stride), :], ref[pl.ds(at + half, rows, stride=stride), :]


def take_shifted(ref, at, rows, by):
    half = ref.shape[0] // 2
    return ref[pl.ds(at + by, rows), :], ref[pl.ds(at + by + half, rows), :]


def put(ref, at, i, value):
    if not isinstance(at, int):
        at = pl.multiple_of(at, ROWS)
    ref[pl.ds(at + i * (ref.shape[0] // 2), value.shape[0]), :] = value


def spread(ref, row):
    half = ref.shape[0] // 2
    return tuple(jnp.broadcast_to(ref[pl.ds(row + i * half, 1), :], (ROWS, LANES)) for i in range(2))


class Kept:
    def __init__(self, ref, base, cx, cy, slots):
        self.ref, self.cy, self.cells = ref, cy, cx * cy
        self.base = base
        self.near_base = base + self.cells + FACES * ROWS
        self.energy_base = self.near_base + FACES * self.cells
        self.slots_base = self.energy_base + slots * ROWS

    @staticmethod
    def rows(cells, slots):
        return cells + FACES * ROWS + FACES * cells + slots * ROWS + ROWS

    def rate(self, x):
        return take(self.ref, self.base + x * self.cy, self.cy)

    def rate_beside(self, k):
        return take(self.ref, self.base + self.cells + k * ROWS, ROWS)

    def near(self, k, x):
        return take(self.ref, self.near_base + k * self.cells + x * self.cy, self.cy)

    def energy(self, q):
        return self.ref[self.energy_base + q * ROWS : self.energy_base + (q + 1) * ROWS, :]


def keep_on(out, out_base, kept, count):
    for i in range(2):
        put(out, out_base, i, take(kept.ref, kept.base, count)[i])


def fill(out, index, pair):
    out[index, :, :LANES], out[index, :, LANES:] = pair


def pair_faces(axis, low, high):
    even = lax.rem(lax.axis_index(axis), 2) == 0
    return even, (jnp.where(even, high, low), jnp.where(even, low, high))


def pack_faces(fields, cx, cy, slots, out_refs, axis, columns, slot_of=lambda place: place[0] * SHARE + place[1]):
    low, high = (LEFT, RIGHT) if columns else (BELOW, ABOVE)
    _, faces = pair_faces(axis, low, high)
    for out, face in zip(out_refs, faces):
        is_high = face == high
        for depth in range(2):
            if columns:
                first = jnp.where(is_high, cy - 1 - depth, depth)
                plane = lambda q: take(fields, q * (cx * cy) + first, cx, cy)
            else:
                first = jnp.where(is_high, cx - 1 - depth, depth) * cy
                plane = lambda q: take(fields, q * (cx * cy) + first, cy)
            for j in range(SHARE):
                fill(out, depth * SHARE + j, plane(slot_of((face, j))))
            if depth == 0:
                s0 = s1 = None
                for q in range(slots):
                    v0, v1 = plane(q)
                    s0 = v0 * v0 if s0 is None else s0 + v0 * v0
                    s1 = v1 * v1 if s1 is None else s1 + v1 * v1
                fill(out, 2 * SHARE, (s0, s1))


def open_body(
    cx, cy, slots, slabs, cols, ids_hbm, rows_hbm, fields_hbm, mask_hbm, coarse_hbm,
    raw, mask, slots_ref, bounds, planes, msg_a, msg_b, ids_smem, rows_smem, ids_ref, coarse_ref, mask_ref, sems,
):
    cells = cx * cy
    loads = [
        pltpu.make_async_copy(ids_hbm, ids_smem, sems.at[0]),
        pltpu.make_async_copy(ids_hbm, ids_ref, sems.at[1]),
        pltpu.make_async_copy(rows_hbm, rows_smem, sems.at[2]),
        pltpu.make_async_copy(coarse_hbm, coarse_ref, sems.at[3]),
    ]
    for i in range(2):
        half = pl.ds(i * LANES, LANES)
        loads.append(
            pltpu.make_async_copy(mask_hbm.at[:, half], mask_ref.at[pl.ds(i * cells, cells), :], sems.at[4 + i])
        )
        rows = slots * cells
        loads.append(
            pltpu.make_async_copy(fields_hbm.at[:, half], raw.at[pl.ds(i * rows, rows), :], sems.at[6 + i])
        )
    for load in loads:
        load.start()
    for load in loads[:4]:
        load.wait()
    place = slot_places(slabs, cols, slots, ids_ref, ids_smem)
    sub = lax.broadcasted_iota(jnp.int32, (slots, LANES), 0).astype(jnp.float32)
    slot_row = jnp.sum(place * sub, axis=0, keepdims=True)
    slots_ref[...] = jnp.broadcast_to(slot_row, (ROWS, LANES))
    lane = lax.broadcasted_iota(jnp.int32, (1, LANES), 1)
    taken = lambda q: jnp.sum(jnp.where(lane == q, slot_row, 0.0)).astype(jnp.int32)
    left = [taken(LEFT * SHARE + j) for j in range(SHARE)]
    right = [taken(RIGHT * SHARE + j) for j in range(SHARE)]

    s = lax.axis_index("slab")
    start = jnp.int32(0)
    for t in range(slabs):
        start = start + jnp.where(t < s, rows_smem[t], 0)
    live = rows_smem[s]
    bounds[0:ROWS, :] = jnp.full((ROWS, LANES), start, jnp.int32)
    bounds[ROWS : 2 * ROWS, :] = jnp.full((ROWS, LANES), start + live, jnp.int32)
    capacity, coarse_y, _ = coarse_ref.shape
    chosen = [
        jnp.clip(plane - start, 0, capacity - 1) for plane in near_planes(cx, slabs)
    ] + [jnp.int32(0), jnp.int32(1), live - 2, live - 1]
    _, faces = pair_faces("col", LEFT, RIGHT)
    for out in (msg_a, msg_b):
        out[2 * SHARE + 2] = jnp.zeros((ROWS, out.shape[2]), jnp.float32)
    planes[...] = jnp.zeros(planes.shape, jnp.float32)
    for i, p in enumerate(chosen):
        planes[i * ROWS + 1 : i * ROWS + 1 + coarse_y, :] = coarse_ref[p]
        for out, face in zip((msg_a, msg_b), faces):
            row = jnp.where(face == RIGHT, coarse_y - 1, 0)
            spot = slice(i // ROWS * LANES, (i // ROWS + 1) * LANES)
            out[2 * SHARE + 2, i % ROWS : i % ROWS + 1, spot] = coarse_ref[p, pl.ds(row, 1), :]

    for load in loads[4:]:
        load.wait()
    mask[...] = mask_ref[...].astype(jnp.float32)

    def slot_of(place):
        face, j = place
        return jnp.where(face == RIGHT, right[j], left[j])

    pack_faces(raw, cx, cy, slots, (msg_a, msg_b), "col", True, slot_of)
    for out, face in zip((msg_a, msg_b), faces):
        first = jnp.where(face == RIGHT, cy - 1, 0)
        fill(out, 2 * SHARE + 1, take(mask, first, cx, cy))


def near_planes(cx, slabs):
    s = lax.axis_index("slab")
    half = cx // 2
    return [jnp.clip(s * half - 1 + i, 0, slabs * half - 1) for i in range(half + 2)]


def arrange_body(
    cx, cy, slots, raw, mask, slots_ref, ids_ref, energy_ref, fields, energy_out, pre_a, pre_b
):
    cells = cx * cy
    s, c = lax.axis_index("slab"), lax.axis_index("col")
    for q in range(slots):
        slot = slots_ref[0, q].astype(jnp.int32)
        for i, part in enumerate(take(raw, slot * cells, cells)):
            put(fields, q * cells, i, part)
        value = jnp.full((ROWS, LANES), energy_ref[ids_ref[s, c, slot]], jnp.float32)
        energy_out[q * ROWS : (q + 1) * ROWS, :] = value
    pack_faces(fields, cx, cy, slots, (pre_a, pre_b), "slab", False)
    _, faces = pair_faces("slab", BELOW, ABOVE)
    for out, face in zip((pre_a, pre_b), faces):
        first = jnp.where(face == ABOVE, cx - 1, 0) * cy
        fill(out, 2 * SHARE + 1, take(mask, first, cy))


def slab_body(cx, slabs, cols, coarse_y, own, pre_a, pre_b, got_a, got_b, msg_a, msg_b, planes):
    have = present(slabs, cols)
    even, _ = pair_faces("col", LEFT, RIGHT)
    thermal = 2 * SHARE + 2
    from_a, from_b = got_a[thermal], got_b[thermal]
    lower = jnp.where(even, from_b, from_a)
    upper = jnp.where(even, from_a, from_b)
    sub = lax.broadcasted_iota(jnp.int32, (ROWS, LANES), 0)
    last = coarse_y + 1
    widened = []
    for i in range(cx // 2 + 6):
        plane = own[i * ROWS : (i + 1) * ROWS, :]
        spot = slice(i // ROWS * LANES, (i // ROWS + 1) * LANES)
        below = jnp.where(have[LEFT], lower[i % ROWS : i % ROWS + 1, spot], plane[1:2, :])
        above = jnp.where(have[RIGHT], upper[i % ROWS : i % ROWS + 1, spot], plane[coarse_y : coarse_y + 1, :])
        plane = jnp.where(sub == 0, below, jnp.where(sub == last, above, plane))
        widened.append(plane)
        if i < cx // 2 + 2:
            planes[i * ROWS : (i + 1) * ROWS, :] = plane
    first = cx // 2 + 2
    _, faces = pair_faces("slab", BELOW, ABOVE)
    for out, pre, face in zip((msg_a, msg_b), (pre_a, pre_b), faces):
        out[:thermal] = pre[...]
        for i in range(2):
            plane = jnp.where(face == ABOVE, widened[first + 2 + i], widened[first + i])
            out[thermal, :, i * LANES : (i + 1) * LANES] = plane


def axis_weights(cells):
    fine = np.arange(-1, cells + 1)
    lower = (2 * fine - 1) // 4
    weight = (2 * fine - 1 - 4 * lower) / 4.0
    out = np.zeros((cells + 2, cells // 2 + 2), np.float32)
    out[np.arange(cells + 2), lower + 1] += 1.0 - weight
    out[np.arange(cells + 2), lower + 2] += weight
    return out


def plane_weights(cx, cy):
    along, across = axis_weights(cx), axis_weights(cy)
    inner = [(x + 1, y + 1) for x in range(cx) for y in range(cy)]
    inner += [(0, y + 1) for y in range(cy)] + [(cx + 1, y + 1) for y in range(cy)]
    inner += [(x + 1, 0) for x in range(cx)] + [(x + 1, cy + 1) for x in range(cx)]
    out = np.zeros((len(inner), cx // 2 + 2, ROWS), np.float32)
    for row, (x, y) in enumerate(inner):
        out[row, :, : cy // 2 + 2] = along[x][:, None] * across[y][None, :]
    return out.reshape(len(inner), -1)


def height_weights(cells, coarse):
    fine = np.arange(cells)
    lower = (2 * fine - 1) // 4
    weight = (2 * fine - 1 - 4 * lower) / 4.0
    out = np.zeros((coarse, cells), np.float32)
    np.add.at(out, (np.clip(lower, 0, coarse - 1), fine), 1.0 - weight)
    np.add.at(out, (np.clip(lower + 1, 0, coarse - 1), fine), weight)
    return out


def mobility_body(
    cx, cy, slots, slabs, cols, planes, bounds, mask_ref, weights, height, energy, slots_ref,
    col_a, col_b, slab_a, slab_b, keep, near,
):
    start, end = bounds[0:ROWS, :], bounds[ROWS : 2 * ROWS, :]
    even_s, _ = pair_faces("slab", BELOW, ABOVE)
    even_c, _ = pair_faces("col", LEFT, RIGHT)
    thermal, mask = 2 * SHARE + 2, 2 * SHARE + 1
    below = jnp.where(even_s, slab_b[thermal], slab_a[thermal])
    above = jnp.where(even_s, slab_a[thermal], slab_b[thermal])
    for i, p in enumerate(near_planes(cx, slabs)):
        p = jnp.full((ROWS, LANES), p, jnp.int32)
        own = planes[i * ROWS : (i + 1) * ROWS, :]
        lower = jnp.where(p == start - 2, below[:, :LANES], below[:, LANES:])
        upper = jnp.where(p == end, above[:, :LANES], above[:, LANES:])
        near[i * ROWS : (i + 1) * ROWS, :] = jnp.where(p < start, lower, jnp.where(p < end, own, upper))
    flat = jnp.dot(weights[...], near[...], precision=HIGHEST, preferred_element_type=jnp.float32)
    profile = jnp.dot(flat, height[...], precision=HIGHEST, preferred_element_type=jnp.float32)
    mobility = jnp.exp(2.0 * (profile - 1.0)) * TIME_STEP
    cells = cx * cy
    kept = Kept(keep, 0, cx, cy, slots)
    for i, part in enumerate(take(mask_ref, 0, cells)):
        put(keep, 0, i, part * mobility[:cells, i * LANES : (i + 1) * LANES])
    have = present(slabs, cols)
    masks = (
        jnp.where(even_s, slab_b[mask], slab_a[mask]),
        jnp.where(even_s, slab_a[mask], slab_b[mask]),
        jnp.where(even_c, col_b[mask], col_a[mask]),
        jnp.where(even_c, col_a[mask], col_b[mask]),
    )
    for k in range(FACES):
        at = cells + k * ROWS
        for i, part in enumerate(split(jnp.where(have[k], masks[k] * mobility[at : at + ROWS], 0.0))):
            put(keep, at, i, part)
    for i in range(2):
        put(keep, kept.energy_base, i, energy[...])
        put(keep, kept.slots_base, i, slots_ref[...])
    marks = edges()
    top, bottom = marks[2:]
    for x in range(cx):
        sums = neighbours(x, cx - 1, kept.rate, kept.rate(x), None, None, marks)
        extra = [None] * FACES
        if x == 0:
            extra[BELOW] = kept.rate_beside(BELOW)
        if x == cx - 1:
            extra[ABOVE] = kept.rate_beside(ABOVE)
        extra[LEFT] = [jnp.where(top, v, 0.0) for v in spread(keep, cells + LEFT * ROWS + x)]
        extra[RIGHT] = [jnp.where(bottom, v, 0.0) for v in spread(keep, cells + RIGHT * ROWS + x)]
        for k in range(FACES):
            for i in range(2):
                value = sums[i] if extra[k] is None else sums[i] + extra[k][i]
                put(keep, kept.near_base + k * cells + x * cy, i, value)


def split(value):
    return value[:, :LANES], value[:, LANES:]


def along_height(v0, v1, first, last):
    r0, r1 = pltpu.roll(v0, 1, 1), pltpu.roll(v1, 1, 1)
    q0, q1 = pltpu.roll(v0, LANES - 1, 1), pltpu.roll(v1, LANES - 1, 1)
    return (
        jnp.where(first, 0.0, r0) + jnp.where(last, q1, q0),
        jnp.where(first, r0, r1) + jnp.where(last, 0.0, q1),
    )


def along_rows(v, top, bottom, lower, upper, shifted=None):
    before, after = shifted or (pltpu.roll(v, 1, 0), pltpu.roll(v, ROWS - 1, 0))
    down = jnp.where(top, 0.0 if lower is None else lower, before)
    up = jnp.where(bottom, 0.0 if upper is None else upper, after)
    return down + up


def edges():
    lane = lax.broadcasted_iota(jnp.int32, (ROWS, LANES), 1)
    row = lax.broadcasted_iota(jnp.int32, (ROWS, LANES), 0)
    return lane == 0, lane == LANES - 1, row == 0, row == ROWS - 1


def neighbours(x, last_x, load, centre, halo, kind, marks, shift=None):
    first, last, top, bottom = marks
    v0, v1 = centre
    n0, n1 = along_height(v0, v1, first, last)
    low = high = (None, None)
    if kind == LEFT:
        low = halo(x)
    if kind == RIGHT:
        high = halo(x)
    shifted = (None, None)
    if shift is not None and 0 < x < last_x:
        before, after = shift(x, -1), shift(x, 1)
        shifted = tuple(zip(before, after))
    n0 = n0 + along_rows(v0, top, bottom, low[0], high[0], shifted[0])
    n1 = n1 + along_rows(v1, top, bottom, low[1], high[1], shifted[1])
    sides = []
    if not (isinstance(x, int) and x == 0):
        sides.append(load(x - 1))
    elif kind == BELOW:
        sides.append(halo(None))
    if not (isinstance(x, int) and x == last_x):
        sides.append(load(x + 1))
    elif kind == ABOVE:
        sides.append(halo(None))
    for a, b in sides:
        n0, n1 = n0 + a, n1 + b
    return n0, n1


def over_planes(cx, visit, carry):
    carry = visit(0, carry)
    carry = lax.fori_loop(1, cx - 1, visit, carry)
    return visit(cx - 1, carry)


def slot_access(fields, halos, base, q, cells, cy):
    def load(x):
        return take(fields, q * cells + x * cy, cy)

    def halo(x):
        if x is None:
            return take(halos, base + q * ROWS, ROWS)
        return spread(halos, base + q * ROWS + x)

    return load, halo


def force_of(v, n, squares3, energy):
    return v * (squares3 + ((5.0 - energy) + v * (energy - 2.0 * v))) - n


def triple_squares(fields, x, slots, cells, cy):
    total = None
    for q in range(slots):
        v0, v1 = take(fields, q * cells + x * cy, cy)
        total = (v0 * v0, v1 * v1) if total is None else (total[0] + v0 * v0, total[1] + v1 * v1)
    return 2.0 * COUPLING * total[0], 2.0 * COUPLING * total[1]


def inner_body(cx, cy, slots, base, *refs):
    fields, force_out = refs[0], refs[-1]
    cells = cx * cy
    marks = edges()
    if base is None:
        energy = lambda q: refs[1][q * ROWS : (q + 1) * ROWS, :]
    else:
        energy = Kept(fields, base, cx, cy, slots).energy

    def visit(x, carry):
        squares = triple_squares(fields, x, slots, cells, cy)
        for q in range(slots):
            load, _ = slot_access(fields, None, None, q, cells, cy)
            centre = load(x)
            shift = lambda y, by: take_shifted(fields, q * cells + y * cy, cy, by)
            near = neighbours(x, cx - 1, load, centre, None, None, marks, shift)
            e = energy(q)
            for i in range(2):
                put(force_out, q * cells + x * cy, i, force_of(centre[i], near[i], squares[i], e))
        return carry

    for x in range(cx):
        visit(x, 0)


def arrivals(col_a, col_b, slab_a, slab_b):
    even_s, _ = pair_faces("slab", BELOW, ABOVE)
    even_c, _ = pair_faces("col", LEFT, RIGHT)
    pairs = ((slab_b, slab_a, even_s), (slab_a, slab_b, even_s), (col_b, col_a, even_c), (col_a, col_b, even_c))
    return [functools.partial(lambda u, v, even, i: jnp.where(even, u[i], v[i]), *pair) for pair in pairs]


class Grown:
    def __init__(self, cx, cy, slots):
        self.cells = cx * cy
        self.sum = slots * self.cells
        self.squares = self.sum + self.cells
        self.halos = self.squares + self.cells
        self.kept = self.halos + slots * ROWS
        self.count = Kept.rows(self.cells, slots)
        self.rows = self.kept + self.count


def sums_body(
    cx, cy, slots, slabs, cols, devices, base, fields, keep, force_in, col_a, col_b, slab_a, slab_b,
    grown, sums_ref, halos,
):
    cells = cx * cy
    marks = edges()
    first, last, top, bottom = marks
    have = present(slabs, cols)
    kept = Kept(keep, base, cx, cy, slots)
    layout = Grown(cx, cy, slots)
    keep_on(grown, layout.kept, kept, layout.count)
    for k, pick in enumerate(arrivals(col_a, col_b, slab_a, slab_b)):
        s0, s1 = split(2.0 * COUPLING * pick(2 * SHARE))
        h0, h1 = kept.rate_beside(k)
        for j in range(SHARE):
            q = k * SHARE + j
            v0, v1 = split(jnp.where(have[k], pick(j), 0.0))
            put(halos, q * ROWS, 0, v0)
            put(halos, q * ROWS, 1, v1)
            o0, o1 = split(pick(SHARE + j))
            if k == BELOW:
                i0, i1 = take(fields, q * cells, cy)
            elif k == ABOVE:
                i0, i1 = take(fields, (q + 1) * cells - cy, cy)
            elif k == LEFT:
                i0, i1 = take(fields, q * cells, cx, cy)
            else:
                i0, i1 = take(fields, q * cells + cy - 1, cx, cy)
            n0, n1 = along_height(v0, v1, first, last)
            n0 = n0 + along_rows(v0, top, bottom, None, None) + o0 + i0
            n1 = n1 + along_rows(v1, top, bottom, None, None) + o1 + i1
            e = kept.energy(q)
            put(grown, layout.halos + q * ROWS, 0, v0 - h0 * force_of(v0, n0, s0, e))
            put(grown, layout.halos + q * ROWS, 1, v1 - h1 * force_of(v1, n1, s1, e))

    energy_sum = None
    for q in range(slots):
        energy_sum = kept.energy(q) if energy_sum is None else energy_sum + kept.energy(q)
    zero = jnp.zeros((ROWS, LANES), jnp.float32)

    def visit(x, carry):
        total, c0, c1, c2, c3, weight = carry
        rate = kept.rate(x)
        forces, powers = [zero, zero], [zero, zero]
        a2, b1 = [zero, zero], [zero, zero]
        a1 = [[zero, zero] for _ in range(FACES)]
        for q in range(slots):
            k = q // SHARE
            centre = take(fields, q * cells + x * cy, cy)
            inner = take(force_in, q * cells + x * cy, cy)
            e = kept.energy(q)
            cross = (None, None)
            if k in (LEFT, RIGHT):
                row = spread(halos, q * ROWS + x)
                cross = [jnp.where(top if k == LEFT else bottom, row[i], 0.0) for i in range(2)]
            elif isinstance(x, int) and (k, x) in ((BELOW, 0), (ABOVE, cx - 1)):
                cross = take(halos, q * ROWS, ROWS)
            for i in range(2):
                force = inner[i] if cross[i] is None else inner[i] - cross[i]
                g = centre[i] - rate[i] * force
                put(grown, q * cells + x * cy, i, g)
                weighted, square = e * g, g * g
                forces[i] = forces[i] + force
                powers[i] = powers[i] + g * (weighted - (square + square))
                a1[k][i] = a1[k][i] + g
                a2[i] = a2[i] + square
                b1[i] = b1[i] + weighted
        beside = [kept.near(k, x) for k in range(FACES)]
        for i in range(2):
            h = rate[i]
            whole = (a1[0][i] + a1[1][i]) + (a1[2][i] + a1[3][i])
            near = [beside[k][i] for k in range(FACES)]
            put(grown, layout.sum + x * cy, i, whole)
            put(grown, layout.squares + x * cy, i, a2[i])
            total = total + h * forces[i]
            c0 = c0 + h * (powers[i] + 5.0 * whole - b1[i] + 2.0 * COUPLING * whole * a2[i])
            for k in range(FACES):
                c0 = c0 - a1[k][i] * near[k]
            linear = (
                energy_sum
                - 5.0 * slots
                - 2.0 * b1[i]
                + (6.0 - 2.0 * COUPLING * slots) * a2[i]
                - 4.0 * COUPLING * (whole * whole)
            )
            c1 = c1 + h * (h * linear + float(SHARE) * ((near[0] + near[1]) + (near[2] + near[3])))
            c2 = c2 + h * h * h * (energy_sum + (6.0 * COUPLING * slots - 6.0) * whole)
            c3 = c3 + (h * h) * (h * h)
            weight = weight + h
        return total, c0, c1, c2, c3, weight

    parts = over_planes(cx, visit, (zero,) * 6)
    back = -1.0 / TIME_STEP
    scales = (back, back, back, back, back * (2.0 * slots - 2.0 * COUPLING * slots * slots), 1.0 / TIME_STEP)
    lane = lax.broadcasted_iota(jnp.int32, (1, LANES), 1)
    row = jnp.zeros((1, LANES), jnp.float32)
    for i, (part, scale) in enumerate(zip(parts, scales)):
        value = jnp.sum(jnp.sum(part, axis=0, keepdims=True), axis=1, keepdims=True) * scale
        row = jnp.where(lane == i, value, row)
    sums_ref[...] = jnp.broadcast_to(row[None], (devices, 1, LANES))


def multipliers(got, slots):
    total = jnp.sum(got[...], axis=0)
    lane = lax.broadcasted_iota(jnp.int32, (1, LANES), 1)
    part = [jnp.sum(jnp.where(lane == i, total, 0.0), axis=1, keepdims=True) for i in range(6)]
    whole = slots * part[5]
    here = part[0] / whole
    later = (part[1] + here * (part[2] + here * (part[3] + here * part[4]))) / whole
    return jnp.broadcast_to(here, (ROWS, LANES)), jnp.broadcast_to(later, (ROWS, LANES))


def settle(cx, cy, slots, got, grown, store, done=None):
    cells = cx * cy
    marks = edges()
    here, later = multipliers(got, slots)
    layout = Grown(cx, cy, slots)
    kept = Kept(grown, layout.kept, cx, cy, slots)
    for k in range(FACES):

        def visit(x, carry):
            rate = kept.rate(x)
            near = kept.near(k, x)
            a1 = take(grown, layout.sum + x * cy, cy)
            a2 = take(grown, layout.squares + x * cy, cy)
            off = [here * rate[i] for i in range(2)]
            base = [
                5.0 + 2.0 * COUPLING * (a2[i] - off[i] * (2.0 * a1[i] - float(slots) * off[i])) for i in range(2)
            ]
            extra = [here * near[i] + later for i in range(2)]
            for q in range(k * SHARE, (k + 1) * SHARE):
                e = kept.energy(q)
                load, halo = slot_access(grown, grown, layout.halos, q, cells, cy)
                shift = lambda y, by: take_shifted(grown, q * cells + y * cy, cy, by)
                g = load(x)
                n = neighbours(x, cx - 1, load, g, halo, k, marks, shift)
                for i in range(2):
                    f = g[i] - off[i]
                    force = f * ((base[i] - e) + f * (e - (f + f))) - (n[i] - extra[i])
                    store(q, x, i, f - rate[i] * force)
            return carry

        for x in range(cx):
            visit(x, 0)
        if done is not None:
            done(k)


def middle_body(cx, cy, slots, got, grown, fields, slab_a, slab_b):
    def store(q, x, i, value):
        put(fields, q * cx * cy + x * cy, i, value)

    settle(cx, cy, slots, got, grown, store)
    pack_faces(fields, cx, cy, slots, (slab_a, slab_b), "slab", False)
    layout = Grown(cx, cy, slots)
    keep_on(fields, slots * cx * cy, Kept(grown, layout.kept, cx, cy, slots), layout.count)


def cols_body(cx, cy, slots, fields, col_a, col_b):
    pack_faces(fields, cx, cy, slots, (col_a, col_b), "col", True)


def last_body(cx, cy, slots, got, grown, out, result, order, sems, order_sem):
    kept = Kept(grown, Grown(cx, cy, slots).kept, cx, cy, slots)
    fetch = pltpu.make_async_copy(grown.at[pl.ds(kept.slots_base, ROWS), :], order, order_sem)
    fetch.start()

    def store(q, x, i, value):
        at = x * cy if isinstance(x, int) else pl.multiple_of(x * cy, ROWS)
        result[q, pl.ds(at, cy), i * LANES : (i + 1) * LANES] = value

    def send(q):
        return pltpu.make_async_copy(result.at[q], out.at[order[0, q].astype(jnp.int32)], sems.at[q])

    def done(k):
        if k == 0:
            fetch.wait()
        for q in range(k * SHARE, (k + 1) * SHARE):
            send(q).start()

    settle(cx, cy, slots, got, grown, store, done)
    for q in range(slots):
        send(q).wait()


def exchange_cols(first, second):
    count = lax.axis_size("col")
    one = [(i, i ^ 1) for i in range(count)]
    two = [(i, (i - 1) % count if i % 2 == 0 else (i + 1) % count) for i in range(count)]
    return lax.ppermute(first, "col", one), lax.ppermute(second, "col", two)


def exchange_slabs(first, second):
    count, cols = lax.axis_size("slab"), lax.axis_size("col")
    one = [(i, i ^ 1) for i in range(count)]
    two = []
    for s in range(count):
        other = s - 1 if s % 2 == 0 else s + 1
        for c in range(cols):
            target = other * cols + c if 0 <= other < count else s * cols + (c ^ 1)
            two.append((s * cols + c, target))
    return lax.ppermute(second, ("slab", "col"), two), lax.ppermute(first, "slab", one)


def per_device(order_params, layer_mask, coarse_temp, coarse_rows, grain_ids, energy):
    slots, cx, cy, cz = order_params.shape
    slabs, cols = lax.axis_size("slab"), lax.axis_size("col")
    devices = slabs * cols
    cells = cx * cy
    capacity, _, coarse_z = coarse_temp.shape
    raw = order_params.reshape(slots * cells, cz)
    mask = layer_mask.reshape(cells, cz)
    message = f32(2 * SHARE + 3, ROWS, cz)
    short = f32(2 * SHARE + 1, ROWS, cz)
    state = f32(2 * slots * cells, cz // 2)

    hbm = lambda x: pltpu.with_memory_space_constraint(x, pltpu.HBM)
    near = cx // 2 + 2
    raw, mask, slot_order, bounds, planes, col_a, col_b = call(
        functools.partial(open_body, cx, cy, slots, slabs, cols),
        (
            state,
            f32(2 * cells, LANES),
            f32(ROWS, LANES),
            jax.ShapeDtypeStruct((2 * ROWS, LANES), jnp.int32),
            f32((near + 4) * ROWS, LANES),
            message,
            message,
        ),
        [HBM] * 5,
        (VMEM,) * 7,
        [
            pltpu.SMEM(grain_ids.shape, jnp.int32),
            pltpu.SMEM(coarse_rows.shape, jnp.int32),
            pltpu.VMEM(grain_ids.shape, jnp.int32),
            pltpu.VMEM(coarse_temp.shape, jnp.float32),
            pltpu.VMEM((2 * cells, LANES), jnp.int32),
            pltpu.SemaphoreType.DMA((8,)),
        ],
    )(hbm(grain_ids), hbm(coarse_rows), hbm(raw), hbm(mask), hbm(coarse_temp))
    col_a, col_b = exchange_cols(col_a, col_b)
    packed = f32(2 * SHARE + 2, ROWS, cz)
    fields, slot_energy, pre_a, pre_b = call(
        functools.partial(arrange_body, cx, cy, slots),
        (state, f32(slots * ROWS, LANES), packed, packed),
        [VMEM, VMEM, SMEM, SMEM, SMEM],
        (VMEM,) * 4,
    )(raw, mask, slot_order, grain_ids, energy)
    slab_a, slab_b, planes = call(
        functools.partial(slab_body, cx, slabs, cols, coarse_temp.shape[1]),
        (message, message, f32(near * ROWS, LANES)),
        [VMEM] * 5,
        (VMEM,) * 3,
    )(planes, pre_a, pre_b, col_a, col_b)
    slab_b, slab_a = exchange_slabs(slab_a, slab_b)
    weights = jnp.asarray(plane_weights(cx, cy))
    height = jnp.asarray(height_weights(cz, coarse_z))
    count = Kept.rows(cells, slots)
    keep = call(
        functools.partial(mobility_body, cx, cy, slots, slabs, cols),
        f32(2 * count, LANES),
        [VMEM] * 11,
        VMEM,
        [pltpu.VMEM((near * ROWS, LANES), jnp.float32)],
    )(planes, bounds, mask, weights, height, slot_energy, slot_order, col_a, col_b, slab_a, slab_b)

    for pair in range(STEPS // 2):
        base = None if pair == 0 else slots * cells
        inputs = (fields, slot_energy) if pair == 0 else (fields,)
        force = call(
            functools.partial(inner_body, cx, cy, slots, base),
            state,
            [VMEM] * len(inputs),
            VMEM,
            flops=1 << 23,
            size=1 << 22,
        )(*inputs)
        grown, sums = call(
            functools.partial(sums_body, cx, cy, slots, slabs, cols, devices, base or 0),
            (f32(2 * Grown(cx, cy, slots).rows, LANES), f32(devices, 1, LANES)),
            [VMEM] * 7,
            (VMEM,) * 2,
            [pltpu.VMEM((2 * slots * ROWS, LANES), jnp.float32)],
        )(fields, keep if pair == 0 else fields, force, col_a, col_b, slab_a, slab_b)
        got = lax.all_to_all(sums, ("slab", "col"), 0, 0)
        if pair < STEPS // 2 - 1:
            fields, slab_a, slab_b = call(
                functools.partial(middle_body, cx, cy, slots),
                (f32(2 * (slots * cells + count), LANES), short, short),
                [VMEM] * 2,
                (VMEM,) * 3,
            )(got, grown)
            col_a, col_b = call(
                functools.partial(cols_body, cx, cy, slots), (short, short), [VMEM], (VMEM,) * 2
            )(fields)
            slab_b, slab_a = exchange_slabs(slab_a, slab_b)
            col_a, col_b = exchange_cols(col_a, col_b)
        else:
            fields = call(
                functools.partial(last_body, cx, cy, slots),
                f32(slots, cells, cz),
                [VMEM] * 2,
                HBM,
                [
                    pltpu.VMEM((slots, cells, cz), jnp.float32),
                    pltpu.SMEM((ROWS, LANES), jnp.float32),
                    pltpu.SemaphoreType.DMA((slots,)),
                    pltpu.SemaphoreType.DMA(()),
                ],
            )(got, grown)
    return fields.reshape(order_params.shape)


def solution(mesh):
    in_specs = (
        P(None, "slab", "col", None),
        P("slab", "col", None),
        P("slab", "col", None),
        P(),
        P(),
        P(),
    )
    out_specs = P(None, "slab", "col", None)
    return jax.shard_map(
        per_device, mesh=mesh, in_specs=in_specs, out_specs=out_specs, check_vma=False
    )
```

```python
import functools

import jax
import jax.numpy as jnp
import numpy as np
from jax import lax
from jax.experimental import pallas as pl
from jax.experimental.pallas import tpu as pltpu
from jax.sharding import PartitionSpec as P

SHARE = 4
STEPS = 4
TIME_STEP = 0.05
COUPLING = 1.5
BELOW, ABOVE, LEFT, RIGHT = range(4)
FACES = 4
MASK = 2 * SHARE
THERMAL = MASK + 1
LANES = 128
ROWS = 8
HIGHEST = lax.Precision.HIGHEST

VMEM = pl.BlockSpec(memory_space=pltpu.VMEM)
SMEM = pl.BlockSpec(memory_space=pltpu.SMEM)
HBM = pl.BlockSpec(memory_space=pltpu.HBM)


def call(body, out_shape, in_specs, out_specs, scratch=(), flops=1 << 20, size=1 << 20):
    return pl.pallas_call(
        body,
        out_shape=out_shape,
        in_specs=in_specs,
        out_specs=out_specs,
        scratch_shapes=list(scratch),
        compiler_params=pltpu.CompilerParams(vmem_limit_bytes=20 << 20),
        cost_estimate=pl.CostEstimate(flops=flops, bytes_accessed=size, transcendentals=0),
    )


def f32(*shape):
    return jax.ShapeDtypeStruct(shape, jnp.float32)


def present(slabs, cols):
    s, c = lax.axis_index("slab"), lax.axis_index("col")
    return (s > 0, s < slabs - 1, c > 0, c < cols - 1)


def beside(slabs, cols):
    s, c = lax.axis_index("slab"), lax.axis_index("col")
    return (
        (jnp.maximum(s - 1, 0), c),
        (jnp.minimum(s + 1, slabs - 1), c),
        (s, jnp.maximum(c - 1, 0)),
        (s, jnp.minimum(c + 1, cols - 1)),
    )


def slot_places(slabs, cols, slots, ids_ref, ids_smem):
    s, c = lax.axis_index("slab"), lax.axis_index("col")
    sub = lax.broadcasted_iota(jnp.int32, (slots, LANES), 0)
    lane = lax.broadcasted_iota(jnp.int32, (slots, LANES), 1)
    own = jnp.zeros((slots, LANES), jnp.int32)
    for q in range(slots):
        own = jnp.where(sub == q, ids_smem[s, c, q], own)
    one, zero = jnp.float32(1.0), jnp.float32(0.0)
    have = present(slabs, cols)
    matches, ranks = [], []
    for k, (ns, nc) in enumerate(beside(slabs, cols)):
        row = ids_ref[ns, pl.ds(nc, 1), :]
        row = jnp.concatenate([row, jnp.full((1, LANES - slots), -1, jnp.int32)], axis=1)
        row = jnp.broadcast_to(jnp.where(have[k], row, -1), (slots, LANES))
        hit = jnp.where((own == row) & (row >= 0), one, zero)
        shared = jnp.max(hit, axis=0, keepdims=True)
        matches.append(jnp.sum(hit, axis=1, keepdims=True))
        ranks.append(jnp.sum(jnp.where(row < own, shared, zero), axis=1, keepdims=True))
    free = one - (matches[0] + matches[1] + matches[2] + matches[3])
    lanef = lane.astype(jnp.float32)
    free_row = jnp.sum(jnp.where(sub == lane, free, zero), axis=0, keepdims=True)
    free_rank = jnp.sum(jnp.where(lane < sub, free_row, zero), axis=1, keepdims=True)
    place = jnp.zeros((slots, LANES), jnp.float32)
    skipped = jnp.int32(0)
    for k in range(FACES):
        at = matches[k] * (ranks[k] + k * SHARE - lanef)
        place = jnp.where((matches[k] > 0.5) & (jnp.abs(at) < 0.5), one, place)
        local = free_rank - (skipped * SHARE).astype(jnp.float32)
        inside = (local > -0.5) & (local < SHARE - 0.5) & (free > 0.5)
        inside = inside & jnp.logical_not(have[k])
        place = jnp.where(inside & (jnp.abs(local + k * SHARE - lanef) < 0.5), one, place)
        skipped = skipped + jnp.where(have[k], 0, 1)
    return place


def take(ref, at, rows, stride=1):
    half = ref.shape[0] // 2
    if stride == 1:
        if not isinstance(at, int):
            at = pl.multiple_of(at, ROWS)
        return ref[pl.ds(at, rows), :], ref[pl.ds(at + half, rows), :]
    return ref[pl.ds(at, rows, stride=stride), :], ref[pl.ds(at + half, rows, stride=stride), :]


def take_shifted(ref, at, rows, by):
    half = ref.shape[0] // 2
    return ref[pl.ds(at + by, rows), :], ref[pl.ds(at + by + half, rows), :]


def put(ref, at, i, value):
    if not isinstance(at, int):
        at = pl.multiple_of(at, ROWS)
    ref[pl.ds(at + i * (ref.shape[0] // 2), value.shape[0]), :] = value


def spread(ref, row):
    half = ref.shape[0] // 2
    return tuple(jnp.broadcast_to(ref[pl.ds(row + i * half, 1), :], (ROWS, LANES)) for i in range(2))


class Kept:
    def __init__(self, ref, base, cx, cy, slots):
        self.ref, self.cy, self.cells = ref, cy, cx * cy
        self.base = base
        self.near_base = base + self.cells + FACES * ROWS
        self.energy_base = self.near_base + FACES * self.cells
        self.slots_base = self.energy_base + slots * ROWS

    @staticmethod
    def rows(cells, slots):
        return cells + FACES * ROWS + FACES * cells + slots * ROWS + ROWS

    def rate(self, x):
        return take(self.ref, self.base + x * self.cy, self.cy)

    def rate_beside(self, k):
        return take(self.ref, self.base + self.cells + k * ROWS, ROWS)

    def near(self, k, x):
        return take(self.ref, self.near_base + k * self.cells + x * self.cy, self.cy)

    def energy(self, q):
        at = self.energy_base + q * ROWS
        return self.ref[pl.ds(at if isinstance(at, int) else pl.multiple_of(at, ROWS), ROWS), :]


def keep_on(out, out_base, kept, count):
    for i in range(2):
        put(out, out_base, i, take(kept.ref, kept.base, count)[i])


def fill(out, index, pair):
    out[index, :, :LANES], out[index, :, LANES:] = pair


def pair_faces(axis, low, high):
    even = lax.rem(lax.axis_index(axis), 2) == 0
    return even, (jnp.where(even, high, low), jnp.where(even, low, high))


def pack_faces(fields, energy, cx, cy, slots, out_refs, axis, columns):
    low, high = (LEFT, RIGHT) if columns else (BELOW, ABOVE)
    first, last, top, bottom = edges()
    _, faces = pair_faces(axis, low, high)
    for out, face in zip(out_refs, faces):

        def plane(q, depth):
            if columns:
                return take(fields, q * (cx * cy) + jnp.where(face == high, cy - 1 - depth, depth), cx, cy)
            return take(fields, q * (cx * cy) + jnp.where(face == high, cx - 1 - depth, depth) * cy, cy)

        squares = [None, None]
        for q in range(slots):
            for i, v in enumerate(plane(q, 0)):
                squares[i] = v * v if squares[i] is None else squares[i] + v * v
        for j in range(SHARE):
            q = face * SHARE + j
            centre, inner = plane(q, 0), plane(q, 1)
            near = along_height(centre[0], centre[1], first, last)
            e = energy(q)
            forces = []
            for i in range(2):
                n = near[i] + along_rows(centre[i], top, bottom, None, None) + inner[i]
                forces.append(force_of(centre[i], n, 2.0 * COUPLING * squares[i], e))
            fill(out, j, centre)
            fill(out, SHARE + j, forces)


def open_body(
    cx, cy, slots, slabs, cols, ids_hbm, rows_hbm, energy_hbm, fields_hbm, mask_hbm, coarse_hbm,
    fields, mask, slots_ref, energy_out, bounds, planes, msg_a, msg_b,
    ids_smem, rows_smem, energy_smem, ids_ref, coarse_ref, mask_ref, raw, sems,
):
    cells = cx * cy
    loads = [
        pltpu.make_async_copy(ids_hbm, ids_smem, sems.at[0]),
        pltpu.make_async_copy(ids_hbm, ids_ref, sems.at[1]),
        pltpu.make_async_copy(rows_hbm, rows_smem, sems.at[2]),
        pltpu.make_async_copy(coarse_hbm, coarse_ref, sems.at[3]),
        pltpu.make_async_copy(energy_hbm, energy_smem, sems.at[8]),
    ]
    for i in range(2):
        half = pl.ds(i * LANES, LANES)
        loads.append(
            pltpu.make_async_copy(mask_hbm.at[:, half], mask_ref.at[pl.ds(i * cells, cells), :], sems.at[4 + i])
        )
        rows = slots * cells
        loads.append(
            pltpu.make_async_copy(fields_hbm.at[:, half], raw.at[pl.ds(i * rows, rows), :], sems.at[6 + i])
        )
    for load in loads:
        load.start()
    for load in loads[:5]:
        load.wait()
    place = slot_places(slabs, cols, slots, ids_ref, ids_smem)
    sub = lax.broadcasted_iota(jnp.int32, (slots, LANES), 0).astype(jnp.float32)
    slot_row = jnp.sum(place * sub, axis=0, keepdims=True)
    slots_ref[...] = jnp.broadcast_to(slot_row, (ROWS, LANES))
    lane = lax.broadcasted_iota(jnp.int32, (1, LANES), 1)
    taken = [jnp.sum(jnp.where(lane == q, slot_row, 0.0)).astype(jnp.int32) for q in range(slots)]
    at_rows = lax.broadcasted_iota(jnp.int32, (slots, LANES), 0)
    own_energy = jnp.zeros((slots, LANES), jnp.float32)
    s, c = lax.axis_index("slab"), lax.axis_index("col")
    for q in range(slots):
        own_energy = jnp.where(at_rows == q, energy_smem[ids_smem[s, c, q]], own_energy)
    energy_row = jnp.sum(place * own_energy, axis=0, keepdims=True)
    for q in range(slots):
        value = jnp.sum(jnp.where(lane == q, energy_row, 0.0), axis=1, keepdims=True)
        energy_out[q * ROWS : (q + 1) * ROWS, :] = jnp.broadcast_to(value, (ROWS, LANES))

    start = jnp.int32(0)
    for t in range(slabs):
        start = start + jnp.where(t < s, rows_smem[t], 0)
    live = rows_smem[s]
    bounds[0:ROWS, :] = jnp.full((ROWS, LANES), start, jnp.int32)
    bounds[ROWS : 2 * ROWS, :] = jnp.full((ROWS, LANES), start + live, jnp.int32)
    capacity, coarse_y, _ = coarse_ref.shape
    chosen = [
        jnp.clip(plane - start, 0, capacity - 1) for plane in near_planes(cx, slabs)
    ] + [jnp.int32(0), jnp.int32(1), live - 2, live - 1]
    _, faces = pair_faces("col", LEFT, RIGHT)
    for out in (msg_a, msg_b):
        out[THERMAL] = jnp.zeros((ROWS, out.shape[2]), jnp.float32)
    planes[...] = jnp.zeros(planes.shape, jnp.float32)
    for i, p in enumerate(chosen):
        planes[i * ROWS + 1 : i * ROWS + 1 + coarse_y, :] = coarse_ref[p]
        for out, face in zip((msg_a, msg_b), faces):
            row = jnp.where(face == RIGHT, coarse_y - 1, 0)
            spot = slice(i // ROWS * LANES, (i // ROWS + 1) * LANES)
            out[THERMAL, i % ROWS : i % ROWS + 1, spot] = coarse_ref[p, pl.ds(row, 1), :]

    for load in loads[5:]:
        load.wait()
    mask[...] = mask_ref[...].astype(jnp.float32)

    for q in range(slots):
        for i, part in enumerate(take(raw, taken[q] * cells, cells)):
            put(fields, q * cells, i, part)
    energy_of = lambda q: energy_out[pl.ds(pl.multiple_of(q * ROWS, ROWS), ROWS), :]
    pack_faces(fields, energy_of, cx, cy, slots, (msg_a, msg_b), "col", True)
    for out, face in zip((msg_a, msg_b), faces):
        first = jnp.where(face == RIGHT, cy - 1, 0)
        fill(out, MASK, take(mask, first, cx, cy))


def near_planes(cx, slabs):
    s = lax.axis_index("slab")
    half = cx // 2
    return [jnp.clip(s * half - 1 + i, 0, slabs * half - 1) for i in range(half + 2)]


def faces_body(cx, cy, slots, fields, energy, mask, msg_a, msg_b):
    energy_of = lambda q: energy[pl.ds(pl.multiple_of(q * ROWS, ROWS), ROWS), :]
    pack_faces(fields, energy_of, cx, cy, slots, (msg_a, msg_b), "slab", False)
    _, faces = pair_faces("slab", BELOW, ABOVE)
    for out, face in zip((msg_a, msg_b), faces):
        first = jnp.where(face == ABOVE, cx - 1, 0) * cy
        fill(out, MASK, take(mask, first, cy))


def slab_body(cx, slabs, cols, coarse_y, own, got_a, got_b, msg_a, msg_b, planes):
    have = present(slabs, cols)
    even, _ = pair_faces("col", LEFT, RIGHT)
    from_a, from_b = got_a[THERMAL], got_b[THERMAL]
    lower = jnp.where(even, from_b, from_a)
    upper = jnp.where(even, from_a, from_b)
    sub = lax.broadcasted_iota(jnp.int32, (ROWS, LANES), 0)
    last = coarse_y + 1
    widened = []
    for i in range(cx // 2 + 6):
        plane = own[i * ROWS : (i + 1) * ROWS, :]
        spot = slice(i // ROWS * LANES, (i // ROWS + 1) * LANES)
        below = jnp.where(have[LEFT], lower[i % ROWS : i % ROWS + 1, spot], plane[1:2, :])
        above = jnp.where(have[RIGHT], upper[i % ROWS : i % ROWS + 1, spot], plane[coarse_y : coarse_y + 1, :])
        plane = jnp.where(sub == 0, below, jnp.where(sub == last, above, plane))
        widened.append(plane)
        if i < cx // 2 + 2:
            planes[i * ROWS : (i + 1) * ROWS, :] = plane
    first = cx // 2 + 2
    _, faces = pair_faces("slab", BELOW, ABOVE)
    for out, face in zip((msg_a, msg_b), faces):
        for i in range(2):
            plane = jnp.where(face == ABOVE, widened[first + 2 + i], widened[first + i])
            out[:, i * LANES : (i + 1) * LANES] = plane


def axis_weights(cells):
    fine = np.arange(-1, cells + 1)
    lower = (2 * fine - 1) // 4
    weight = (2 * fine - 1 - 4 * lower) / 4.0
    out = np.zeros((cells + 2, cells // 2 + 2), np.float32)
    out[np.arange(cells + 2), lower + 1] += 1.0 - weight
    out[np.arange(cells + 2), lower + 2] += weight
    return out


def plane_weights(cx, cy):
    along, across = axis_weights(cx), axis_weights(cy)
    inner = [(x + 1, y + 1) for x in range(cx) for y in range(cy)]
    inner += [(0, y + 1) for y in range(cy)] + [(cx + 1, y + 1) for y in range(cy)]
    inner += [(x + 1, 0) for x in range(cx)] + [(x + 1, cy + 1) for x in range(cx)]
    out = np.zeros((len(inner), cx // 2 + 2, ROWS), np.float32)
    for row, (x, y) in enumerate(inner):
        out[row, :, : cy // 2 + 2] = along[x][:, None] * across[y][None, :]
    return out.reshape(len(inner), -1)


def height_weights(cells, coarse):
    fine = np.arange(cells)
    lower = (2 * fine - 1) // 4
    weight = (2 * fine - 1 - 4 * lower) / 4.0
    out = np.zeros((coarse, cells), np.float32)
    np.add.at(out, (np.clip(lower, 0, coarse - 1), fine), 1.0 - weight)
    np.add.at(out, (np.clip(lower + 1, 0, coarse - 1), fine), weight)
    return out


def mobility_body(
    cx, cy, slots, slabs, cols, planes, bounds, mask_ref, weights, height, energy, slots_ref,
    col_a, col_b, slab_a, slab_b, ends_a, ends_b, keep, near,
):
    start, end = bounds[0:ROWS, :], bounds[ROWS : 2 * ROWS, :]
    even_s, _ = pair_faces("slab", BELOW, ABOVE)
    even_c, _ = pair_faces("col", LEFT, RIGHT)
    mask = MASK
    below = jnp.where(even_s, ends_b[...], ends_a[...])
    above = jnp.where(even_s, ends_a[...], ends_b[...])
    for i, p in enumerate(near_planes(cx, slabs)):
        p = jnp.full((ROWS, LANES), p, jnp.int32)
        own = planes[i * ROWS : (i + 1) * ROWS, :]
        lower = jnp.where(p == start - 2, below[:, :LANES], below[:, LANES:])
        upper = jnp.where(p == end, above[:, :LANES], above[:, LANES:])
        near[i * ROWS : (i + 1) * ROWS, :] = jnp.where(p < start, lower, jnp.where(p < end, own, upper))
    flat = jnp.dot(weights[...], near[...], precision=HIGHEST, preferred_element_type=jnp.float32)
    profile = jnp.dot(flat, height[...], precision=HIGHEST, preferred_element_type=jnp.float32)
    mobility = jnp.exp(2.0 * (profile - 1.0)) * TIME_STEP
    cells = cx * cy
    kept = Kept(keep, 0, cx, cy, slots)
    for i, part in enumerate(take(mask_ref, 0, cells)):
        put(keep, 0, i, part * mobility[:cells, i * LANES : (i + 1) * LANES])
    have = present(slabs, cols)
    masks = (
        jnp.where(even_s, slab_b[mask], slab_a[mask]),
        jnp.where(even_s, slab_a[mask], slab_b[mask]),
        jnp.where(even_c, col_b[mask], col_a[mask]),
        jnp.where(even_c, col_a[mask], col_b[mask]),
    )
    for k in range(FACES):
        at = cells + k * ROWS
        for i, part in enumerate(split(jnp.where(have[k], masks[k] * mobility[at : at + ROWS], 0.0))):
            put(keep, at, i, part)
    for i in range(2):
        put(keep, kept.energy_base, i, energy[...])
        put(keep, kept.slots_base, i, slots_ref[...])
    marks = edges()
    top, bottom = marks[2:]
    for x in range(cx):
        sums = neighbours(x, cx - 1, kept.rate, kept.rate(x), None, None, marks)
        extra = [None] * FACES
        if x == 0:
            extra[BELOW] = kept.rate_beside(BELOW)
        if x == cx - 1:
            extra[ABOVE] = kept.rate_beside(ABOVE)
        extra[LEFT] = [jnp.where(top, v, 0.0) for v in spread(keep, cells + LEFT * ROWS + x)]
        extra[RIGHT] = [jnp.where(bottom, v, 0.0) for v in spread(keep, cells + RIGHT * ROWS + x)]
        for k in range(FACES):
            for i in range(2):
                value = sums[i] if extra[k] is None else sums[i] + extra[k][i]
                put(keep, kept.near_base + k * cells + x * cy, i, value)


def split(value):
    return value[:, :LANES], value[:, LANES:]


def along_height(v0, v1, first, last):
    r0, r1 = pltpu.roll(v0, 1, 1), pltpu.roll(v1, 1, 1)
    q0, q1 = pltpu.roll(v0, LANES - 1, 1), pltpu.roll(v1, LANES - 1, 1)
    return (
        jnp.where(first, 0.0, r0) + jnp.where(last, q1, q0),
        jnp.where(first, r0, r1) + jnp.where(last, 0.0, q1),
    )


def along_rows(v, top, bottom, lower, upper, shifted=None):
    before, after = shifted or (pltpu.roll(v, 1, 0), pltpu.roll(v, ROWS - 1, 0))
    down = jnp.where(top, 0.0 if lower is None else lower, before)
    up = jnp.where(bottom, 0.0 if upper is None else upper, after)
    return down + up


def edges():
    lane = lax.broadcasted_iota(jnp.int32, (ROWS, LANES), 1)
    row = lax.broadcasted_iota(jnp.int32, (ROWS, LANES), 0)
    return lane == 0, lane == LANES - 1, row == 0, row == ROWS - 1


def neighbours(x, last_x, load, centre, halo, kind, marks, shift=None):
    first, last, top, bottom = marks
    v0, v1 = centre
    n0, n1 = along_height(v0, v1, first, last)
    low = high = (None, None)
    if kind == LEFT:
        low = halo(x)
    if kind == RIGHT:
        high = halo(x)
    shifted = (None, None)
    if shift is not None and 0 < x < last_x:
        before, after = shift(x, -1), shift(x, 1)
        shifted = tuple(zip(before, after))
    n0 = n0 + along_rows(v0, top, bottom, low[0], high[0], shifted[0])
    n1 = n1 + along_rows(v1, top, bottom, low[1], high[1], shifted[1])
    sides = []
    if not (isinstance(x, int) and x == 0):
        sides.append(load(x - 1))
    elif kind == BELOW:
        sides.append(halo(None))
    if not (isinstance(x, int) and x == last_x):
        sides.append(load(x + 1))
    elif kind == ABOVE:
        sides.append(halo(None))
    for a, b in sides:
        n0, n1 = n0 + a, n1 + b
    return n0, n1


def over_planes(cx, visit, carry):
    carry = visit(0, carry)
    carry = lax.fori_loop(1, cx - 1, visit, carry)
    return visit(cx - 1, carry)


def slot_access(fields, halos, base, q, cells, cy):
    def load(x):
        return take(fields, q * cells + x * cy, cy)

    def halo(x):
        if x is None:
            return take(halos, base + q * ROWS, ROWS)
        return spread(halos, base + q * ROWS + x)

    return load, halo


def force_of(v, n, squares3, energy):
    return v * (squares3 + ((5.0 - energy) + v * (energy - 2.0 * v))) - n


def triple_squares(fields, x, slots, cells, cy):
    total = None
    for q in range(slots):
        v0, v1 = take(fields, q * cells + x * cy, cy)
        total = (v0 * v0, v1 * v1) if total is None else (total[0] + v0 * v0, total[1] + v1 * v1)
    return 2.0 * COUPLING * total[0], 2.0 * COUPLING * total[1]


def inner_body(cx, cy, slots, base, *refs):
    fields, force_out = refs[0], refs[-1]
    cells = cx * cy
    marks = edges()
    if base is None:
        energy = lambda q: refs[1][q * ROWS : (q + 1) * ROWS, :]
    else:
        energy = Kept(fields, base, cx, cy, slots).energy

    def visit(x, carry):
        squares = triple_squares(fields, x, slots, cells, cy)
        for q in range(slots):
            load, _ = slot_access(fields, None, None, q, cells, cy)
            centre = load(x)
            shift = lambda y, by: take_shifted(fields, q * cells + y * cy, cy, by)
            near = neighbours(x, cx - 1, load, centre, None, None, marks, shift)
            e = energy(q)
            for i in range(2):
                put(force_out, q * cells + x * cy, i, force_of(centre[i], near[i], squares[i], e))
        return carry

    for x in range(cx):
        visit(x, 0)


def arrivals(col_a, col_b, slab_a, slab_b):
    even_s, _ = pair_faces("slab", BELOW, ABOVE)
    even_c, _ = pair_faces("col", LEFT, RIGHT)
    pairs = ((slab_b, slab_a, even_s), (slab_a, slab_b, even_s), (col_b, col_a, even_c), (col_a, col_b, even_c))
    return [functools.partial(lambda u, v, even, i: jnp.where(even, u[i], v[i]), *pair) for pair in pairs]


class Grown:
    def __init__(self, cx, cy, slots):
        self.cells = cx * cy
        self.sum = slots * self.cells
        self.squares = self.sum + self.cells
        self.halos = self.squares + self.cells
        self.kept = self.halos + slots * ROWS
        self.count = Kept.rows(self.cells, slots)
        self.rows = self.kept + self.count


def sums_body(
    cx, cy, slots, slabs, cols, devices, base, fields, keep, force_in, col_a, col_b, slab_a, slab_b,
    grown, sums_ref, halos,
):
    cells = cx * cy
    _, _, top, bottom = edges()
    have = present(slabs, cols)
    kept = Kept(keep, base, cx, cy, slots)
    layout = Grown(cx, cy, slots)
    keep_on(grown, layout.kept, kept, layout.count)
    for k, pick in enumerate(arrivals(col_a, col_b, slab_a, slab_b)):
        rate = kept.rate_beside(k)
        for j in range(SHARE):
            q = k * SHARE + j
            if k == BELOW:
                own = take(fields, q * cells, cy)
            elif k == ABOVE:
                own = take(fields, (q + 1) * cells - cy, cy)
            elif k == LEFT:
                own = take(fields, q * cells, cx, cy)
            else:
                own = take(fields, q * cells + cy - 1, cx, cy)
            beside, force = split(jnp.where(have[k], pick(j), 0.0)), split(pick(SHARE + j))
            for i in range(2):
                put(halos, q * ROWS, i, beside[i])
                put(grown, layout.halos + q * ROWS, i, beside[i] - rate[i] * (force[i] - own[i]))

    energy_sum = None
    for q in range(slots):
        energy_sum = kept.energy(q) if energy_sum is None else energy_sum + kept.energy(q)
    zero = jnp.zeros((ROWS, LANES), jnp.float32)

    def visit(x, carry):
        total, c0, c1, c2, c3, weight = carry
        rate = kept.rate(x)
        forces, powers = [zero, zero], [zero, zero]
        a2, b1 = [zero, zero], [zero, zero]
        a1 = [[zero, zero] for _ in range(FACES)]
        for q in range(slots):
            k = q // SHARE
            centre = take(fields, q * cells + x * cy, cy)
            inner = take(force_in, q * cells + x * cy, cy)
            e = kept.energy(q)
            cross = (None, None)
            if k in (LEFT, RIGHT):
                row = spread(halos, q * ROWS + x)
                cross = [jnp.where(top if k == LEFT else bottom, row[i], 0.0) for i in range(2)]
            elif isinstance(x, int) and (k, x) in ((BELOW, 0), (ABOVE, cx - 1)):
                cross = take(halos, q * ROWS, ROWS)
            for i in range(2):
                force = inner[i] if cross[i] is None else inner[i] - cross[i]
                g = centre[i] - rate[i] * force
                put(grown, q * cells + x * cy, i, g)
                weighted, square = e * g, g * g
                forces[i] = forces[i] + force
                powers[i] = powers[i] + g * (weighted - (square + square))
                a1[k][i] = a1[k][i] + g
                a2[i] = a2[i] + square
                b1[i] = b1[i] + weighted
        beside = [kept.near(k, x) for k in range(FACES)]
        for i in range(2):
            h = rate[i]
            whole = (a1[0][i] + a1[1][i]) + (a1[2][i] + a1[3][i])
            near = [beside[k][i] for k in range(FACES)]
            put(grown, layout.sum + x * cy, i, whole)
            put(grown, layout.squares + x * cy, i, a2[i])
            total = total + h * forces[i]
            c0 = c0 + h * (powers[i] + 5.0 * whole - b1[i] + 2.0 * COUPLING * whole * a2[i])
            for k in range(FACES):
                c0 = c0 - a1[k][i] * near[k]
            linear = (
                energy_sum
                - 5.0 * slots
                - 2.0 * b1[i]
                + (6.0 - 2.0 * COUPLING * slots) * a2[i]
                - 4.0 * COUPLING * (whole * whole)
            )
            c1 = c1 + h * (h * linear + float(SHARE) * ((near[0] + near[1]) + (near[2] + near[3])))
            c2 = c2 + h * h * h * (energy_sum + (6.0 * COUPLING * slots - 6.0) * whole)
            c3 = c3 + (h * h) * (h * h)
            weight = weight + h
        return total, c0, c1, c2, c3, weight

    parts = over_planes(cx, visit, (zero,) * 6)
    back = -1.0 / TIME_STEP
    scales = (back, back, back, back, back * (2.0 * slots - 2.0 * COUPLING * slots * slots), 1.0 / TIME_STEP)
    lane = lax.broadcasted_iota(jnp.int32, (1, LANES), 1)
    row = jnp.zeros((1, LANES), jnp.float32)
    for i, (part, scale) in enumerate(zip(parts, scales)):
        value = jnp.sum(jnp.sum(part, axis=0, keepdims=True), axis=1, keepdims=True) * scale
        row = jnp.where(lane == i, value, row)
    sums_ref[...] = jnp.broadcast_to(row[None], (devices, 1, LANES))


def multipliers(got, slots):
    total = jnp.sum(got[...], axis=0)
    lane = lax.broadcasted_iota(jnp.int32, (1, LANES), 1)
    part = [jnp.sum(jnp.where(lane == i, total, 0.0), axis=1, keepdims=True) for i in range(6)]
    whole = slots * part[5]
    here = part[0] / whole
    later = (part[1] + here * (part[2] + here * (part[3] + here * part[4]))) / whole
    return jnp.broadcast_to(here, (ROWS, LANES)), jnp.broadcast_to(later, (ROWS, LANES))


def settle(cx, cy, slots, got, grown, store, done=None):
    cells = cx * cy
    marks = edges()
    here, later = multipliers(got, slots)
    layout = Grown(cx, cy, slots)
    kept = Kept(grown, layout.kept, cx, cy, slots)
    for k in range(FACES):

        def visit(x, carry):
            rate = kept.rate(x)
            near = kept.near(k, x)
            a1 = take(grown, layout.sum + x * cy, cy)
            a2 = take(grown, layout.squares + x * cy, cy)
            off = [here * rate[i] for i in range(2)]
            base = [
                5.0 + 2.0 * COUPLING * (a2[i] - off[i] * (2.0 * a1[i] - float(slots) * off[i])) for i in range(2)
            ]
            extra = [here * near[i] + later for i in range(2)]
            for q in range(k * SHARE, (k + 1) * SHARE):
                e = kept.energy(q)
                load, halo = slot_access(grown, grown, layout.halos, q, cells, cy)
                shift = lambda y, by: take_shifted(grown, q * cells + y * cy, cy, by)
                g = load(x)
                n = neighbours(x, cx - 1, load, g, halo, k, marks, shift)
                for i in range(2):
                    f = g[i] - off[i]
                    force = f * ((base[i] - e) + f * (e - (f + f))) - (n[i] - extra[i])
                    store(q, x, i, f - rate[i] * force)
            return carry

        for x in range(cx):
            visit(x, 0)
        if done is not None:
            done(k)


def middle_body(cx, cy, slots, got, grown, fields, slab_a, slab_b):
    def store(q, x, i, value):
        put(fields, q * cx * cy + x * cy, i, value)

    settle(cx, cy, slots, got, grown, store)
    layout = Grown(cx, cy, slots)
    keep_on(fields, slots * cx * cy, Kept(grown, layout.kept, cx, cy, slots), layout.count)
    energy = Kept(fields, slots * cx * cy, cx, cy, slots).energy
    pack_faces(fields, energy, cx, cy, slots, (slab_a, slab_b), "slab", False)


def cols_body(cx, cy, slots, fields, col_a, col_b):
    energy = Kept(fields, slots * cx * cy, cx, cy, slots).energy
    pack_faces(fields, energy, cx, cy, slots, (col_a, col_b), "col", True)


def last_body(cx, cy, slots, got, grown, out, result, order, sems, order_sem):
    kept = Kept(grown, Grown(cx, cy, slots).kept, cx, cy, slots)
    fetch = pltpu.make_async_copy(grown.at[pl.ds(kept.slots_base, ROWS), :], order, order_sem)
    fetch.start()

    def store(q, x, i, value):
        at = x * cy if isinstance(x, int) else pl.multiple_of(x * cy, ROWS)
        result[q, pl.ds(at, cy), i * LANES : (i + 1) * LANES] = value

    def send(q):
        return pltpu.make_async_copy(result.at[q], out.at[order[0, q].astype(jnp.int32)], sems.at[q])

    def done(k):
        if k == 0:
            fetch.wait()
        for q in range(k * SHARE, (k + 1) * SHARE):
            send(q).start()

    settle(cx, cy, slots, got, grown, store, done)
    for q in range(slots):
        send(q).wait()


def exchange_cols(first, second):
    count = lax.axis_size("col")
    one = [(i, i ^ 1) for i in range(count)]
    two = [(i, (i - 1) % count if i % 2 == 0 else (i + 1) % count) for i in range(count)]
    return lax.ppermute(first, "col", one), lax.ppermute(second, "col", two)


def exchange_slabs(first, second):
    count, cols = lax.axis_size("slab"), lax.axis_size("col")
    one = [(i, i ^ 1) for i in range(count)]
    two = []
    for s in range(count):
        other = s - 1 if s % 2 == 0 else s + 1
        for c in range(cols):
            target = other * cols + c if 0 <= other < count else s * cols + (c ^ 1)
            two.append((s * cols + c, target))
    return lax.ppermute(second, ("slab", "col"), two), lax.ppermute(first, "slab", one)


def per_device(order_params, layer_mask, coarse_temp, coarse_rows, grain_ids, energy):
    slots, cx, cy, cz = order_params.shape
    slabs, cols = lax.axis_size("slab"), lax.axis_size("col")
    devices = slabs * cols
    cells = cx * cy
    capacity, _, coarse_z = coarse_temp.shape
    raw = order_params.reshape(slots * cells, cz)
    mask = layer_mask.reshape(cells, cz)
    message = f32(THERMAL + 1, ROWS, cz)
    short = f32(2 * SHARE, ROWS, cz)
    state = f32(2 * slots * cells, cz // 2)

    hbm = lambda x: pltpu.with_memory_space_constraint(x, pltpu.HBM)
    near = cx // 2 + 2
    fields, mask, slot_order, slot_energy, bounds, planes, col_a, col_b = call(
        functools.partial(open_body, cx, cy, slots, slabs, cols),
        (
            state,
            f32(2 * cells, LANES),
            f32(ROWS, LANES),
            f32(slots * ROWS, LANES),
            jax.ShapeDtypeStruct((2 * ROWS, LANES), jnp.int32),
            f32((near + 4) * ROWS, LANES),
            message,
            message,
        ),
        [HBM] * 6,
        (VMEM,) * 8,
        [
            pltpu.SMEM(grain_ids.shape, jnp.int32),
            pltpu.SMEM(coarse_rows.shape, jnp.int32),
            pltpu.SMEM(energy.shape, jnp.float32),
            pltpu.VMEM(grain_ids.shape, jnp.int32),
            pltpu.VMEM(coarse_temp.shape, jnp.float32),
            pltpu.VMEM((2 * cells, LANES), jnp.int32),
            pltpu.VMEM(state.shape, jnp.float32),
            pltpu.SemaphoreType.DMA((9,)),
        ],
    )(hbm(grain_ids), hbm(coarse_rows), hbm(energy), hbm(raw), hbm(mask), hbm(coarse_temp))
    col_a, col_b = exchange_cols(col_a, col_b)
    slab_a, slab_b = call(
        functools.partial(faces_body, cx, cy, slots),
        (f32(THERMAL, ROWS, cz),) * 2,
        [VMEM] * 3,
        (VMEM,) * 2,
    )(fields, slot_energy, mask)
    slab_b, slab_a = exchange_slabs(slab_a, slab_b)
    ends_a, ends_b, planes = call(
        functools.partial(slab_body, cx, slabs, cols, coarse_temp.shape[1]),
        (f32(ROWS, cz), f32(ROWS, cz), f32(near * ROWS, LANES)),
        [VMEM] * 3,
        (VMEM,) * 3,
    )(planes, col_a, col_b)
    ends_b, ends_a = exchange_slabs(ends_a, ends_b)
    weights = jnp.asarray(plane_weights(cx, cy))
    height = jnp.asarray(height_weights(cz, coarse_z))
    count = Kept.rows(cells, slots)
    keep = call(
        functools.partial(mobility_body, cx, cy, slots, slabs, cols),
        f32(2 * count, LANES),
        [VMEM] * 13,
        VMEM,
        [pltpu.VMEM((near * ROWS, LANES), jnp.float32)],
    )(planes, bounds, mask, weights, height, slot_energy, slot_order, col_a, col_b, slab_a, slab_b, ends_a, ends_b)

    for pair in range(STEPS // 2):
        base = None if pair == 0 else slots * cells
        inputs = (fields, slot_energy) if pair == 0 else (fields,)
        force = call(
            functools.partial(inner_body, cx, cy, slots, base),
            state,
            [VMEM] * len(inputs),
            VMEM,
            flops=1 << 23,
            size=1 << 22,
        )(*inputs)
        grown, sums = call(
            functools.partial(sums_body, cx, cy, slots, slabs, cols, devices, base or 0),
            (f32(2 * Grown(cx, cy, slots).rows, LANES), f32(devices, 1, LANES)),
            [VMEM] * 7,
            (VMEM,) * 2,
            [pltpu.VMEM((2 * slots * ROWS, LANES), jnp.float32)],
        )(fields, keep if pair == 0 else fields, force, col_a, col_b, slab_a, slab_b)
        got = lax.all_to_all(sums, ("slab", "col"), 0, 0)
        if pair < STEPS // 2 - 1:
            fields, slab_a, slab_b = call(
                functools.partial(middle_body, cx, cy, slots),
                (f32(2 * (slots * cells + count), LANES), short, short),
                [VMEM] * 2,
                (VMEM,) * 3,
            )(got, grown)
            col_a, col_b = call(
                functools.partial(cols_body, cx, cy, slots), (short, short), [VMEM], (VMEM,) * 2
            )(fields)
            slab_b, slab_a = exchange_slabs(slab_a, slab_b)
            col_a, col_b = exchange_cols(col_a, col_b)
        else:
            fields = call(
                functools.partial(last_body, cx, cy, slots),
                f32(slots, cells, cz),
                [VMEM] * 2,
                HBM,
                [
                    pltpu.VMEM((slots, cells, cz), jnp.float32),
                    pltpu.SMEM((ROWS, LANES), jnp.float32),
                    pltpu.SemaphoreType.DMA((slots,)),
                    pltpu.SemaphoreType.DMA(()),
                ],
            )(got, grown)
    return fields.reshape(order_params.shape)


def solution(mesh):
    in_specs = (
        P(None, "slab", "col", None),
        P("slab", "col", None),
        P("slab", "col", None),
        P(),
        P(),
        P(),
    )
    out_specs = P(None, "slab", "col", None)
    return jax.shard_map(
        per_device, mesh=mesh, in_specs=in_specs, out_specs=out_specs, check_vma=False
    )
```

```python
import functools

import jax
import jax.numpy as jnp
import numpy as np
from jax import lax
from jax.experimental import pallas as pl
from jax.experimental.pallas import tpu as pltpu
from jax.sharding import PartitionSpec as P

SHARE = 4
STEPS = 4
TIME_STEP = 0.05
COUPLING = 1.5
BELOW, ABOVE, LEFT, RIGHT = range(4)
FACES = 4
MASK = 2 * SHARE
THERMAL = MASK + 1
LANES = 128
ROWS = 8
HIGHEST = lax.Precision.HIGHEST

VMEM = pl.BlockSpec(memory_space=pltpu.VMEM)
SMEM = pl.BlockSpec(memory_space=pltpu.SMEM)
HBM = pl.BlockSpec(memory_space=pltpu.HBM)


def call(body, out_shape, in_specs, out_specs, scratch=(), flops=1 << 20, size=1 << 20):
    return pl.pallas_call(
        body,
        out_shape=out_shape,
        in_specs=in_specs,
        out_specs=out_specs,
        scratch_shapes=list(scratch),
        compiler_params=pltpu.CompilerParams(vmem_limit_bytes=20 << 20),
        cost_estimate=pl.CostEstimate(flops=flops, bytes_accessed=size, transcendentals=0),
    )


def f32(*shape):
    return jax.ShapeDtypeStruct(shape, jnp.float32)


def present(slabs, cols):
    s, c = lax.axis_index("slab"), lax.axis_index("col")
    return (s > 0, s < slabs - 1, c > 0, c < cols - 1)


def beside(slabs, cols):
    s, c = lax.axis_index("slab"), lax.axis_index("col")
    return (
        (jnp.maximum(s - 1, 0), c),
        (jnp.minimum(s + 1, slabs - 1), c),
        (s, jnp.maximum(c - 1, 0)),
        (s, jnp.minimum(c + 1, cols - 1)),
    )


def slot_places(slabs, cols, slots, ids_ref, ids_smem):
    s, c = lax.axis_index("slab"), lax.axis_index("col")
    sub = lax.broadcasted_iota(jnp.int32, (slots, LANES), 0)
    lane = lax.broadcasted_iota(jnp.int32, (slots, LANES), 1)
    own = jnp.zeros((slots, LANES), jnp.int32)
    for q in range(slots):
        own = jnp.where(sub == q, ids_smem[s, c, q], own)
    one, zero = jnp.float32(1.0), jnp.float32(0.0)
    have = present(slabs, cols)
    matches, ranks = [], []
    for k, (ns, nc) in enumerate(beside(slabs, cols)):
        row = ids_ref[ns, pl.ds(nc, 1), :]
        row = jnp.concatenate([row, jnp.full((1, LANES - slots), -1, jnp.int32)], axis=1)
        row = jnp.broadcast_to(jnp.where(have[k], row, -1), (slots, LANES))
        hit = jnp.where((own == row) & (row >= 0), one, zero)
        shared = jnp.max(hit, axis=0, keepdims=True)
        matches.append(jnp.sum(hit, axis=1, keepdims=True))
        ranks.append(jnp.sum(jnp.where(row < own, shared, zero), axis=1, keepdims=True))
    free = one - (matches[0] + matches[1] + matches[2] + matches[3])
    lanef = lane.astype(jnp.float32)
    free_row = jnp.sum(jnp.where(sub == lane, free, zero), axis=0, keepdims=True)
    free_rank = jnp.sum(jnp.where(lane < sub, free_row, zero), axis=1, keepdims=True)
    place = jnp.zeros((slots, LANES), jnp.float32)
    skipped = jnp.int32(0)
    for k in range(FACES):
        at = matches[k] * (ranks[k] + k * SHARE - lanef)
        place = jnp.where((matches[k] > 0.5) & (jnp.abs(at) < 0.5), one, place)
        local = free_rank - (skipped * SHARE).astype(jnp.float32)
        inside = (local > -0.5) & (local < SHARE - 0.5) & (free > 0.5)
        inside = inside & jnp.logical_not(have[k])
        place = jnp.where(inside & (jnp.abs(local + k * SHARE - lanef) < 0.5), one, place)
        skipped = skipped + jnp.where(have[k], 0, 1)
    return place


def take(ref, at, rows, stride=1):
    half = ref.shape[0] // 2
    if stride == 1:
        if not isinstance(at, int):
            at = pl.multiple_of(at, ROWS)
        return ref[pl.ds(at, rows), :], ref[pl.ds(at + half, rows), :]
    return ref[pl.ds(at, rows, stride=stride), :], ref[pl.ds(at + half, rows, stride=stride), :]


def take_shifted(ref, at, rows, by):
    half = ref.shape[0] // 2
    return ref[pl.ds(at + by, rows), :], ref[pl.ds(at + by + half, rows), :]


def put(ref, at, i, value):
    if not isinstance(at, int):
        at = pl.multiple_of(at, ROWS)
    ref[pl.ds(at + i * (ref.shape[0] // 2), value.shape[0]), :] = value


def spread(ref, row):
    half = ref.shape[0] // 2
    return tuple(jnp.broadcast_to(ref[pl.ds(row + i * half, 1), :], (ROWS, LANES)) for i in range(2))


class Kept:
    def __init__(self, ref, base, cx, cy, slots):
        self.ref, self.cy, self.cells = ref, cy, cx * cy
        self.base = base
        self.near_base = base + self.cells + FACES * ROWS
        self.energy_base = self.near_base + FACES * self.cells
        self.slots_base = self.energy_base + slots * ROWS

    @staticmethod
    def rows(cells, slots):
        return cells + FACES * ROWS + FACES * cells + slots * ROWS + ROWS

    def rate(self, x):
        return take(self.ref, self.base + x * self.cy, self.cy)

    def rate_beside(self, k):
        return take(self.ref, self.base + self.cells + k * ROWS, ROWS)

    def near(self, k, x):
        return take(self.ref, self.near_base + k * self.cells + x * self.cy, self.cy)

    def energy(self, q):
        at = self.energy_base + q * ROWS
        return self.ref[pl.ds(at if isinstance(at, int) else pl.multiple_of(at, ROWS), ROWS), :]


def keep_on(out, out_base, kept, count):
    for i in range(2):
        put(out, out_base, i, take(kept.ref, kept.base, count)[i])


def fill(out, index, pair):
    out[index, :, :LANES], out[index, :, LANES:] = pair


def pair_faces(axis, low, high):
    even = lax.rem(lax.axis_index(axis), 2) == 0
    return even, (jnp.where(even, high, low), jnp.where(even, low, high))


def pack_faces(fields, energy, cx, cy, slots, out_refs, axis, columns):
    low, high = (LEFT, RIGHT) if columns else (BELOW, ABOVE)
    first, last, top, bottom = edges()
    _, faces = pair_faces(axis, low, high)
    for out, face in zip(out_refs, faces):

        def plane(q, depth):
            if columns:
                return take(fields, q * (cx * cy) + jnp.where(face == high, cy - 1 - depth, depth), cx, cy)
            return take(fields, q * (cx * cy) + jnp.where(face == high, cx - 1 - depth, depth) * cy, cy)

        squares = [None, None]
        for q in range(slots):
            for i, v in enumerate(plane(q, 0)):
                squares[i] = v * v if squares[i] is None else squares[i] + v * v
        for j in range(SHARE):
            q = face * SHARE + j
            centre, inner = plane(q, 0), plane(q, 1)
            near = along_height(centre[0], centre[1], first, last)
            e = energy(q)
            forces = []
            for i in range(2):
                n = near[i] + along_rows(centre[i], top, bottom, None, None) + inner[i]
                forces.append(force_of(centre[i], n, 2.0 * COUPLING * squares[i], e))
            fill(out, j, centre)
            fill(out, SHARE + j, forces)


def open_body(
    cx, cy, slots, slabs, cols, ids_hbm, rows_hbm, energy_hbm, fields_hbm, mask_hbm, coarse_hbm,
    fields, mask, slots_ref, energy_out, bounds, planes, msg_a, msg_b,
    ids_smem, rows_smem, energy_smem, ids_ref, coarse_ref, mask_ref, raw, sems,
):
    cells = cx * cy
    loads = [
        pltpu.make_async_copy(ids_hbm, ids_smem, sems.at[0]),
        pltpu.make_async_copy(ids_hbm, ids_ref, sems.at[1]),
        pltpu.make_async_copy(rows_hbm, rows_smem, sems.at[2]),
        pltpu.make_async_copy(coarse_hbm, coarse_ref, sems.at[3]),
        pltpu.make_async_copy(energy_hbm, energy_smem, sems.at[8]),
    ]
    for i in range(2):
        half = pl.ds(i * LANES, LANES)
        loads.append(
            pltpu.make_async_copy(mask_hbm.at[:, half], mask_ref.at[pl.ds(i * cells, cells), :], sems.at[4 + i])
        )
        rows = slots * cells
        loads.append(
            pltpu.make_async_copy(fields_hbm.at[:, half], raw.at[pl.ds(i * rows, rows), :], sems.at[6 + i])
        )
    for load in loads:
        load.start()
    for load in loads[:5]:
        load.wait()
    place = slot_places(slabs, cols, slots, ids_ref, ids_smem)
    sub = lax.broadcasted_iota(jnp.int32, (slots, LANES), 0).astype(jnp.float32)
    slot_row = jnp.sum(place * sub, axis=0, keepdims=True)
    slots_ref[...] = jnp.broadcast_to(slot_row, (ROWS, LANES))
    lane = lax.broadcasted_iota(jnp.int32, (1, LANES), 1)
    taken = [jnp.sum(jnp.where(lane == q, slot_row, 0.0)).astype(jnp.int32) for q in range(slots)]
    at_rows = lax.broadcasted_iota(jnp.int32, (slots, LANES), 0)
    own_energy = jnp.zeros((slots, LANES), jnp.float32)
    s, c = lax.axis_index("slab"), lax.axis_index("col")
    for q in range(slots):
        own_energy = jnp.where(at_rows == q, energy_smem[ids_smem[s, c, q]], own_energy)
    energy_row = jnp.sum(place * own_energy, axis=0, keepdims=True)
    for q in range(slots):
        value = jnp.sum(jnp.where(lane == q, energy_row, 0.0), axis=1, keepdims=True)
        energy_out[q * ROWS : (q + 1) * ROWS, :] = jnp.broadcast_to(value, (ROWS, LANES))

    start = jnp.int32(0)
    for t in range(slabs):
        start = start + jnp.where(t < s, rows_smem[t], 0)
    live = rows_smem[s]
    bounds[0:ROWS, :] = jnp.full((ROWS, LANES), start, jnp.int32)
    bounds[ROWS : 2 * ROWS, :] = jnp.full((ROWS, LANES), start + live, jnp.int32)
    capacity, coarse_y, _ = coarse_ref.shape
    chosen = [
        jnp.clip(plane - start, 0, capacity - 1) for plane in near_planes(cx, slabs)
    ] + [jnp.int32(0), jnp.int32(1), live - 2, live - 1]
    _, faces = pair_faces("col", LEFT, RIGHT)
    for out in (msg_a, msg_b):
        out[THERMAL] = jnp.zeros((ROWS, out.shape[2]), jnp.float32)
    planes[...] = jnp.zeros(planes.shape, jnp.float32)
    for i, p in enumerate(chosen):
        planes[i * ROWS + 1 : i * ROWS + 1 + coarse_y, :] = coarse_ref[p]
        for out, face in zip((msg_a, msg_b), faces):
            row = jnp.where(face == RIGHT, coarse_y - 1, 0)
            spot = slice(i // ROWS * LANES, (i // ROWS + 1) * LANES)
            out[THERMAL, i % ROWS : i % ROWS + 1, spot] = coarse_ref[p, pl.ds(row, 1), :]

    for load in loads[5:]:
        load.wait()
    mask[...] = mask_ref[...].astype(jnp.float32)

    for q in range(slots):
        for i, part in enumerate(take(raw, taken[q] * cells, cells)):
            put(fields, q * cells, i, part)
    energy_of = lambda q: energy_out[pl.ds(pl.multiple_of(q * ROWS, ROWS), ROWS), :]
    pack_faces(fields, energy_of, cx, cy, slots, (msg_a, msg_b), "col", True)
    for out, face in zip((msg_a, msg_b), faces):
        first = jnp.where(face == RIGHT, cy - 1, 0)
        fill(out, MASK, take(mask, first, cx, cy))


def near_planes(cx, slabs):
    s = lax.axis_index("slab")
    half = cx // 2
    return [jnp.clip(s * half - 1 + i, 0, slabs * half - 1) for i in range(half + 2)]


def faces_body(cx, cy, slots, fields, energy, mask, msg_a, msg_b):
    energy_of = lambda q: energy[pl.ds(pl.multiple_of(q * ROWS, ROWS), ROWS), :]
    pack_faces(fields, energy_of, cx, cy, slots, (msg_a, msg_b), "slab", False)
    _, faces = pair_faces("slab", BELOW, ABOVE)
    for out, face in zip((msg_a, msg_b), faces):
        first = jnp.where(face == ABOVE, cx - 1, 0) * cy
        fill(out, MASK, take(mask, first, cy))


def slab_body(cx, slabs, cols, coarse_y, own, got_a, got_b, msg_a, msg_b, planes):
    have = present(slabs, cols)
    even, _ = pair_faces("col", LEFT, RIGHT)
    from_a, from_b = got_a[THERMAL], got_b[THERMAL]
    lower = jnp.where(even, from_b, from_a)
    upper = jnp.where(even, from_a, from_b)
    sub = lax.broadcasted_iota(jnp.int32, (ROWS, LANES), 0)
    last = coarse_y + 1
    widened = []
    for i in range(cx // 2 + 6):
        plane = own[i * ROWS : (i + 1) * ROWS, :]
        spot = slice(i // ROWS * LANES, (i // ROWS + 1) * LANES)
        below = jnp.where(have[LEFT], lower[i % ROWS : i % ROWS + 1, spot], plane[1:2, :])
        above = jnp.where(have[RIGHT], upper[i % ROWS : i % ROWS + 1, spot], plane[coarse_y : coarse_y + 1, :])
        plane = jnp.where(sub == 0, below, jnp.where(sub == last, above, plane))
        widened.append(plane)
        if i < cx // 2 + 2:
            planes[i * ROWS : (i + 1) * ROWS, :] = plane
    first = cx // 2 + 2
    _, faces = pair_faces("slab", BELOW, ABOVE)
    for out, face in zip((msg_a, msg_b), faces):
        for i in range(2):
            plane = jnp.where(face == ABOVE, widened[first + 2 + i], widened[first + i])
            out[:, i * LANES : (i + 1) * LANES] = plane


def axis_weights(cells):
    fine = np.arange(-1, cells + 1)
    lower = (2 * fine - 1) // 4
    weight = (2 * fine - 1 - 4 * lower) / 4.0
    out = np.zeros((cells + 2, cells // 2 + 2), np.float32)
    out[np.arange(cells + 2), lower + 1] += 1.0 - weight
    out[np.arange(cells + 2), lower + 2] += weight
    return out


def plane_weights(cx, cy):
    along, across = axis_weights(cx), axis_weights(cy)
    inner = [(x + 1, y + 1) for x in range(cx) for y in range(cy)]
    inner += [(0, y + 1) for y in range(cy)] + [(cx + 1, y + 1) for y in range(cy)]
    inner += [(x + 1, 0) for x in range(cx)] + [(x + 1, cy + 1) for x in range(cx)]
    out = np.zeros((len(inner), cx // 2 + 2, ROWS), np.float32)
    for row, (x, y) in enumerate(inner):
        out[row, :, : cy // 2 + 2] = along[x][:, None] * across[y][None, :]
    return out.reshape(len(inner), -1)


def height_weights(cells, coarse):
    fine = np.arange(cells)
    lower = (2 * fine - 1) // 4
    weight = (2 * fine - 1 - 4 * lower) / 4.0
    out = np.zeros((coarse, cells), np.float32)
    np.add.at(out, (np.clip(lower, 0, coarse - 1), fine), 1.0 - weight)
    np.add.at(out, (np.clip(lower + 1, 0, coarse - 1), fine), weight)
    return out


def mobility_body(
    cx, cy, slots, slabs, cols, planes, bounds, mask_ref, weights, height, energy, slots_ref,
    col_a, col_b, slab_a, slab_b, ends_b, ends_a, keep, near,
):
    start, end = bounds[0:ROWS, :], bounds[ROWS : 2 * ROWS, :]
    even_s, _ = pair_faces("slab", BELOW, ABOVE)
    even_c, _ = pair_faces("col", LEFT, RIGHT)
    mask = MASK
    below = jnp.where(even_s, ends_b[...], ends_a[...])
    above = jnp.where(even_s, ends_a[...], ends_b[...])
    for i, p in enumerate(near_planes(cx, slabs)):
        p = jnp.full((ROWS, LANES), p, jnp.int32)
        own = planes[i * ROWS : (i + 1) * ROWS, :]
        lower = jnp.where(p == start - 2, below[:, :LANES], below[:, LANES:])
        upper = jnp.where(p == end, above[:, :LANES], above[:, LANES:])
        near[i * ROWS : (i + 1) * ROWS, :] = jnp.where(p < start, lower, jnp.where(p < end, own, upper))
    flat = jnp.dot(weights[...], near[...], precision=HIGHEST, preferred_element_type=jnp.float32)
    profile = jnp.dot(flat, height[...], precision=HIGHEST, preferred_element_type=jnp.float32)
    mobility = jnp.exp(2.0 * (profile - 1.0)) * TIME_STEP
    cells = cx * cy
    kept = Kept(keep, 0, cx, cy, slots)
    for i, part in enumerate(take(mask_ref, 0, cells)):
        put(keep, 0, i, part * mobility[:cells, i * LANES : (i + 1) * LANES])
    have = present(slabs, cols)
    masks = (
        jnp.where(even_s, slab_b[mask], slab_a[mask]),
        jnp.where(even_s, slab_a[mask], slab_b[mask]),
        jnp.where(even_c, col_b[mask], col_a[mask]),
        jnp.where(even_c, col_a[mask], col_b[mask]),
    )
    for k in range(FACES):
        at = cells + k * ROWS
        for i, part in enumerate(split(jnp.where(have[k], masks[k] * mobility[at : at + ROWS], 0.0))):
            put(keep, at, i, part)
    for i in range(2):
        put(keep, kept.energy_base, i, energy[...])
        put(keep, kept.slots_base, i, slots_ref[...])
    marks = edges()
    top, bottom = marks[2:]
    for x in range(cx):
        sums = neighbours(x, cx - 1, kept.rate, kept.rate(x), None, None, marks)
        extra = [None] * FACES
        if x == 0:
            extra[BELOW] = kept.rate_beside(BELOW)
        if x == cx - 1:
            extra[ABOVE] = kept.rate_beside(ABOVE)
        extra[LEFT] = [jnp.where(top, v, 0.0) for v in spread(keep, cells + LEFT * ROWS + x)]
        extra[RIGHT] = [jnp.where(bottom, v, 0.0) for v in spread(keep, cells + RIGHT * ROWS + x)]
        for k in range(FACES):
            for i in range(2):
                value = sums[i] if extra[k] is None else sums[i] + extra[k][i]
                put(keep, kept.near_base + k * cells + x * cy, i, value)


def split(value):
    return value[:, :LANES], value[:, LANES:]


def along_height(v0, v1, first, last):
    r0, r1 = pltpu.roll(v0, 1, 1), pltpu.roll(v1, 1, 1)
    q0, q1 = pltpu.roll(v0, LANES - 1, 1), pltpu.roll(v1, LANES - 1, 1)
    return (
        jnp.where(first, 0.0, r0) + jnp.where(last, q1, q0),
        jnp.where(first, r0, r1) + jnp.where(last, 0.0, q1),
    )


def along_rows(v, top, bottom, lower, upper, shifted=None):
    before, after = shifted or (pltpu.roll(v, 1, 0), pltpu.roll(v, ROWS - 1, 0))
    down = jnp.where(top, 0.0 if lower is None else lower, before)
    up = jnp.where(bottom, 0.0 if upper is None else upper, after)
    return down + up


def edges():
    lane = lax.broadcasted_iota(jnp.int32, (ROWS, LANES), 1)
    row = lax.broadcasted_iota(jnp.int32, (ROWS, LANES), 0)
    return lane == 0, lane == LANES - 1, row == 0, row == ROWS - 1


def neighbours(x, last_x, load, centre, halo, kind, marks, shift=None):
    first, last, top, bottom = marks
    v0, v1 = centre
    n0, n1 = along_height(v0, v1, first, last)
    low = high = (None, None)
    if kind == LEFT:
        low = halo(x)
    if kind == RIGHT:
        high = halo(x)
    shifted = (None, None)
    if shift is not None and 0 < x < last_x:
        before, after = shift(x, -1), shift(x, 1)
        shifted = tuple(zip(before, after))
    n0 = n0 + along_rows(v0, top, bottom, low[0], high[0], shifted[0])
    n1 = n1 + along_rows(v1, top, bottom, low[1], high[1], shifted[1])
    sides = []
    if not (isinstance(x, int) and x == 0):
        sides.append(load(x - 1))
    elif kind == BELOW:
        sides.append(halo(None))
    if not (isinstance(x, int) and x == last_x):
        sides.append(load(x + 1))
    elif kind == ABOVE:
        sides.append(halo(None))
    for a, b in sides:
        n0, n1 = n0 + a, n1 + b
    return n0, n1


def over_planes(cx, visit, carry):
    carry = visit(0, carry)
    carry = lax.fori_loop(1, cx - 1, visit, carry)
    return visit(cx - 1, carry)


def slot_access(fields, halos, base, q, cells, cy):
    def load(x):
        return take(fields, q * cells + x * cy, cy)

    def halo(x):
        if x is None:
            return take(halos, base + q * ROWS, ROWS)
        return spread(halos, base + q * ROWS + x)

    return load, halo


def force_of(v, n, squares3, energy):
    return v * (squares3 + ((5.0 - energy) + v * (energy - 2.0 * v))) - n


def triple_squares(fields, x, slots, cells, cy):
    total = None
    for q in range(slots):
        v0, v1 = take(fields, q * cells + x * cy, cy)
        total = (v0 * v0, v1 * v1) if total is None else (total[0] + v0 * v0, total[1] + v1 * v1)
    return 2.0 * COUPLING * total[0], 2.0 * COUPLING * total[1]


def inner_body(cx, cy, slots, base, *refs):
    fields, force_out = refs[0], refs[-1]
    cells = cx * cy
    marks = edges()
    if base is None:
        energy = lambda q: refs[1][q * ROWS : (q + 1) * ROWS, :]
    else:
        energy = Kept(fields, base, cx, cy, slots).energy

    def visit(x, carry):
        squares = triple_squares(fields, x, slots, cells, cy)
        for q in range(slots):
            load, _ = slot_access(fields, None, None, q, cells, cy)
            centre = load(x)
            shift = lambda y, by: take_shifted(fields, q * cells + y * cy, cy, by)
            near = neighbours(x, cx - 1, load, centre, None, None, marks, shift)
            e = energy(q)
            for i in range(2):
                put(force_out, q * cells + x * cy, i, force_of(centre[i], near[i], squares[i], e))
        return carry

    for x in range(cx):
        visit(x, 0)


def arrivals(col_a, col_b, slab_a, slab_b):
    even_s, _ = pair_faces("slab", BELOW, ABOVE)
    even_c, _ = pair_faces("col", LEFT, RIGHT)
    pairs = ((slab_b, slab_a, even_s), (slab_a, slab_b, even_s), (col_b, col_a, even_c), (col_a, col_b, even_c))
    return [functools.partial(lambda u, v, even, i: jnp.where(even, u[i], v[i]), *pair) for pair in pairs]


class Grown:
    def __init__(self, cx, cy, slots):
        self.cells = cx * cy
        self.sum = slots * self.cells
        self.squares = self.sum + self.cells
        self.halos = self.squares + self.cells
        self.kept = self.halos + slots * ROWS
        self.count = Kept.rows(self.cells, slots)
        self.rows = self.kept + self.count


def sums_body(
    cx, cy, slots, slabs, cols, devices, base, fields, keep, force_in, col_a, col_b, slab_a, slab_b,
    grown, sums_ref, halos,
):
    cells = cx * cy
    _, _, top, bottom = edges()
    have = present(slabs, cols)
    kept = Kept(keep, base, cx, cy, slots)
    layout = Grown(cx, cy, slots)
    keep_on(grown, layout.kept, kept, layout.count)
    for k, pick in enumerate(arrivals(col_a, col_b, slab_a, slab_b)):
        rate = kept.rate_beside(k)
        for j in range(SHARE):
            q = k * SHARE + j
            if k == BELOW:
                own = take(fields, q * cells, cy)
            elif k == ABOVE:
                own = take(fields, (q + 1) * cells - cy, cy)
            elif k == LEFT:
                own = take(fields, q * cells, cx, cy)
            else:
                own = take(fields, q * cells + cy - 1, cx, cy)
            beside, force = split(jnp.where(have[k], pick(j), 0.0)), split(pick(SHARE + j))
            for i in range(2):
                put(halos, q * ROWS, i, beside[i])
                put(grown, layout.halos + q * ROWS, i, beside[i] - rate[i] * (force[i] - own[i]))

    energy_sum = None
    for q in range(slots):
        energy_sum = kept.energy(q) if energy_sum is None else energy_sum + kept.energy(q)
    zero = jnp.zeros((ROWS, LANES), jnp.float32)

    def visit(x, carry):
        total, c0, c1, c2, c3, weight = carry
        rate = kept.rate(x)
        forces, powers = [zero, zero], [zero, zero]
        a2, b1 = [zero, zero], [zero, zero]
        a1 = [[zero, zero] for _ in range(FACES)]
        for q in range(slots):
            k = q // SHARE
            centre = take(fields, q * cells + x * cy, cy)
            inner = take(force_in, q * cells + x * cy, cy)
            e = kept.energy(q)
            cross = (None, None)
            if k in (LEFT, RIGHT):
                row = spread(halos, q * ROWS + x)
                cross = [jnp.where(top if k == LEFT else bottom, row[i], 0.0) for i in range(2)]
            elif isinstance(x, int) and (k, x) in ((BELOW, 0), (ABOVE, cx - 1)):
                cross = take(halos, q * ROWS, ROWS)
            for i in range(2):
                force = inner[i] if cross[i] is None else inner[i] - cross[i]
                g = centre[i] - rate[i] * force
                put(grown, q * cells + x * cy, i, g)
                weighted, square = e * g, g * g
                forces[i] = forces[i] + force
                powers[i] = powers[i] + g * (weighted - (square + square))
                a1[k][i] = a1[k][i] + g
                a2[i] = a2[i] + square
                b1[i] = b1[i] + weighted
        beside = [kept.near(k, x) for k in range(FACES)]
        for i in range(2):
            h = rate[i]
            whole = (a1[0][i] + a1[1][i]) + (a1[2][i] + a1[3][i])
            near = [beside[k][i] for k in range(FACES)]
            put(grown, layout.sum + x * cy, i, whole)
            put(grown, layout.squares + x * cy, i, a2[i])
            total = total + h * forces[i]
            c0 = c0 + h * (powers[i] + 5.0 * whole - b1[i] + 2.0 * COUPLING * whole * a2[i])
            for k in range(FACES):
                c0 = c0 - a1[k][i] * near[k]
            linear = (
                energy_sum
                - 5.0 * slots
                - 2.0 * b1[i]
                + (6.0 - 2.0 * COUPLING * slots) * a2[i]
                - 4.0 * COUPLING * (whole * whole)
            )
            c1 = c1 + h * (h * linear + float(SHARE) * ((near[0] + near[1]) + (near[2] + near[3])))
            c2 = c2 + h * h * h * (energy_sum + (6.0 * COUPLING * slots - 6.0) * whole)
            c3 = c3 + (h * h) * (h * h)
            weight = weight + h
        return total, c0, c1, c2, c3, weight

    parts = over_planes(cx, visit, (zero,) * 6)
    back = -1.0 / TIME_STEP
    scales = (back, back, back, back, back * (2.0 * slots - 2.0 * COUPLING * slots * slots), 1.0 / TIME_STEP)
    lane = lax.broadcasted_iota(jnp.int32, (1, LANES), 1)
    row = jnp.zeros((1, LANES), jnp.float32)
    for i, (part, scale) in enumerate(zip(parts, scales)):
        value = jnp.sum(jnp.sum(part, axis=0, keepdims=True), axis=1, keepdims=True) * scale
        row = jnp.where(lane == i, value, row)
    sums_ref[...] = jnp.broadcast_to(row[None], (devices, 1, LANES))


def multipliers(got, slots):
    total = jnp.sum(got[...], axis=0)
    lane = lax.broadcasted_iota(jnp.int32, (1, LANES), 1)
    part = [jnp.sum(jnp.where(lane == i, total, 0.0), axis=1, keepdims=True) for i in range(6)]
    whole = slots * part[5]
    here = part[0] / whole
    later = (part[1] + here * (part[2] + here * (part[3] + here * part[4]))) / whole
    return jnp.broadcast_to(here, (ROWS, LANES)), jnp.broadcast_to(later, (ROWS, LANES))


def settle(cx, cy, slots, got, grown, store, done=None):
    cells = cx * cy
    marks = edges()
    here, later = multipliers(got, slots)
    layout = Grown(cx, cy, slots)
    kept = Kept(grown, layout.kept, cx, cy, slots)
    for k in range(FACES):

        def visit(x, carry):
            rate = kept.rate(x)
            near = kept.near(k, x)
            a1 = take(grown, layout.sum + x * cy, cy)
            a2 = take(grown, layout.squares + x * cy, cy)
            off = [here * rate[i] for i in range(2)]
            base = [
                5.0 + 2.0 * COUPLING * (a2[i] - off[i] * (2.0 * a1[i] - float(slots) * off[i])) for i in range(2)
            ]
            extra = [here * near[i] + later for i in range(2)]
            for q in range(k * SHARE, (k + 1) * SHARE):
                e = kept.energy(q)
                load, halo = slot_access(grown, grown, layout.halos, q, cells, cy)
                shift = lambda y, by: take_shifted(grown, q * cells + y * cy, cy, by)
                g = load(x)
                n = neighbours(x, cx - 1, load, g, halo, k, marks, shift)
                for i in range(2):
                    f = g[i] - off[i]
                    force = f * ((base[i] - e) + f * (e - (f + f))) - (n[i] - extra[i])
                    store(q, x, i, f - rate[i] * force)
            return carry

        for x in range(cx):
            visit(x, 0)
        if done is not None:
            done(k)


def middle_body(cx, cy, slots, got, grown, fields, slab_a, slab_b):
    def store(q, x, i, value):
        put(fields, q * cx * cy + x * cy, i, value)

    settle(cx, cy, slots, got, grown, store)
    layout = Grown(cx, cy, slots)
    keep_on(fields, slots * cx * cy, Kept(grown, layout.kept, cx, cy, slots), layout.count)
    energy = Kept(fields, slots * cx * cy, cx, cy, slots).energy
    pack_faces(fields, energy, cx, cy, slots, (slab_a, slab_b), "slab", False)


def cols_body(cx, cy, slots, fields, col_a, col_b):
    energy = Kept(fields, slots * cx * cy, cx, cy, slots).energy
    pack_faces(fields, energy, cx, cy, slots, (col_a, col_b), "col", True)


def last_body(cx, cy, slots, got, grown, out, result, order, sems, order_sem):
    kept = Kept(grown, Grown(cx, cy, slots).kept, cx, cy, slots)
    fetch = pltpu.make_async_copy(grown.at[pl.ds(kept.slots_base, ROWS), :], order, order_sem)
    fetch.start()

    def store(q, x, i, value):
        at = x * cy if isinstance(x, int) else pl.multiple_of(x * cy, ROWS)
        result[q, pl.ds(at, cy), i * LANES : (i + 1) * LANES] = value

    def send(q):
        return pltpu.make_async_copy(result.at[q], out.at[order[0, q].astype(jnp.int32)], sems.at[q])

    def done(k):
        if k == 0:
            fetch.wait()
        for q in range(k * SHARE, (k + 1) * SHARE):
            send(q).start()

    settle(cx, cy, slots, got, grown, store, done)
    for q in range(slots):
        send(q).wait()


def exchange_cols(first, second):
    count = lax.axis_size("col")
    one = [(i, i ^ 1) for i in range(count)]
    two = [(i, (i - 1) % count if i % 2 == 0 else (i + 1) % count) for i in range(count)]
    return lax.ppermute(first, "col", one), lax.ppermute(second, "col", two)


def exchange_slabs(first, second):
    count, cols = lax.axis_size("slab"), lax.axis_size("col")
    one = [(i, i ^ 1) for i in range(count)]
    two = []
    for s in range(count):
        other = s - 1 if s % 2 == 0 else s + 1
        for c in range(cols):
            target = other * cols + c if 0 <= other < count else s * cols + (c ^ 1)
            two.append((s * cols + c, target))
    return lax.ppermute(second, ("slab", "col"), two), lax.ppermute(first, "slab", one)


def per_device(order_params, layer_mask, coarse_temp, coarse_rows, grain_ids, energy):
    slots, cx, cy, cz = order_params.shape
    slabs, cols = lax.axis_size("slab"), lax.axis_size("col")
    devices = slabs * cols
    cells = cx * cy
    capacity, _, coarse_z = coarse_temp.shape
    raw = order_params.reshape(slots * cells, cz)
    mask = layer_mask.reshape(cells, cz)
    message = f32(THERMAL + 1, ROWS, cz)
    short = f32(2 * SHARE, ROWS, cz)
    state = f32(2 * slots * cells, cz // 2)

    hbm = lambda x: pltpu.with_memory_space_constraint(x, pltpu.HBM)
    near = cx // 2 + 2
    fields, mask, slot_order, slot_energy, bounds, planes, col_a, col_b = call(
        functools.partial(open_body, cx, cy, slots, slabs, cols),
        (
            state,
            f32(2 * cells, LANES),
            f32(ROWS, LANES),
            f32(slots * ROWS, LANES),
            jax.ShapeDtypeStruct((2 * ROWS, LANES), jnp.int32),
            f32((near + 4) * ROWS, LANES),
            message,
            message,
        ),
        [HBM] * 6,
        (VMEM,) * 8,
        [
            pltpu.SMEM(grain_ids.shape, jnp.int32),
            pltpu.SMEM(coarse_rows.shape, jnp.int32),
            pltpu.SMEM(energy.shape, jnp.float32),
            pltpu.VMEM(grain_ids.shape, jnp.int32),
            pltpu.VMEM(coarse_temp.shape, jnp.float32),
            pltpu.VMEM((2 * cells, LANES), jnp.int32),
            pltpu.VMEM(state.shape, jnp.float32),
            pltpu.SemaphoreType.DMA((9,)),
        ],
    )(hbm(grain_ids), hbm(coarse_rows), hbm(energy), hbm(raw), hbm(mask), hbm(coarse_temp))
    col_a, col_b = exchange_cols(col_a, col_b)
    slab_a, slab_b = call(
        functools.partial(faces_body, cx, cy, slots),
        (f32(THERMAL, ROWS, cz),) * 2,
        [VMEM] * 3,
        (VMEM,) * 2,
    )(fields, slot_energy, mask)
    slab_b, slab_a = exchange_slabs(slab_a, slab_b)
    ends_a, ends_b, planes = call(
        functools.partial(slab_body, cx, slabs, cols, coarse_temp.shape[1]),
        (f32(ROWS, cz), f32(ROWS, cz), f32(near * ROWS, LANES)),
        [VMEM] * 3,
        (VMEM,) * 3,
    )(planes, col_a, col_b)
    ends_b, ends_a = exchange_slabs(ends_a, ends_b)
    weights = jnp.asarray(plane_weights(cx, cy))
    height = jnp.asarray(height_weights(cz, coarse_z))
    count = Kept.rows(cells, slots)
    keep = call(
        functools.partial(mobility_body, cx, cy, slots, slabs, cols),
        f32(2 * count, LANES),
        [VMEM] * 13,
        VMEM,
        [pltpu.VMEM((near * ROWS, LANES), jnp.float32)],
    )(planes, bounds, mask, weights, height, slot_energy, slot_order, col_a, col_b, slab_a, slab_b, ends_b, ends_a)

    for pair in range(STEPS // 2):
        base = None if pair == 0 else slots * cells
        inputs = (fields, slot_energy) if pair == 0 else (fields,)
        force = call(
            functools.partial(inner_body, cx, cy, slots, base),
            state,
            [VMEM] * len(inputs),
            VMEM,
            flops=1 << 23,
            size=1 << 22,
        )(*inputs)
        grown, sums = call(
            functools.partial(sums_body, cx, cy, slots, slabs, cols, devices, base or 0),
            (f32(2 * Grown(cx, cy, slots).rows, LANES), f32(devices, 1, LANES)),
            [VMEM] * 7,
            (VMEM,) * 2,
            [pltpu.VMEM((2 * slots * ROWS, LANES), jnp.float32)],
        )(fields, keep if pair == 0 else fields, force, col_a, col_b, slab_a, slab_b)
        got = lax.all_to_all(sums, ("slab", "col"), 0, 0)
        if pair < STEPS // 2 - 1:
            fields, slab_a, slab_b = call(
                functools.partial(middle_body, cx, cy, slots),
                (f32(2 * (slots * cells + count), LANES), short, short),
                [VMEM] * 2,
                (VMEM,) * 3,
            )(got, grown)
            col_a, col_b = call(
                functools.partial(cols_body, cx, cy, slots), (short, short), [VMEM], (VMEM,) * 2
            )(fields)
            slab_b, slab_a = exchange_slabs(slab_a, slab_b)
            col_a, col_b = exchange_cols(col_a, col_b)
        else:
            fields = call(
                functools.partial(last_body, cx, cy, slots),
                f32(slots, cells, cz),
                [VMEM] * 2,
                HBM,
                [
                    pltpu.VMEM((slots, cells, cz), jnp.float32),
                    pltpu.SMEM((ROWS, LANES), jnp.float32),
                    pltpu.SemaphoreType.DMA((slots,)),
                    pltpu.SemaphoreType.DMA(()),
                ],
            )(got, grown)
    return fields.reshape(order_params.shape)


def solution(mesh):
    in_specs = (
        P(None, "slab", "col", None),
        P("slab", "col", None),
        P("slab", "col", None),
        P(),
        P(),
        P(),
    )
    out_specs = P(None, "slab", "col", None)
    return jax.shard_map(
        per_device, mesh=mesh, in_specs=in_specs, out_specs=out_specs, check_vma=False
    )
```

```python
import functools

import jax
import jax.numpy as jnp
import numpy as np
from jax import lax
from jax.experimental import pallas as pl
from jax.experimental.pallas import tpu as pltpu
from jax.sharding import PartitionSpec as P

SHARE = 4
STEPS = 4
TIME_STEP = 0.05
COUPLING = 1.5
BELOW, ABOVE, LEFT, RIGHT = range(4)
FACES = 4
MASK = 2 * SHARE
THERMAL = MASK + 1
LANES = 128
ROWS = 8
HIGHEST = lax.Precision.HIGHEST

VMEM = pl.BlockSpec(memory_space=pltpu.VMEM)
SMEM = pl.BlockSpec(memory_space=pltpu.SMEM)
HBM = pl.BlockSpec(memory_space=pltpu.HBM)


def call(body, out_shape, in_specs, out_specs, scratch=(), flops=1 << 20, size=1 << 20):
    return pl.pallas_call(
        body,
        out_shape=out_shape,
        in_specs=in_specs,
        out_specs=out_specs,
        scratch_shapes=list(scratch),
        compiler_params=pltpu.CompilerParams(vmem_limit_bytes=20 << 20),
        cost_estimate=pl.CostEstimate(flops=flops, bytes_accessed=size, transcendentals=0),
    )


def f32(*shape):
    return jax.ShapeDtypeStruct(shape, jnp.float32)


def present(slabs, cols):
    s, c = lax.axis_index("slab"), lax.axis_index("col")
    return (s > 0, s < slabs - 1, c > 0, c < cols - 1)


def beside(slabs, cols):
    s, c = lax.axis_index("slab"), lax.axis_index("col")
    return (
        (jnp.maximum(s - 1, 0), c),
        (jnp.minimum(s + 1, slabs - 1), c),
        (s, jnp.maximum(c - 1, 0)),
        (s, jnp.minimum(c + 1, cols - 1)),
    )


def slot_places(slabs, cols, slots, ids_ref, ids_smem):
    s, c = lax.axis_index("slab"), lax.axis_index("col")
    sub = lax.broadcasted_iota(jnp.int32, (slots, LANES), 0)
    lane = lax.broadcasted_iota(jnp.int32, (slots, LANES), 1)
    own = jnp.zeros((slots, LANES), jnp.int32)
    for q in range(slots):
        own = jnp.where(sub == q, ids_smem[s, c, q], own)
    one, zero = jnp.float32(1.0), jnp.float32(0.0)
    have = present(slabs, cols)
    matches, ranks = [], []
    for k, (ns, nc) in enumerate(beside(slabs, cols)):
        row = ids_ref[ns, pl.ds(nc, 1), :]
        row = jnp.concatenate([row, jnp.full((1, LANES - slots), -1, jnp.int32)], axis=1)
        row = jnp.broadcast_to(jnp.where(have[k], row, -1), (slots, LANES))
        hit = jnp.where((own == row) & (row >= 0), one, zero)
        shared = jnp.max(hit, axis=0, keepdims=True)
        matches.append(jnp.sum(hit, axis=1, keepdims=True))
        ranks.append(jnp.sum(jnp.where(row < own, shared, zero), axis=1, keepdims=True))
    free = one - (matches[0] + matches[1] + matches[2] + matches[3])
    lanef = lane.astype(jnp.float32)
    free_row = jnp.sum(jnp.where(sub == lane, free, zero), axis=0, keepdims=True)
    free_rank = jnp.sum(jnp.where(lane < sub, free_row, zero), axis=1, keepdims=True)
    place = jnp.zeros((slots, LANES), jnp.float32)
    skipped = jnp.int32(0)
    for k in range(FACES):
        at = matches[k] * (ranks[k] + k * SHARE - lanef)
        place = jnp.where((matches[k] > 0.5) & (jnp.abs(at) < 0.5), one, place)
        local = free_rank - (skipped * SHARE).astype(jnp.float32)
        inside = (local > -0.5) & (local < SHARE - 0.5) & (free > 0.5)
        inside = inside & jnp.logical_not(have[k])
        place = jnp.where(inside & (jnp.abs(local + k * SHARE - lanef) < 0.5), one, place)
        skipped = skipped + jnp.where(have[k], 0, 1)
    return place


def take(ref, at, rows, stride=1):
    half = ref.shape[0] // 2
    if stride == 1:
        if not isinstance(at, int):
            at = pl.multiple_of(at, ROWS)
        return ref[pl.ds(at, rows), :], ref[pl.ds(at + half, rows), :]
    return ref[pl.ds(at, rows, stride=stride), :], ref[pl.ds(at + half, rows, stride=stride), :]


def take_shifted(ref, at, rows, by):
    half = ref.shape[0] // 2
    return ref[pl.ds(at + by, rows), :], ref[pl.ds(at + by + half, rows), :]


def put(ref, at, i, value):
    if not isinstance(at, int):
        at = pl.multiple_of(at, ROWS)
    ref[pl.ds(at + i * (ref.shape[0] // 2), value.shape[0]), :] = value


def spread(ref, row):
    half = ref.shape[0] // 2
    return tuple(jnp.broadcast_to(ref[pl.ds(row + i * half, 1), :], (ROWS, LANES)) for i in range(2))


class Kept:
    def __init__(self, ref, base, cx, cy, slots):
        self.ref, self.cy, self.cells = ref, cy, cx * cy
        self.base = base
        self.near_base = base + self.cells + FACES * ROWS
        self.energy_base = self.near_base + FACES * self.cells
        self.slots_base = self.energy_base + slots * ROWS

    @staticmethod
    def rows(cells, slots):
        return cells + FACES * ROWS + FACES * cells + slots * ROWS + ROWS

    def rate(self, x):
        return take(self.ref, self.base + x * self.cy, self.cy)

    def rate_beside(self, k):
        return take(self.ref, self.base + self.cells + k * ROWS, ROWS)

    def near(self, k, x):
        return take(self.ref, self.near_base + k * self.cells + x * self.cy, self.cy)

    def energy(self, q):
        at = self.energy_base + q * ROWS
        return self.ref[pl.ds(at if isinstance(at, int) else pl.multiple_of(at, ROWS), ROWS), :]


def keep_on(out, out_base, kept, count):
    for i in range(2):
        put(out, out_base, i, take(kept.ref, kept.base, count)[i])


def fill(out, index, pair):
    out[index, :, :LANES], out[index, :, LANES:] = pair


def pair_faces(axis, low, high):
    even = lax.rem(lax.axis_index(axis), 2) == 0
    return even, (jnp.where(even, high, low), jnp.where(even, low, high))


def pack_faces(fields, energy, cx, cy, slots, out_refs, axis, columns):
    low, high = (LEFT, RIGHT) if columns else (BELOW, ABOVE)
    first, last, top, bottom = edges()
    _, faces = pair_faces(axis, low, high)
    for out, face in zip(out_refs, faces):

        def plane(q, depth):
            if columns:
                return take(fields, q * (cx * cy) + jnp.where(face == high, cy - 1 - depth, depth), cx, cy)
            return take(fields, q * (cx * cy) + jnp.where(face == high, cx - 1 - depth, depth) * cy, cy)

        squares = [None, None]
        for q in range(slots):
            for i, v in enumerate(plane(q, 0)):
                squares[i] = v * v if squares[i] is None else squares[i] + v * v
        for j in range(SHARE):
            q = face * SHARE + j
            centre, inner = plane(q, 0), plane(q, 1)
            near = along_height(centre[0], centre[1], first, last)
            e = energy(q)
            forces = []
            for i in range(2):
                n = near[i] + along_rows(centre[i], top, bottom, None, None) + inner[i]
                forces.append(force_of(centre[i], n, 2.0 * COUPLING * squares[i], e))
            fill(out, j, centre)
            fill(out, SHARE + j, forces)


def open_body(
    cx, cy, slots, slabs, cols, ids_hbm, rows_hbm, energy_hbm, fields_hbm, mask_hbm, coarse_hbm,
    fields, mask, slots_ref, energy_out, bounds, planes, msg_a, msg_b,
    ids_smem, rows_smem, energy_smem, ids_ref, coarse_ref, mask_ref, raw, sems,
):
    cells = cx * cy
    loads = [
        pltpu.make_async_copy(ids_hbm, ids_smem, sems.at[0]),
        pltpu.make_async_copy(ids_hbm, ids_ref, sems.at[1]),
        pltpu.make_async_copy(rows_hbm, rows_smem, sems.at[2]),
        pltpu.make_async_copy(coarse_hbm, coarse_ref, sems.at[3]),
        pltpu.make_async_copy(energy_hbm, energy_smem, sems.at[8]),
    ]
    for i in range(2):
        half = pl.ds(i * LANES, LANES)
        loads.append(
            pltpu.make_async_copy(mask_hbm.at[:, half], mask_ref.at[pl.ds(i * cells, cells), :], sems.at[4 + i])
        )
        rows = slots * cells
        loads.append(
            pltpu.make_async_copy(fields_hbm.at[:, half], raw.at[pl.ds(i * rows, rows), :], sems.at[6 + i])
        )
    for load in loads:
        load.start()
    for load in loads[:5]:
        load.wait()
    place = slot_places(slabs, cols, slots, ids_ref, ids_smem)
    sub = lax.broadcasted_iota(jnp.int32, (slots, LANES), 0).astype(jnp.float32)
    slot_row = jnp.sum(place * sub, axis=0, keepdims=True)
    slots_ref[...] = jnp.broadcast_to(slot_row, (ROWS, LANES))
    lane = lax.broadcasted_iota(jnp.int32, (1, LANES), 1)
    taken = [jnp.sum(jnp.where(lane == q, slot_row, 0.0)).astype(jnp.int32) for q in range(slots)]
    at_rows = lax.broadcasted_iota(jnp.int32, (slots, LANES), 0)
    own_energy = jnp.zeros((slots, LANES), jnp.float32)
    s, c = lax.axis_index("slab"), lax.axis_index("col")
    for q in range(slots):
        own_energy = jnp.where(at_rows == q, energy_smem[ids_smem[s, c, q]], own_energy)
    energy_row = jnp.sum(place * own_energy, axis=0, keepdims=True)
    for q in range(slots):
        value = jnp.sum(jnp.where(lane == q, energy_row, 0.0), axis=1, keepdims=True)
        energy_out[q * ROWS : (q + 1) * ROWS, :] = jnp.broadcast_to(value, (ROWS, LANES))

    start = jnp.int32(0)
    for t in range(slabs):
        start = start + jnp.where(t < s, rows_smem[t], 0)
    live = rows_smem[s]
    bounds[0:ROWS, :] = jnp.full((ROWS, LANES), start, jnp.int32)
    bounds[ROWS : 2 * ROWS, :] = jnp.full((ROWS, LANES), start + live, jnp.int32)
    capacity, coarse_y, _ = coarse_ref.shape
    chosen = [
        jnp.clip(plane - start, 0, capacity - 1) for plane in near_planes(cx, slabs)
    ] + [jnp.int32(0), jnp.int32(1), live - 2, live - 1]
    _, faces = pair_faces("col", LEFT, RIGHT)
    for out in (msg_a, msg_b):
        out[THERMAL] = jnp.zeros((ROWS, out.shape[2]), jnp.float32)
    planes[...] = jnp.zeros(planes.shape, jnp.float32)
    for i, p in enumerate(chosen):
        planes[i * ROWS + 1 : i * ROWS + 1 + coarse_y, :] = coarse_ref[p]
        for out, face in zip((msg_a, msg_b), faces):
            row = jnp.where(face == RIGHT, coarse_y - 1, 0)
            spot = slice(i // ROWS * LANES, (i // ROWS + 1) * LANES)
            out[THERMAL, i % ROWS : i % ROWS + 1, spot] = coarse_ref[p, pl.ds(row, 1), :]

    for load in loads[5:]:
        load.wait()
    mask[...] = mask_ref[...].astype(jnp.float32)

    for q in range(slots):
        for i, part in enumerate(take(raw, taken[q] * cells, cells)):
            put(fields, q * cells, i, part)
    energy_of = lambda q: energy_out[pl.ds(pl.multiple_of(q * ROWS, ROWS), ROWS), :]
    pack_faces(fields, energy_of, cx, cy, slots, (msg_a, msg_b), "col", True)
    for out, face in zip((msg_a, msg_b), faces):
        first = jnp.where(face == RIGHT, cy - 1, 0)
        fill(out, MASK, take(mask, first, cx, cy))


def near_planes(cx, slabs):
    s = lax.axis_index("slab")
    half = cx // 2
    return [jnp.clip(s * half - 1 + i, 0, slabs * half - 1) for i in range(half + 2)]


def faces_body(cx, cy, slots, fields, energy, mask, msg_a, msg_b):
    energy_of = lambda q: energy[pl.ds(pl.multiple_of(q * ROWS, ROWS), ROWS), :]
    pack_faces(fields, energy_of, cx, cy, slots, (msg_a, msg_b), "slab", False)
    _, faces = pair_faces("slab", BELOW, ABOVE)
    for out, face in zip((msg_a, msg_b), faces):
        first = jnp.where(face == ABOVE, cx - 1, 0) * cy
        fill(out, MASK, take(mask, first, cy))


def slab_body(cx, slabs, cols, coarse_y, own, got_a, got_b, msg_a, msg_b, planes):
    have = present(slabs, cols)
    even, _ = pair_faces("col", LEFT, RIGHT)
    from_a, from_b = got_a[THERMAL], got_b[THERMAL]
    lower = jnp.where(even, from_b, from_a)
    upper = jnp.where(even, from_a, from_b)
    sub = lax.broadcasted_iota(jnp.int32, (ROWS, LANES), 0)
    last = coarse_y + 1
    widened = []
    for i in range(cx // 2 + 6):
        plane = own[i * ROWS : (i + 1) * ROWS, :]
        spot = slice(i // ROWS * LANES, (i // ROWS + 1) * LANES)
        below = jnp.where(have[LEFT], lower[i % ROWS : i % ROWS + 1, spot], plane[1:2, :])
        above = jnp.where(have[RIGHT], upper[i % ROWS : i % ROWS + 1, spot], plane[coarse_y : coarse_y + 1, :])
        plane = jnp.where(sub == 0, below, jnp.where(sub == last, above, plane))
        widened.append(plane)
        if i < cx // 2 + 2:
            planes[i * ROWS : (i + 1) * ROWS, :] = plane
    first = cx // 2 + 2
    _, faces = pair_faces("slab", BELOW, ABOVE)
    for out, face in zip((msg_a, msg_b), faces):
        for i in range(2):
            plane = jnp.where(face == ABOVE, widened[first + 2 + i], widened[first + i])
            out[:, i * LANES : (i + 1) * LANES] = plane


def axis_weights(cells):
    fine = np.arange(-1, cells + 1)
    lower = (2 * fine - 1) // 4
    weight = (2 * fine - 1 - 4 * lower) / 4.0
    out = np.zeros((cells + 2, cells // 2 + 2), np.float32)
    out[np.arange(cells + 2), lower + 1] += 1.0 - weight
    out[np.arange(cells + 2), lower + 2] += weight
    return out


def plane_weights(cx, cy):
    along, across = axis_weights(cx), axis_weights(cy)
    inner = [(x + 1, y + 1) for x in range(cx) for y in range(cy)]
    inner += [(0, y + 1) for y in range(cy)] + [(cx + 1, y + 1) for y in range(cy)]
    inner += [(x + 1, 0) for x in range(cx)] + [(x + 1, cy + 1) for x in range(cx)]
    out = np.zeros((len(inner), cx // 2 + 2, ROWS), np.float32)
    for row, (x, y) in enumerate(inner):
        out[row, :, : cy // 2 + 2] = along[x][:, None] * across[y][None, :]
    return out.reshape(len(inner), -1)


def height_weights(cells, coarse):
    fine = np.arange(cells)
    lower = (2 * fine - 1) // 4
    weight = (2 * fine - 1 - 4 * lower) / 4.0
    out = np.zeros((coarse, cells), np.float32)
    np.add.at(out, (np.clip(lower, 0, coarse - 1), fine), 1.0 - weight)
    np.add.at(out, (np.clip(lower + 1, 0, coarse - 1), fine), weight)
    return out


def parts_of(value):
    parts = []
    for _ in range(3):
        parts.append(value.astype(jnp.bfloat16))
        value = value - parts[-1].astype(jnp.float32)
    return parts


def mobility_body(
    cx, cy, slots, slabs, cols, planes, bounds, mask_ref, weights, height, energy, slots_ref,
    ends_b, ends_a, col_a, col_b, slab_a, slab_b, keep, near,
):
    start, end = bounds[0:ROWS, :], bounds[ROWS : 2 * ROWS, :]
    even_s, _ = pair_faces("slab", BELOW, ABOVE)
    even_c, _ = pair_faces("col", LEFT, RIGHT)
    mask = MASK
    below = jnp.where(even_s, ends_b[...], ends_a[...])
    above = jnp.where(even_s, ends_a[...], ends_b[...])
    for i, p in enumerate(near_planes(cx, slabs)):
        p = jnp.full((ROWS, LANES), p, jnp.int32)
        own = planes[i * ROWS : (i + 1) * ROWS, :]
        lower = jnp.where(p == start - 2, below[:, :LANES], below[:, LANES:])
        upper = jnp.where(p == end, above[:, :LANES], above[:, LANES:])
        near[i * ROWS : (i + 1) * ROWS, :] = jnp.where(p < start, lower, jnp.where(p < end, own, upper))
    dot = functools.partial(jnp.dot, preferred_element_type=jnp.float32)
    flat = sum(dot(weights[...], part) for part in parts_of(near[...]))
    profile = sum(dot(part, height[...]) for part in parts_of(flat))
    mobility = jnp.exp(2.0 * (profile - 1.0)) * TIME_STEP
    cells = cx * cy
    kept = Kept(keep, 0, cx, cy, slots)
    for i, part in enumerate(take(mask_ref, 0, cells)):
        put(keep, 0, i, part * mobility[:cells, i * LANES : (i + 1) * LANES])
    have = present(slabs, cols)
    masks = (
        jnp.where(even_s, slab_b[mask], slab_a[mask]),
        jnp.where(even_s, slab_a[mask], slab_b[mask]),
        jnp.where(even_c, col_b[mask], col_a[mask]),
        jnp.where(even_c, col_a[mask], col_b[mask]),
    )
    for k in range(FACES):
        at = cells + k * ROWS
        for i, part in enumerate(split(jnp.where(have[k], masks[k] * mobility[at : at + ROWS], 0.0))):
            put(keep, at, i, part)
    for i in range(2):
        put(keep, kept.energy_base, i, energy[...])
        put(keep, kept.slots_base, i, slots_ref[...])
    marks = edges()
    top, bottom = marks[2:]
    for x in range(cx):
        sums = neighbours(x, cx - 1, kept.rate, kept.rate(x), None, None, marks)
        extra = [None] * FACES
        if x == 0:
            extra[BELOW] = kept.rate_beside(BELOW)
        if x == cx - 1:
            extra[ABOVE] = kept.rate_beside(ABOVE)
        extra[LEFT] = [jnp.where(top, v, 0.0) for v in spread(keep, cells + LEFT * ROWS + x)]
        extra[RIGHT] = [jnp.where(bottom, v, 0.0) for v in spread(keep, cells + RIGHT * ROWS + x)]
        for k in range(FACES):
            for i in range(2):
                value = sums[i] if extra[k] is None else sums[i] + extra[k][i]
                put(keep, kept.near_base + k * cells + x * cy, i, value)


def split(value):
    return value[:, :LANES], value[:, LANES:]


def along_height(v0, v1, first, last):
    r0, r1 = pltpu.roll(v0, 1, 1), pltpu.roll(v1, 1, 1)
    q0, q1 = pltpu.roll(v0, LANES - 1, 1), pltpu.roll(v1, LANES - 1, 1)
    return (
        jnp.where(first, 0.0, r0) + jnp.where(last, q1, q0),
        jnp.where(first, r0, r1) + jnp.where(last, 0.0, q1),
    )


def along_rows(v, top, bottom, lower, upper, shifted=None):
    before, after = shifted or (pltpu.roll(v, 1, 0), pltpu.roll(v, ROWS - 1, 0))
    down = jnp.where(top, 0.0 if lower is None else lower, before)
    up = jnp.where(bottom, 0.0 if upper is None else upper, after)
    return down + up


def edges():
    lane = lax.broadcasted_iota(jnp.int32, (ROWS, LANES), 1)
    row = lax.broadcasted_iota(jnp.int32, (ROWS, LANES), 0)
    return lane == 0, lane == LANES - 1, row == 0, row == ROWS - 1


def neighbours(x, last_x, load, centre, halo, kind, marks, shift=None):
    first, last, top, bottom = marks
    v0, v1 = centre
    n0, n1 = along_height(v0, v1, first, last)
    low = high = (None, None)
    if kind == LEFT:
        low = halo(x)
    if kind == RIGHT:
        high = halo(x)
    shifted = (None, None)
    if shift is not None and 0 < x < last_x:
        before, after = shift(x, -1), shift(x, 1)
        shifted = tuple(zip(before, after))
    n0 = n0 + along_rows(v0, top, bottom, low[0], high[0], shifted[0])
    n1 = n1 + along_rows(v1, top, bottom, low[1], high[1], shifted[1])
    sides = []
    if not (isinstance(x, int) and x == 0):
        sides.append(load(x - 1))
    elif kind == BELOW:
        sides.append(halo(None))
    if not (isinstance(x, int) and x == last_x):
        sides.append(load(x + 1))
    elif kind == ABOVE:
        sides.append(halo(None))
    for a, b in sides:
        n0, n1 = n0 + a, n1 + b
    return n0, n1


def over_planes(cx, visit, carry):
    carry = visit(0, carry)
    carry = lax.fori_loop(1, cx - 1, visit, carry)
    return visit(cx - 1, carry)


def slot_access(fields, halos, base, q, cells, cy):
    def load(x):
        return take(fields, q * cells + x * cy, cy)

    def halo(x):
        if x is None:
            return take(halos, base + q * ROWS, ROWS)
        return spread(halos, base + q * ROWS + x)

    return load, halo


def force_of(v, n, squares3, energy):
    return v * (squares3 + ((5.0 - energy) + v * (energy - 2.0 * v))) - n


def triple_squares(fields, x, slots, cells, cy):
    total = None
    for q in range(slots):
        v0, v1 = take(fields, q * cells + x * cy, cy)
        total = (v0 * v0, v1 * v1) if total is None else (total[0] + v0 * v0, total[1] + v1 * v1)
    return 2.0 * COUPLING * total[0], 2.0 * COUPLING * total[1]


def inner_body(cx, cy, slots, base, *refs):
    fields, force_out = refs[0], refs[-1]
    cells = cx * cy
    marks = edges()
    if base is None:
        energy = lambda q: refs[1][q * ROWS : (q + 1) * ROWS, :]
    else:
        energy = Kept(fields, base, cx, cy, slots).energy

    def visit(x, carry):
        squares = triple_squares(fields, x, slots, cells, cy)
        for q in range(slots):
            load, _ = slot_access(fields, None, None, q, cells, cy)
            centre = load(x)
            shift = lambda y, by: take_shifted(fields, q * cells + y * cy, cy, by)
            near = neighbours(x, cx - 1, load, centre, None, None, marks, shift)
            e = energy(q)
            for i in range(2):
                put(force_out, q * cells + x * cy, i, force_of(centre[i], near[i], squares[i], e))
        return carry

    for x in range(cx):
        visit(x, 0)


def arrivals(col_a, col_b, slab_a, slab_b):
    even_s, _ = pair_faces("slab", BELOW, ABOVE)
    even_c, _ = pair_faces("col", LEFT, RIGHT)
    pairs = ((slab_b, slab_a, even_s), (slab_a, slab_b, even_s), (col_b, col_a, even_c), (col_a, col_b, even_c))
    return [functools.partial(lambda u, v, even, i: jnp.where(even, u[i], v[i]), *pair) for pair in pairs]


class Grown:
    def __init__(self, cx, cy, slots):
        self.cells = cx * cy
        self.sum = slots * self.cells
        self.squares = self.sum + self.cells
        self.halos = self.squares + self.cells
        self.kept = self.halos + slots * ROWS
        self.count = Kept.rows(self.cells, slots)
        self.rows = self.kept + self.count


def sums_body(
    cx, cy, slots, slabs, cols, devices, base, fields, keep, force_in, col_a, col_b, slab_a, slab_b,
    grown, sums_ref, halos,
):
    cells = cx * cy
    _, _, top, bottom = edges()
    have = present(slabs, cols)
    kept = Kept(keep, base, cx, cy, slots)
    layout = Grown(cx, cy, slots)
    keep_on(grown, layout.kept, kept, layout.count)
    for k, pick in enumerate(arrivals(col_a, col_b, slab_a, slab_b)):
        rate = kept.rate_beside(k)
        for j in range(SHARE):
            q = k * SHARE + j
            if k == BELOW:
                own = take(fields, q * cells, cy)
            elif k == ABOVE:
                own = take(fields, (q + 1) * cells - cy, cy)
            elif k == LEFT:
                own = take(fields, q * cells, cx, cy)
            else:
                own = take(fields, q * cells + cy - 1, cx, cy)
            beside, force = split(jnp.where(have[k], pick(j), 0.0)), split(pick(SHARE + j))
            for i in range(2):
                put(halos, q * ROWS, i, beside[i])
                put(grown, layout.halos + q * ROWS, i, beside[i] - rate[i] * (force[i] - own[i]))

    energy_sum = None
    for q in range(slots):
        energy_sum = kept.energy(q) if energy_sum is None else energy_sum + kept.energy(q)
    zero = jnp.zeros((ROWS, LANES), jnp.float32)

    def visit(x, carry):
        total, c0, c1, c2, c3, weight = carry
        rate = kept.rate(x)
        forces, powers = [zero, zero], [zero, zero]
        a2, b1 = [zero, zero], [zero, zero]
        a1 = [[zero, zero] for _ in range(FACES)]
        for q in range(slots):
            k = q // SHARE
            centre = take(fields, q * cells + x * cy, cy)
            inner = take(force_in, q * cells + x * cy, cy)
            e = kept.energy(q)
            cross = (None, None)
            if k in (LEFT, RIGHT):
                row = spread(halos, q * ROWS + x)
                cross = [jnp.where(top if k == LEFT else bottom, row[i], 0.0) for i in range(2)]
            elif isinstance(x, int) and (k, x) in ((BELOW, 0), (ABOVE, cx - 1)):
                cross = take(halos, q * ROWS, ROWS)
            for i in range(2):
                force = inner[i] if cross[i] is None else inner[i] - cross[i]
                g = centre[i] - rate[i] * force
                put(grown, q * cells + x * cy, i, g)
                weighted, square = e * g, g * g
                forces[i] = forces[i] + force
                powers[i] = powers[i] + g * (weighted - (square + square))
                a1[k][i] = a1[k][i] + g
                a2[i] = a2[i] + square
                b1[i] = b1[i] + weighted
        beside = [kept.near(k, x) for k in range(FACES)]
        for i in range(2):
            h = rate[i]
            whole = (a1[0][i] + a1[1][i]) + (a1[2][i] + a1[3][i])
            near = [beside[k][i] for k in range(FACES)]
            put(grown, layout.sum + x * cy, i, whole)
            put(grown, layout.squares + x * cy, i, a2[i])
            total = total + h * forces[i]
            c0 = c0 + h * (powers[i] + 5.0 * whole - b1[i] + 2.0 * COUPLING * whole * a2[i])
            for k in range(FACES):
                c0 = c0 - a1[k][i] * near[k]
            linear = (
                energy_sum
                - 5.0 * slots
                - 2.0 * b1[i]
                + (6.0 - 2.0 * COUPLING * slots) * a2[i]
                - 4.0 * COUPLING * (whole * whole)
            )
            c1 = c1 + h * (h * linear + float(SHARE) * ((near[0] + near[1]) + (near[2] + near[3])))
            c2 = c2 + h * h * h * (energy_sum + (6.0 * COUPLING * slots - 6.0) * whole)
            c3 = c3 + (h * h) * (h * h)
            weight = weight + h
        return total, c0, c1, c2, c3, weight

    parts = over_planes(cx, visit, (zero,) * 6)
    back = -1.0 / TIME_STEP
    scales = (back, back, back, back, back * (2.0 * slots - 2.0 * COUPLING * slots * slots), 1.0 / TIME_STEP)
    lane = lax.broadcasted_iota(jnp.int32, (1, LANES), 1)
    row = jnp.zeros((1, LANES), jnp.float32)
    for i, (part, scale) in enumerate(zip(parts, scales)):
        value = jnp.sum(jnp.sum(part, axis=0, keepdims=True), axis=1, keepdims=True) * scale
        row = jnp.where(lane == i, value, row)
    sums_ref[...] = jnp.broadcast_to(row[None], (devices, 1, LANES))


def multipliers(got, slots):
    total = jnp.sum(got[...], axis=0)
    lane = lax.broadcasted_iota(jnp.int32, (1, LANES), 1)
    part = [jnp.sum(jnp.where(lane == i, total, 0.0), axis=1, keepdims=True) for i in range(6)]
    whole = slots * part[5]
    here = part[0] / whole
    later = (part[1] + here * (part[2] + here * (part[3] + here * part[4]))) / whole
    return jnp.broadcast_to(here, (ROWS, LANES)), jnp.broadcast_to(later, (ROWS, LANES))


def settle(cx, cy, slots, got, grown, store, done=None):
    cells = cx * cy
    marks = edges()
    here, later = multipliers(got, slots)
    layout = Grown(cx, cy, slots)
    kept = Kept(grown, layout.kept, cx, cy, slots)
    for k in range(FACES):

        def visit(x, carry):
            rate = kept.rate(x)
            near = kept.near(k, x)
            a1 = take(grown, layout.sum + x * cy, cy)
            a2 = take(grown, layout.squares + x * cy, cy)
            off = [here * rate[i] for i in range(2)]
            base = [
                5.0 + 2.0 * COUPLING * (a2[i] - off[i] * (2.0 * a1[i] - float(slots) * off[i])) for i in range(2)
            ]
            extra = [here * near[i] + later for i in range(2)]
            for q in range(k * SHARE, (k + 1) * SHARE):
                e = kept.energy(q)
                load, halo = slot_access(grown, grown, layout.halos, q, cells, cy)
                shift = lambda y, by: take_shifted(grown, q * cells + y * cy, cy, by)
                g = load(x)
                n = neighbours(x, cx - 1, load, g, halo, k, marks, shift)
                for i in range(2):
                    f = g[i] - off[i]
                    force = f * ((base[i] - e) + f * (e - (f + f))) - (n[i] - extra[i])
                    store(q, x, i, f - rate[i] * force)
            return carry

        for x in range(cx):
            visit(x, 0)
        if done is not None:
            done(k)


def middle_body(cx, cy, slots, got, grown, fields, slab_a, slab_b):
    def store(q, x, i, value):
        put(fields, q * cx * cy + x * cy, i, value)

    settle(cx, cy, slots, got, grown, store)
    layout = Grown(cx, cy, slots)
    keep_on(fields, slots * cx * cy, Kept(grown, layout.kept, cx, cy, slots), layout.count)
    energy = Kept(fields, slots * cx * cy, cx, cy, slots).energy
    pack_faces(fields, energy, cx, cy, slots, (slab_a, slab_b), "slab", False)


def cols_body(cx, cy, slots, fields, col_a, col_b):
    energy = Kept(fields, slots * cx * cy, cx, cy, slots).energy
    pack_faces(fields, energy, cx, cy, slots, (col_a, col_b), "col", True)


def last_body(cx, cy, slots, got, grown, out, result, order, sems, order_sem):
    kept = Kept(grown, Grown(cx, cy, slots).kept, cx, cy, slots)
    fetch = pltpu.make_async_copy(grown.at[pl.ds(kept.slots_base, ROWS), :], order, order_sem)
    fetch.start()

    def store(q, x, i, value):
        at = x * cy if isinstance(x, int) else pl.multiple_of(x * cy, ROWS)
        result[q, pl.ds(at, cy), i * LANES : (i + 1) * LANES] = value

    def send(q):
        return pltpu.make_async_copy(result.at[q], out.at[order[0, q].astype(jnp.int32)], sems.at[q])

    def done(k):
        if k == 0:
            fetch.wait()
        for q in range(k * SHARE, (k + 1) * SHARE):
            send(q).start()

    settle(cx, cy, slots, got, grown, store, done)
    for q in range(slots):
        send(q).wait()


def exchange_cols(first, second):
    count = lax.axis_size("col")
    one = [(i, i ^ 1) for i in range(count)]
    two = [(i, (i - 1) % count if i % 2 == 0 else (i + 1) % count) for i in range(count)]
    return lax.ppermute(first, "col", one), lax.ppermute(second, "col", two)


def exchange_slabs(first, second):
    count, cols = lax.axis_size("slab"), lax.axis_size("col")
    one = [(i, i ^ 1) for i in range(count)]
    two = []
    for s in range(count):
        other = s - 1 if s % 2 == 0 else s + 1
        for c in range(cols):
            target = other * cols + c if 0 <= other < count else s * cols + (c ^ 1)
            two.append((s * cols + c, target))
    return lax.ppermute(second, ("slab", "col"), two), lax.ppermute(first, "slab", one)


def per_device(order_params, layer_mask, coarse_temp, coarse_rows, grain_ids, energy):
    slots, cx, cy, cz = order_params.shape
    slabs, cols = lax.axis_size("slab"), lax.axis_size("col")
    devices = slabs * cols
    cells = cx * cy
    capacity, _, coarse_z = coarse_temp.shape
    raw = order_params.reshape(slots * cells, cz)
    mask = layer_mask.reshape(cells, cz)
    message = f32(THERMAL + 1, ROWS, cz)
    short = f32(2 * SHARE, ROWS, cz)
    state = f32(2 * slots * cells, cz // 2)

    hbm = lambda x: pltpu.with_memory_space_constraint(x, pltpu.HBM)
    near = cx // 2 + 2
    fields, mask, slot_order, slot_energy, bounds, planes, col_a, col_b = call(
        functools.partial(open_body, cx, cy, slots, slabs, cols),
        (
            state,
            f32(2 * cells, LANES),
            f32(ROWS, LANES),
            f32(slots * ROWS, LANES),
            jax.ShapeDtypeStruct((2 * ROWS, LANES), jnp.int32),
            f32((near + 4) * ROWS, LANES),
            message,
            message,
        ),
        [HBM] * 6,
        (VMEM,) * 8,
        [
            pltpu.SMEM(grain_ids.shape, jnp.int32),
            pltpu.SMEM(coarse_rows.shape, jnp.int32),
            pltpu.SMEM(energy.shape, jnp.float32),
            pltpu.VMEM(grain_ids.shape, jnp.int32),
            pltpu.VMEM(coarse_temp.shape, jnp.float32),
            pltpu.VMEM((2 * cells, LANES), jnp.int32),
            pltpu.VMEM(state.shape, jnp.float32),
            pltpu.SemaphoreType.DMA((9,)),
        ],
    )(hbm(grain_ids), hbm(coarse_rows), hbm(energy), hbm(raw), hbm(mask), hbm(coarse_temp))
    col_a, col_b = exchange_cols(col_a, col_b)
    slab_a, slab_b = call(
        functools.partial(faces_body, cx, cy, slots),
        (f32(THERMAL, ROWS, cz),) * 2,
        [VMEM] * 3,
        (VMEM,) * 2,
    )(fields, slot_energy, mask)
    slab_b, slab_a = exchange_slabs(slab_a, slab_b)
    ends_a, ends_b, planes = call(
        functools.partial(slab_body, cx, slabs, cols, coarse_temp.shape[1]),
        (f32(ROWS, cz), f32(ROWS, cz), f32(near * ROWS, LANES)),
        [VMEM] * 3,
        (VMEM,) * 3,
    )(planes, col_a, col_b)
    ends_b, ends_a = exchange_slabs(ends_a, ends_b)
    weights = jnp.asarray(plane_weights(cx, cy), jnp.bfloat16)
    height = jnp.asarray(height_weights(cz, coarse_z), jnp.bfloat16)
    count = Kept.rows(cells, slots)
    keep = call(
        functools.partial(mobility_body, cx, cy, slots, slabs, cols),
        f32(2 * count, LANES),
        [VMEM] * 13,
        VMEM,
        [pltpu.VMEM((near * ROWS, LANES), jnp.float32)],
    )(planes, bounds, mask, weights, height, slot_energy, slot_order, ends_b, ends_a, col_a, col_b, slab_a, slab_b)

    for pair in range(STEPS // 2):
        base = None if pair == 0 else slots * cells
        inputs = (fields, slot_energy) if pair == 0 else (fields,)
        force = call(
            functools.partial(inner_body, cx, cy, slots, base),
            state,
            [VMEM] * len(inputs),
            VMEM,
            flops=1 << 23,
            size=1 << 22,
        )(*inputs)
        grown, sums = call(
            functools.partial(sums_body, cx, cy, slots, slabs, cols, devices, base or 0),
            (f32(2 * Grown(cx, cy, slots).rows, LANES), f32(devices, 1, LANES)),
            [VMEM] * 7,
            (VMEM,) * 2,
            [pltpu.VMEM((2 * slots * ROWS, LANES), jnp.float32)],
        )(fields, keep if pair == 0 else fields, force, col_a, col_b, slab_a, slab_b)
        got = lax.all_to_all(sums, ("slab", "col"), 0, 0)
        if pair < STEPS // 2 - 1:
            fields, slab_a, slab_b = call(
                functools.partial(middle_body, cx, cy, slots),
                (f32(2 * (slots * cells + count), LANES), short, short),
                [VMEM] * 2,
                (VMEM,) * 3,
            )(got, grown)
            col_a, col_b = call(
                functools.partial(cols_body, cx, cy, slots), (short, short), [VMEM], (VMEM,) * 2
            )(fields)
            slab_b, slab_a = exchange_slabs(slab_a, slab_b)
            col_a, col_b = exchange_cols(col_a, col_b)
        else:
            fields = call(
                functools.partial(last_body, cx, cy, slots),
                f32(slots, cells, cz),
                [VMEM] * 2,
                HBM,
                [
                    pltpu.VMEM((slots, cells, cz), jnp.float32),
                    pltpu.SMEM((ROWS, LANES), jnp.float32),
                    pltpu.SemaphoreType.DMA((slots,)),
                    pltpu.SemaphoreType.DMA(()),
                ],
            )(got, grown)
    return fields.reshape(order_params.shape)


def solution(mesh):
    in_specs = (
        P(None, "slab", "col", None),
        P("slab", "col", None),
        P("slab", "col", None),
        P(),
        P(),
        P(),
    )
    out_specs = P(None, "slab", "col", None)
    return jax.shard_map(
        per_device, mesh=mesh, in_specs=in_specs, out_specs=out_specs, check_vma=False
    )
```

```python
import functools

import jax
import jax.numpy as jnp
import numpy as np
from jax import lax
from jax.experimental import pallas as pl
from jax.experimental.pallas import tpu as pltpu
from jax.sharding import PartitionSpec as P

SHARE = 4
STEPS = 4
TIME_STEP = 0.05
COUPLING = 1.5
BELOW, ABOVE, LEFT, RIGHT = range(4)
FACES = 4
MASK = 2 * SHARE
THERMAL = MASK + 1
LANES = 128
ROWS = 8
HIGHEST = lax.Precision.HIGHEST

VMEM = pl.BlockSpec(memory_space=pltpu.VMEM)
SMEM = pl.BlockSpec(memory_space=pltpu.SMEM)
HBM = pl.BlockSpec(memory_space=pltpu.HBM)


def call(body, out_shape, in_specs, out_specs, scratch=(), flops=1 << 20, size=1 << 20):
    return pl.pallas_call(
        body,
        out_shape=out_shape,
        in_specs=in_specs,
        out_specs=out_specs,
        scratch_shapes=list(scratch),
        compiler_params=pltpu.CompilerParams(vmem_limit_bytes=20 << 20),
        cost_estimate=pl.CostEstimate(flops=flops, bytes_accessed=size, transcendentals=0),
    )


def f32(*shape):
    return jax.ShapeDtypeStruct(shape, jnp.float32)


def present(slabs, cols):
    s, c = lax.axis_index("slab"), lax.axis_index("col")
    return (s > 0, s < slabs - 1, c > 0, c < cols - 1)


def beside(slabs, cols):
    s, c = lax.axis_index("slab"), lax.axis_index("col")
    return (
        (jnp.maximum(s - 1, 0), c),
        (jnp.minimum(s + 1, slabs - 1), c),
        (s, jnp.maximum(c - 1, 0)),
        (s, jnp.minimum(c + 1, cols - 1)),
    )


def slot_places(slabs, cols, slots, ids_ref, ids_smem):
    s, c = lax.axis_index("slab"), lax.axis_index("col")
    sub = lax.broadcasted_iota(jnp.int32, (slots, LANES), 0)
    lane = lax.broadcasted_iota(jnp.int32, (slots, LANES), 1)
    own = jnp.zeros((slots, LANES), jnp.int32)
    for q in range(slots):
        own = jnp.where(sub == q, ids_smem[s, c, q], own)
    one, zero = jnp.float32(1.0), jnp.float32(0.0)
    have = present(slabs, cols)
    matches, ranks = [], []
    for k, (ns, nc) in enumerate(beside(slabs, cols)):
        row = ids_ref[ns, pl.ds(nc, 1), :]
        row = jnp.concatenate([row, jnp.full((1, LANES - slots), -1, jnp.int32)], axis=1)
        row = jnp.broadcast_to(jnp.where(have[k], row, -1), (slots, LANES))
        hit = jnp.where((own == row) & (row >= 0), one, zero)
        shared = jnp.max(hit, axis=0, keepdims=True)
        matches.append(jnp.sum(hit, axis=1, keepdims=True))
        ranks.append(jnp.sum(jnp.where(row < own, shared, zero), axis=1, keepdims=True))
    free = one - (matches[0] + matches[1] + matches[2] + matches[3])
    lanef = lane.astype(jnp.float32)
    own_row = ids_ref[s, pl.ds(c, 1), :]
    own_row = jnp.concatenate([own_row, jnp.full((1, LANES - slots), -2, jnp.int32)], axis=1)
    own_row = jnp.broadcast_to(own_row, (slots, LANES))
    held = jnp.zeros((slots, LANES), jnp.float32)
    for k, (ns, nc) in enumerate(beside(slabs, cols)):
        theirs = jnp.zeros((slots, LANES), jnp.int32)
        for r in range(slots):
            theirs = jnp.where(sub == r, ids_smem[ns, nc, r], theirs)
        held = jnp.where((theirs == own_row) & have[k], one, held)
    free_row = one - jnp.max(held, axis=0, keepdims=True)
    free_rank = jnp.sum(jnp.where(lane < sub, free_row, zero), axis=1, keepdims=True)
    place = jnp.zeros((slots, LANES), jnp.float32)
    skipped = jnp.int32(0)
    for k in range(FACES):
        at = matches[k] * (ranks[k] + k * SHARE - lanef)
        place = jnp.where((matches[k] > 0.5) & (jnp.abs(at) < 0.5), one, place)
        local = free_rank - (skipped * SHARE).astype(jnp.float32)
        inside = (local > -0.5) & (local < SHARE - 0.5) & (free > 0.5)
        inside = inside & jnp.logical_not(have[k])
        place = jnp.where(inside & (jnp.abs(local + k * SHARE - lanef) < 0.5), one, place)
        skipped = skipped + jnp.where(have[k], 0, 1)
    return place


def take(ref, at, rows, stride=1):
    half = ref.shape[0] // 2
    if stride == 1:
        if not isinstance(at, int):
            at = pl.multiple_of(at, ROWS)
        return ref[pl.ds(at, rows), :], ref[pl.ds(at + half, rows), :]
    return ref[pl.ds(at, rows, stride=stride), :], ref[pl.ds(at + half, rows, stride=stride), :]


def take_shifted(ref, at, rows, by):
    half = ref.shape[0] // 2
    return ref[pl.ds(at + by, rows), :], ref[pl.ds(at + by + half, rows), :]


def put(ref, at, i, value):
    if not isinstance(at, int):
        at = pl.multiple_of(at, ROWS)
    ref[pl.ds(at + i * (ref.shape[0] // 2), value.shape[0]), :] = value


def spread(ref, row):
    half = ref.shape[0] // 2
    return tuple(jnp.broadcast_to(ref[pl.ds(row + i * half, 1), :], (ROWS, LANES)) for i in range(2))


class Kept:
    def __init__(self, ref, base, cx, cy, slots):
        self.ref, self.cy, self.cells = ref, cy, cx * cy
        self.base = base
        self.near_base = base + self.cells + FACES * ROWS
        self.energy_base = self.near_base + FACES * self.cells
        self.slots_base = self.energy_base + slots * ROWS

    @staticmethod
    def rows(cells, slots):
        return cells + FACES * ROWS + FACES * cells + slots * ROWS + ROWS

    def rate(self, x):
        return take(self.ref, self.base + x * self.cy, self.cy)

    def rate_beside(self, k):
        return take(self.ref, self.base + self.cells + k * ROWS, ROWS)

    def near(self, k, x):
        return take(self.ref, self.near_base + k * self.cells + x * self.cy, self.cy)

    def energy(self, q):
        at = self.energy_base + q * ROWS
        return self.ref[pl.ds(at if isinstance(at, int) else pl.multiple_of(at, ROWS), ROWS), :]


def keep_on(out, out_base, kept, count):
    for i in range(2):
        put(out, out_base, i, take(kept.ref, kept.base, count)[i])


def fill(out, index, pair):
    out[index, :, :LANES], out[index, :, LANES:] = pair


def pair_faces(axis, low, high):
    even = lax.rem(lax.axis_index(axis), 2) == 0
    return even, (jnp.where(even, high, low), jnp.where(even, low, high))


def pack_faces(fields, energy, cx, cy, slots, out_refs, axis, columns):
    low, high = (LEFT, RIGHT) if columns else (BELOW, ABOVE)
    first, last, top, bottom = edges()
    _, faces = pair_faces(axis, low, high)
    for out, face in zip(out_refs, faces):

        def plane(q, depth):
            if columns:
                return take(fields, q * (cx * cy) + jnp.where(face == high, cy - 1 - depth, depth), cx, cy)
            return take(fields, q * (cx * cy) + jnp.where(face == high, cx - 1 - depth, depth) * cy, cy)

        squares = [None, None]
        for q in range(slots):
            for i, v in enumerate(plane(q, 0)):
                squares[i] = v * v if squares[i] is None else squares[i] + v * v
        for j in range(SHARE):
            q = face * SHARE + j
            centre, inner = plane(q, 0), plane(q, 1)
            near = along_height(centre[0], centre[1], first, last)
            e = energy(q)
            forces = []
            for i in range(2):
                n = near[i] + along_rows(centre[i], top, bottom, None, None) + inner[i]
                forces.append(force_of(centre[i], n, 2.0 * COUPLING * squares[i], e))
            fill(out, j, centre)
            fill(out, SHARE + j, forces)


def open_body(
    cx, cy, slots, slabs, cols, ids_hbm, rows_hbm, energy_hbm, fields_hbm, mask_hbm, coarse_hbm,
    fields, mask, slots_ref, energy_out, bounds, planes, msg_a, msg_b,
    ids_smem, rows_smem, energy_smem, ids_ref, coarse_ref, mask_ref, raw, sems,
):
    cells = cx * cy
    loads = [
        pltpu.make_async_copy(ids_hbm, ids_smem, sems.at[0]),
        pltpu.make_async_copy(ids_hbm, ids_ref, sems.at[1]),
        pltpu.make_async_copy(rows_hbm, rows_smem, sems.at[2]),
        pltpu.make_async_copy(coarse_hbm, coarse_ref, sems.at[3]),
        pltpu.make_async_copy(energy_hbm, energy_smem, sems.at[8]),
    ]
    for i in range(2):
        half = pl.ds(i * LANES, LANES)
        loads.append(
            pltpu.make_async_copy(mask_hbm.at[:, half], mask_ref.at[pl.ds(i * cells, cells), :], sems.at[4 + i])
        )
        rows = slots * cells
        loads.append(
            pltpu.make_async_copy(fields_hbm.at[:, half], raw.at[pl.ds(i * rows, rows), :], sems.at[6 + i])
        )
    for load in loads:
        load.start()
    for load in loads[:5]:
        load.wait()
    place = slot_places(slabs, cols, slots, ids_ref, ids_smem)
    sub = lax.broadcasted_iota(jnp.int32, (slots, LANES), 0).astype(jnp.float32)
    slot_row = jnp.sum(place * sub, axis=0, keepdims=True)
    slots_ref[...] = jnp.broadcast_to(slot_row, (ROWS, LANES))
    lane = lax.broadcasted_iota(jnp.int32, (1, LANES), 1)
    taken = [jnp.sum(jnp.where(lane == q, slot_row, 0.0)).astype(jnp.int32) for q in range(slots)]
    at_rows = lax.broadcasted_iota(jnp.int32, (slots, LANES), 0)
    own_energy = jnp.zeros((slots, LANES), jnp.float32)
    s, c = lax.axis_index("slab"), lax.axis_index("col")
    for q in range(slots):
        own_energy = jnp.where(at_rows == q, energy_smem[ids_smem[s, c, q]], own_energy)
    energy_row = jnp.sum(place * own_energy, axis=0, keepdims=True)
    for q in range(slots):
        value = jnp.sum(jnp.where(lane == q, energy_row, 0.0), axis=1, keepdims=True)
        energy_out[q * ROWS : (q + 1) * ROWS, :] = jnp.broadcast_to(value, (ROWS, LANES))

    start = jnp.int32(0)
    for t in range(slabs):
        start = start + jnp.where(t < s, rows_smem[t], 0)
    live = rows_smem[s]
    bounds[0:ROWS, :] = jnp.full((ROWS, LANES), start, jnp.int32)
    bounds[ROWS : 2 * ROWS, :] = jnp.full((ROWS, LANES), start + live, jnp.int32)
    capacity, coarse_y, _ = coarse_ref.shape
    chosen = [
        jnp.clip(plane - start, 0, capacity - 1) for plane in near_planes(cx, slabs)
    ] + [jnp.int32(0), jnp.int32(1), live - 2, live - 1]
    _, faces = pair_faces("col", LEFT, RIGHT)
    for out in (msg_a, msg_b):
        out[THERMAL] = jnp.zeros((ROWS, out.shape[2]), jnp.float32)
    planes[...] = jnp.zeros(planes.shape, jnp.float32)
    for i, p in enumerate(chosen):
        planes[i * ROWS + 1 : i * ROWS + 1 + coarse_y, :] = coarse_ref[p]
        for out, face in zip((msg_a, msg_b), faces):
            row = jnp.where(face == RIGHT, coarse_y - 1, 0)
            spot = slice(i // ROWS * LANES, (i // ROWS + 1) * LANES)
            out[THERMAL, i % ROWS : i % ROWS + 1, spot] = coarse_ref[p, pl.ds(row, 1), :]

    for load in loads[5:]:
        load.wait()
    mask[...] = mask_ref[...].astype(jnp.float32)

    for q in range(slots):
        for i, part in enumerate(take(raw, taken[q] * cells, cells)):
            put(fields, q * cells, i, part)
    energy_of = lambda q: energy_out[pl.ds(pl.multiple_of(q * ROWS, ROWS), ROWS), :]
    pack_faces(fields, energy_of, cx, cy, slots, (msg_a, msg_b), "col", True)
    for out, face in zip((msg_a, msg_b), faces):
        first = jnp.where(face == RIGHT, cy - 1, 0)
        fill(out, MASK, take(mask, first, cx, cy))


def near_planes(cx, slabs):
    s = lax.axis_index("slab")
    half = cx // 2
    return [jnp.clip(s * half - 1 + i, 0, slabs * half - 1) for i in range(half + 2)]


def faces_body(cx, cy, slots, fields, energy, mask, msg_a, msg_b):
    energy_of = lambda q: energy[pl.ds(pl.multiple_of(q * ROWS, ROWS), ROWS), :]
    pack_faces(fields, energy_of, cx, cy, slots, (msg_a, msg_b), "slab", False)
    _, faces = pair_faces("slab", BELOW, ABOVE)
    for out, face in zip((msg_a, msg_b), faces):
        first = jnp.where(face == ABOVE, cx - 1, 0) * cy
        fill(out, MASK, take(mask, first, cy))


def slab_body(cx, slabs, cols, coarse_y, own, got_a, got_b, msg_a, msg_b, planes):
    have = present(slabs, cols)
    even, _ = pair_faces("col", LEFT, RIGHT)
    from_a, from_b = got_a[THERMAL], got_b[THERMAL]
    lower = jnp.where(even, from_b, from_a)
    upper = jnp.where(even, from_a, from_b)
    sub = lax.broadcasted_iota(jnp.int32, (ROWS, LANES), 0)
    last = coarse_y + 1
    widened = []
    for i in range(cx // 2 + 6):
        plane = own[i * ROWS : (i + 1) * ROWS, :]
        spot = slice(i // ROWS * LANES, (i // ROWS + 1) * LANES)
        below = jnp.where(have[LEFT], lower[i % ROWS : i % ROWS + 1, spot], plane[1:2, :])
        above = jnp.where(have[RIGHT], upper[i % ROWS : i % ROWS + 1, spot], plane[coarse_y : coarse_y + 1, :])
        plane = jnp.where(sub == 0, below, jnp.where(sub == last, above, plane))
        widened.append(plane)
        if i < cx // 2 + 2:
            planes[i * ROWS : (i + 1) * ROWS, :] = plane
    first = cx // 2 + 2
    _, faces = pair_faces("slab", BELOW, ABOVE)
    for out, face in zip((msg_a, msg_b), faces):
        for i in range(2):
            plane = jnp.where(face == ABOVE, widened[first + 2 + i], widened[first + i])
            out[:, i * LANES : (i + 1) * LANES] = plane


def axis_weights(cells):
    fine = np.arange(-1, cells + 1)
    lower = (2 * fine - 1) // 4
    weight = (2 * fine - 1 - 4 * lower) / 4.0
    out = np.zeros((cells + 2, cells // 2 + 2), np.float32)
    out[np.arange(cells + 2), lower + 1] += 1.0 - weight
    out[np.arange(cells + 2), lower + 2] += weight
    return out


def plane_weights(cx, cy):
    along, across = axis_weights(cx), axis_weights(cy)
    inner = [(x + 1, y + 1) for x in range(cx) for y in range(cy)]
    inner += [(0, y + 1) for y in range(cy)] + [(cx + 1, y + 1) for y in range(cy)]
    inner += [(x + 1, 0) for x in range(cx)] + [(x + 1, cy + 1) for x in range(cx)]
    out = np.zeros((len(inner), cx // 2 + 2, ROWS), np.float32)
    for row, (x, y) in enumerate(inner):
        out[row, :, : cy // 2 + 2] = along[x][:, None] * across[y][None, :]
    return out.reshape(len(inner), -1)


def height_weights(cells, coarse):
    fine = np.arange(cells)
    lower = (2 * fine - 1) // 4
    weight = (2 * fine - 1 - 4 * lower) / 4.0
    out = np.zeros((coarse, cells), np.float32)
    np.add.at(out, (np.clip(lower, 0, coarse - 1), fine), 1.0 - weight)
    np.add.at(out, (np.clip(lower + 1, 0, coarse - 1), fine), weight)
    return out


def parts_of(value):
    parts = []
    for _ in range(3):
        parts.append(value.astype(jnp.bfloat16))
        value = value - parts[-1].astype(jnp.float32)
    return parts


def mobility_body(
    cx, cy, slots, slabs, cols, planes, bounds, mask_ref, weights, height, energy, slots_ref,
    ends_b, ends_a, col_a, col_b, slab_a, slab_b, keep, near,
):
    start, end = bounds[0:ROWS, :], bounds[ROWS : 2 * ROWS, :]
    even_s, _ = pair_faces("slab", BELOW, ABOVE)
    even_c, _ = pair_faces("col", LEFT, RIGHT)
    mask = MASK
    below = jnp.where(even_s, ends_b[...], ends_a[...])
    above = jnp.where(even_s, ends_a[...], ends_b[...])
    for i, p in enumerate(near_planes(cx, slabs)):
        p = jnp.full((ROWS, LANES), p, jnp.int32)
        own = planes[i * ROWS : (i + 1) * ROWS, :]
        lower = jnp.where(p == start - 2, below[:, :LANES], below[:, LANES:])
        upper = jnp.where(p == end, above[:, :LANES], above[:, LANES:])
        near[i * ROWS : (i + 1) * ROWS, :] = jnp.where(p < start, lower, jnp.where(p < end, own, upper))
    dot = functools.partial(jnp.dot, preferred_element_type=jnp.float32)
    flat = sum(dot(weights[...], part) for part in parts_of(near[...]))
    profile = sum(dot(part, height[...]) for part in parts_of(flat))
    mobility = jnp.exp(2.0 * (profile - 1.0)) * TIME_STEP
    cells = cx * cy
    kept = Kept(keep, 0, cx, cy, slots)
    for i, part in enumerate(take(mask_ref, 0, cells)):
        put(keep, 0, i, part * mobility[:cells, i * LANES : (i + 1) * LANES])
    have = present(slabs, cols)
    masks = (
        jnp.where(even_s, slab_b[mask], slab_a[mask]),
        jnp.where(even_s, slab_a[mask], slab_b[mask]),
        jnp.where(even_c, col_b[mask], col_a[mask]),
        jnp.where(even_c, col_a[mask], col_b[mask]),
    )
    for k in range(FACES):
        at = cells + k * ROWS
        for i, part in enumerate(split(jnp.where(have[k], masks[k] * mobility[at : at + ROWS], 0.0))):
            put(keep, at, i, part)
    for i in range(2):
        put(keep, kept.energy_base, i, energy[...])
        put(keep, kept.slots_base, i, slots_ref[...])
    marks = edges()
    top, bottom = marks[2:]
    for x in range(cx):
        sums = neighbours(x, cx - 1, kept.rate, kept.rate(x), None, None, marks)
        extra = [None] * FACES
        if x == 0:
            extra[BELOW] = kept.rate_beside(BELOW)
        if x == cx - 1:
            extra[ABOVE] = kept.rate_beside(ABOVE)
        extra[LEFT] = [jnp.where(top, v, 0.0) for v in spread(keep, cells + LEFT * ROWS + x)]
        extra[RIGHT] = [jnp.where(bottom, v, 0.0) for v in spread(keep, cells + RIGHT * ROWS + x)]
        for k in range(FACES):
            for i in range(2):
                value = sums[i] if extra[k] is None else sums[i] + extra[k][i]
                put(keep, kept.near_base + k * cells + x * cy, i, value)


def split(value):
    return value[:, :LANES], value[:, LANES:]


def along_height(v0, v1, first, last):
    r0, r1 = pltpu.roll(v0, 1, 1), pltpu.roll(v1, 1, 1)
    q0, q1 = pltpu.roll(v0, LANES - 1, 1), pltpu.roll(v1, LANES - 1, 1)
    return (
        jnp.where(first, 0.0, r0) + jnp.where(last, q1, q0),
        jnp.where(first, r0, r1) + jnp.where(last, 0.0, q1),
    )


def along_rows(v, top, bottom, lower, upper, shifted=None):
    before, after = shifted or (pltpu.roll(v, 1, 0), pltpu.roll(v, ROWS - 1, 0))
    down = jnp.where(top, 0.0 if lower is None else lower, before)
    up = jnp.where(bottom, 0.0 if upper is None else upper, after)
    return down + up


def edges():
    lane = lax.broadcasted_iota(jnp.int32, (ROWS, LANES), 1)
    row = lax.broadcasted_iota(jnp.int32, (ROWS, LANES), 0)
    return lane == 0, lane == LANES - 1, row == 0, row == ROWS - 1


def neighbours(x, last_x, load, centre, halo, kind, marks, shift=None):
    first, last, top, bottom = marks
    v0, v1 = centre
    n0, n1 = along_height(v0, v1, first, last)
    low = high = (None, None)
    if kind == LEFT:
        low = halo(x)
    if kind == RIGHT:
        high = halo(x)
    shifted = (None, None)
    if shift is not None and 0 < x < last_x:
        before, after = shift(x, -1), shift(x, 1)
        shifted = tuple(zip(before, after))
    n0 = n0 + along_rows(v0, top, bottom, low[0], high[0], shifted[0])
    n1 = n1 + along_rows(v1, top, bottom, low[1], high[1], shifted[1])
    sides = []
    if not (isinstance(x, int) and x == 0):
        sides.append(load(x - 1))
    elif kind == BELOW:
        sides.append(halo(None))
    if not (isinstance(x, int) and x == last_x):
        sides.append(load(x + 1))
    elif kind == ABOVE:
        sides.append(halo(None))
    for a, b in sides:
        n0, n1 = n0 + a, n1 + b
    return n0, n1


def over_planes(cx, visit, carry):
    carry = visit(0, carry)
    carry = lax.fori_loop(1, cx - 1, visit, carry)
    return visit(cx - 1, carry)


def slot_access(fields, halos, base, q, cells, cy):
    def load(x):
        return take(fields, q * cells + x * cy, cy)

    def halo(x):
        if x is None:
            return take(halos, base + q * ROWS, ROWS)
        return spread(halos, base + q * ROWS + x)

    return load, halo


def force_of(v, n, squares3, energy):
    return v * (squares3 + ((5.0 - energy) + v * (energy - 2.0 * v))) - n


def triple_squares(fields, x, slots, cells, cy):
    total = None
    for q in range(slots):
        v0, v1 = take(fields, q * cells + x * cy, cy)
        total = (v0 * v0, v1 * v1) if total is None else (total[0] + v0 * v0, total[1] + v1 * v1)
    return 2.0 * COUPLING * total[0], 2.0 * COUPLING * total[1]


def inner_body(cx, cy, slots, base, *refs):
    fields, force_out = refs[0], refs[-1]
    cells = cx * cy
    marks = edges()
    if base is None:
        energy = lambda q: refs[1][q * ROWS : (q + 1) * ROWS, :]
    else:
        energy = Kept(fields, base, cx, cy, slots).energy

    def visit(x, carry):
        squares = triple_squares(fields, x, slots, cells, cy)
        for q in range(slots):
            load, _ = slot_access(fields, None, None, q, cells, cy)
            centre = load(x)
            shift = lambda y, by: take_shifted(fields, q * cells + y * cy, cy, by)
            near = neighbours(x, cx - 1, load, centre, None, None, marks, shift)
            e = energy(q)
            for i in range(2):
                put(force_out, q * cells + x * cy, i, force_of(centre[i], near[i], squares[i], e))
        return carry

    for x in range(cx):
        visit(x, 0)


def arrivals(col_a, col_b, slab_a, slab_b):
    even_s, _ = pair_faces("slab", BELOW, ABOVE)
    even_c, _ = pair_faces("col", LEFT, RIGHT)
    pairs = ((slab_b, slab_a, even_s), (slab_a, slab_b, even_s), (col_b, col_a, even_c), (col_a, col_b, even_c))
    return [functools.partial(lambda u, v, even, i: jnp.where(even, u[i], v[i]), *pair) for pair in pairs]


class Grown:
    def __init__(self, cx, cy, slots):
        self.cells = cx * cy
        self.sum = slots * self.cells
        self.squares = self.sum + self.cells
        self.halos = self.squares + self.cells
        self.kept = self.halos + slots * ROWS
        self.count = Kept.rows(self.cells, slots)
        self.rows = self.kept + self.count


def sums_body(
    cx, cy, slots, slabs, cols, devices, base, fields, keep, force_in, col_a, col_b, slab_a, slab_b,
    grown, sums_ref, halos,
):
    cells = cx * cy
    _, _, top, bottom = edges()
    have = present(slabs, cols)
    kept = Kept(keep, base, cx, cy, slots)
    layout = Grown(cx, cy, slots)
    keep_on(grown, layout.kept, kept, layout.count)
    for k, pick in enumerate(arrivals(col_a, col_b, slab_a, slab_b)):
        rate = kept.rate_beside(k)
        for j in range(SHARE):
            q = k * SHARE + j
            if k == BELOW:
                own = take(fields, q * cells, cy)
            elif k == ABOVE:
                own = take(fields, (q + 1) * cells - cy, cy)
            elif k == LEFT:
                own = take(fields, q * cells, cx, cy)
            else:
                own = take(fields, q * cells + cy - 1, cx, cy)
            beside, force = split(jnp.where(have[k], pick(j), 0.0)), split(pick(SHARE + j))
            for i in range(2):
                put(halos, q * ROWS, i, beside[i])
                put(grown, layout.halos + q * ROWS, i, beside[i] - rate[i] * (force[i] - own[i]))

    energy_sum = None
    for q in range(slots):
        energy_sum = kept.energy(q) if energy_sum is None else energy_sum + kept.energy(q)
    zero = jnp.zeros((ROWS, LANES), jnp.float32)

    def visit(x, carry):
        total, c0, c1, c2, c3, weight = carry
        rate = kept.rate(x)
        forces, powers = [zero, zero], [zero, zero]
        a2, b1 = [zero, zero], [zero, zero]
        a1 = [[zero, zero] for _ in range(FACES)]
        for q in range(slots):
            k = q // SHARE
            centre = take(fields, q * cells + x * cy, cy)
            inner = take(force_in, q * cells + x * cy, cy)
            e = kept.energy(q)
            cross = (None, None)
            if k in (LEFT, RIGHT):
                row = spread(halos, q * ROWS + x)
                cross = [jnp.where(top if k == LEFT else bottom, row[i], 0.0) for i in range(2)]
            elif isinstance(x, int) and (k, x) in ((BELOW, 0), (ABOVE, cx - 1)):
                cross = take(halos, q * ROWS, ROWS)
            for i in range(2):
                force = inner[i] if cross[i] is None else inner[i] - cross[i]
                g = centre[i] - rate[i] * force
                put(grown, q * cells + x * cy, i, g)
                weighted, square = e * g, g * g
                forces[i] = forces[i] + force
                powers[i] = powers[i] + g * (weighted - (square + square))
                a1[k][i] = a1[k][i] + g
                a2[i] = a2[i] + square
                b1[i] = b1[i] + weighted
        beside = [kept.near(k, x) for k in range(FACES)]
        for i in range(2):
            h = rate[i]
            whole = (a1[0][i] + a1[1][i]) + (a1[2][i] + a1[3][i])
            near = [beside[k][i] for k in range(FACES)]
            put(grown, layout.sum + x * cy, i, whole)
            put(grown, layout.squares + x * cy, i, a2[i])
            total = total + h * forces[i]
            c0 = c0 + h * (powers[i] + 5.0 * whole - b1[i] + 2.0 * COUPLING * whole * a2[i])
            for k in range(FACES):
                c0 = c0 - a1[k][i] * near[k]
            linear = (
                energy_sum
                - 5.0 * slots
                - 2.0 * b1[i]
                + (6.0 - 2.0 * COUPLING * slots) * a2[i]
                - 4.0 * COUPLING * (whole * whole)
            )
            c1 = c1 + h * (h * linear + float(SHARE) * ((near[0] + near[1]) + (near[2] + near[3])))
            c2 = c2 + h * h * h * (energy_sum + (6.0 * COUPLING * slots - 6.0) * whole)
            c3 = c3 + (h * h) * (h * h)
            weight = weight + h
        return total, c0, c1, c2, c3, weight

    parts = over_planes(cx, visit, (zero,) * 6)
    back = -1.0 / TIME_STEP
    scales = (back, back, back, back, back * (2.0 * slots - 2.0 * COUPLING * slots * slots), 1.0 / TIME_STEP)
    lane = lax.broadcasted_iota(jnp.int32, (1, LANES), 1)
    row = jnp.zeros((1, LANES), jnp.float32)
    for i, (part, scale) in enumerate(zip(parts, scales)):
        value = jnp.sum(jnp.sum(part, axis=0, keepdims=True), axis=1, keepdims=True) * scale
        row = jnp.where(lane == i, value, row)
    sums_ref[...] = jnp.broadcast_to(row[None], (devices, 1, LANES))


def multipliers(got, slots):
    total = jnp.sum(got[...], axis=0)
    lane = lax.broadcasted_iota(jnp.int32, (1, LANES), 1)
    part = [jnp.sum(jnp.where(lane == i, total, 0.0), axis=1, keepdims=True) for i in range(6)]
    whole = slots * part[5]
    here = part[0] / whole
    later = (part[1] + here * (part[2] + here * (part[3] + here * part[4]))) / whole
    return jnp.broadcast_to(here, (ROWS, LANES)), jnp.broadcast_to(later, (ROWS, LANES))


def settle(cx, cy, slots, got, grown, store, done=None):
    cells = cx * cy
    marks = edges()
    here, later = multipliers(got, slots)
    layout = Grown(cx, cy, slots)
    kept = Kept(grown, layout.kept, cx, cy, slots)
    for k in range(FACES):

        def visit(x, carry):
            rate = kept.rate(x)
            near = kept.near(k, x)
            a1 = take(grown, layout.sum + x * cy, cy)
            a2 = take(grown, layout.squares + x * cy, cy)
            off = [here * rate[i] for i in range(2)]
            base = [
                5.0 + 2.0 * COUPLING * (a2[i] - off[i] * (2.0 * a1[i] - float(slots) * off[i])) for i in range(2)
            ]
            extra = [here * near[i] + later for i in range(2)]
            for q in range(k * SHARE, (k + 1) * SHARE):
                e = kept.energy(q)
                load, halo = slot_access(grown, grown, layout.halos, q, cells, cy)
                shift = lambda y, by: take_shifted(grown, q * cells + y * cy, cy, by)
                g = load(x)
                n = neighbours(x, cx - 1, load, g, halo, k, marks, shift)
                for i in range(2):
                    f = g[i] - off[i]
                    force = f * ((base[i] - e) + f * (e - (f + f))) - (n[i] - extra[i])
                    store(q, x, i, f - rate[i] * force)
            return carry

        for x in range(cx):
            visit(x, 0)
        if done is not None:
            done(k)


def middle_body(cx, cy, slots, got, grown, fields, slab_a, slab_b):
    def store(q, x, i, value):
        put(fields, q * cx * cy + x * cy, i, value)

    settle(cx, cy, slots, got, grown, store)
    layout = Grown(cx, cy, slots)
    keep_on(fields, slots * cx * cy, Kept(grown, layout.kept, cx, cy, slots), layout.count)
    energy = Kept(fields, slots * cx * cy, cx, cy, slots).energy
    pack_faces(fields, energy, cx, cy, slots, (slab_a, slab_b), "slab", False)


def cols_body(cx, cy, slots, fields, col_a, col_b):
    energy = Kept(fields, slots * cx * cy, cx, cy, slots).energy
    pack_faces(fields, energy, cx, cy, slots, (col_a, col_b), "col", True)


def last_body(cx, cy, slots, got, grown, out, result, order, sems, order_sem):
    kept = Kept(grown, Grown(cx, cy, slots).kept, cx, cy, slots)
    fetch = pltpu.make_async_copy(grown.at[pl.ds(kept.slots_base, ROWS), :], order, order_sem)
    fetch.start()

    def store(q, x, i, value):
        at = x * cy if isinstance(x, int) else pl.multiple_of(x * cy, ROWS)
        result[q, pl.ds(at, cy), i * LANES : (i + 1) * LANES] = value

    def send(q):
        return pltpu.make_async_copy(result.at[q], out.at[order[0, q].astype(jnp.int32)], sems.at[q])

    def done(k):
        if k == 0:
            fetch.wait()
        for q in range(k * SHARE, (k + 1) * SHARE):
            send(q).start()

    settle(cx, cy, slots, got, grown, store, done)
    for q in range(slots):
        send(q).wait()


def exchange_cols(first, second):
    count = lax.axis_size("col")
    one = [(i, i ^ 1) for i in range(count)]
    two = [(i, (i - 1) % count if i % 2 == 0 else (i + 1) % count) for i in range(count)]
    return lax.ppermute(first, "col", one), lax.ppermute(second, "col", two)


def exchange_slabs(first, second):
    count, cols = lax.axis_size("slab"), lax.axis_size("col")
    one = [(i, i ^ 1) for i in range(count)]
    two = []
    for s in range(count):
        other = s - 1 if s % 2 == 0 else s + 1
        for c in range(cols):
            target = other * cols + c if 0 <= other < count else s * cols + (c ^ 1)
            two.append((s * cols + c, target))
    return lax.ppermute(second, ("slab", "col"), two), lax.ppermute(first, "slab", one)


def per_device(order_params, layer_mask, coarse_temp, coarse_rows, grain_ids, energy):
    slots, cx, cy, cz = order_params.shape
    slabs, cols = lax.axis_size("slab"), lax.axis_size("col")
    devices = slabs * cols
    cells = cx * cy
    capacity, _, coarse_z = coarse_temp.shape
    raw = order_params.reshape(slots * cells, cz)
    mask = layer_mask.reshape(cells, cz)
    message = f32(THERMAL + 1, ROWS, cz)
    short = f32(2 * SHARE, ROWS, cz)
    state = f32(2 * slots * cells, cz // 2)

    hbm = lambda x: pltpu.with_memory_space_constraint(x, pltpu.HBM)
    near = cx // 2 + 2
    fields, mask, slot_order, slot_energy, bounds, planes, col_a, col_b = call(
        functools.partial(open_body, cx, cy, slots, slabs, cols),
        (
            state,
            f32(2 * cells, LANES),
            f32(ROWS, LANES),
            f32(slots * ROWS, LANES),
            jax.ShapeDtypeStruct((2 * ROWS, LANES), jnp.int32),
            f32((near + 4) * ROWS, LANES),
            message,
            message,
        ),
        [HBM] * 6,
        (VMEM,) * 8,
        [
            pltpu.SMEM(grain_ids.shape, jnp.int32),
            pltpu.SMEM(coarse_rows.shape, jnp.int32),
            pltpu.SMEM(energy.shape, jnp.float32),
            pltpu.VMEM(grain_ids.shape, jnp.int32),
            pltpu.VMEM(coarse_temp.shape, jnp.float32),
            pltpu.VMEM((2 * cells, LANES), jnp.int32),
            pltpu.VMEM(state.shape, jnp.float32),
            pltpu.SemaphoreType.DMA((9,)),
        ],
    )(hbm(grain_ids), hbm(coarse_rows), hbm(energy), hbm(raw), hbm(mask), hbm(coarse_temp))
    col_a, col_b = exchange_cols(col_a, col_b)
    slab_a, slab_b = call(
        functools.partial(faces_body, cx, cy, slots),
        (f32(THERMAL, ROWS, cz),) * 2,
        [VMEM] * 3,
        (VMEM,) * 2,
    )(fields, slot_energy, mask)
    slab_b, slab_a = exchange_slabs(slab_a, slab_b)
    ends_a, ends_b, planes = call(
        functools.partial(slab_body, cx, slabs, cols, coarse_temp.shape[1]),
        (f32(ROWS, cz), f32(ROWS, cz), f32(near * ROWS, LANES)),
        [VMEM] * 3,
        (VMEM,) * 3,
    )(planes, col_a, col_b)
    ends_b, ends_a = exchange_slabs(ends_a, ends_b)
    weights = jnp.asarray(plane_weights(cx, cy), jnp.bfloat16)
    height = jnp.asarray(height_weights(cz, coarse_z), jnp.bfloat16)
    count = Kept.rows(cells, slots)
    keep = call(
        functools.partial(mobility_body, cx, cy, slots, slabs, cols),
        f32(2 * count, LANES),
        [VMEM] * 13,
        VMEM,
        [pltpu.VMEM((near * ROWS, LANES), jnp.float32)],
    )(planes, bounds, mask, weights, height, slot_energy, slot_order, ends_b, ends_a, col_a, col_b, slab_a, slab_b)

    for pair in range(STEPS // 2):
        base = None if pair == 0 else slots * cells
        inputs = (fields, slot_energy) if pair == 0 else (fields,)
        force = call(
            functools.partial(inner_body, cx, cy, slots, base),
            state,
            [VMEM] * len(inputs),
            VMEM,
            flops=1 << 23,
            size=1 << 22,
        )(*inputs)
        grown, sums = call(
            functools.partial(sums_body, cx, cy, slots, slabs, cols, devices, base or 0),
            (f32(2 * Grown(cx, cy, slots).rows, LANES), f32(devices, 1, LANES)),
            [VMEM] * 7,
            (VMEM,) * 2,
            [pltpu.VMEM((2 * slots * ROWS, LANES), jnp.float32)],
        )(fields, keep if pair == 0 else fields, force, col_a, col_b, slab_a, slab_b)
        got = lax.all_to_all(sums, ("slab", "col"), 0, 0)
        if pair < STEPS // 2 - 1:
            fields, slab_a, slab_b = call(
                functools.partial(middle_body, cx, cy, slots),
                (f32(2 * (slots * cells + count), LANES), short, short),
                [VMEM] * 2,
                (VMEM,) * 3,
            )(got, grown)
            col_a, col_b = call(
                functools.partial(cols_body, cx, cy, slots), (short, short), [VMEM], (VMEM,) * 2
            )(fields)
            slab_b, slab_a = exchange_slabs(slab_a, slab_b)
            col_a, col_b = exchange_cols(col_a, col_b)
        else:
            fields = call(
                functools.partial(last_body, cx, cy, slots),
                f32(slots, cells, cz),
                [VMEM] * 2,
                HBM,
                [
                    pltpu.VMEM((slots, cells, cz), jnp.float32),
                    pltpu.SMEM((ROWS, LANES), jnp.float32),
                    pltpu.SemaphoreType.DMA((slots,)),
                    pltpu.SemaphoreType.DMA(()),
                ],
            )(got, grown)
    return fields.reshape(order_params.shape)


def solution(mesh):
    in_specs = (
        P(None, "slab", "col", None),
        P("slab", "col", None),
        P("slab", "col", None),
        P(),
        P(),
        P(),
    )
    out_specs = P(None, "slab", "col", None)
    return jax.shard_map(
        per_device, mesh=mesh, in_specs=in_specs, out_specs=out_specs, check_vma=False
    )
```
